256 devices in a mesh: src: 2 (over z_hi), bl: 32 (over x, z_lo, core), ch: 4 (over y).
Axes of the slice: x: 4, y: 4, z: 8 (z_hi: 2, z_lo: 4; z = z_hi * 4 + z_lo), core: 2. Of those that a mesh axis runs over, the one named last changes fastest.
Arguments:
- observed: float32 [2, 16, 16384], P(None, 'ch', 'bl'), may hold values from -6 to 6
- weights: float32 [16, 16384], P('ch', 'bl'), may hold values from 0.3 to 3
- pairs: int32 [2, 16384], P(None, 'bl'), may hold values from 0 to 511
- positions: float32 [512, 2], P('bl'), may hold values from -1 to 1
- centres: float32 [2, 32], replicated, may hold values from -0.6 to 0.6
- assign: int32 [512], P('src'), may hold values from 0 to 31
- amplitude: float32 [512], P('src'), may hold values from 0.01 to 0.1
- offsets: float32 [2, 512], P(None, 'src'), may hold values from -2 to 2
- widths: float32 [512], P('src'), may hold values from 0.02 to 0.1
- block_index: int32 [1], replicated, may hold values from 0 to 511
Outputs:
- grad_comp: float32 [4, 512], P(None, 'src')
- grad_centre: float32 [2, 32], replicated
- residual: float32 [2, 16, 16384], P(None, 'ch', 'bl')
The draws below stay inside these ranges and needn't reach their ends.
All inputs are finite; a program needn't handle non-finite values.
Results may differ from the reference program's by a relative error of at most 0.0003.
Values sent between devices are 32-bit elements; how exact they have to be, the bound alone decides.
A program may use at most 64 MiB of HBM per device.

```python
import math
import jax
import jax.numpy as jnp
from jax import lax

STATION_COUNT = 512
BLOCK_CHANNELS = 16
BLOCKS = 512
BASELINE_SHARD = 512
BASELINE_TOTAL = 16384
COMPONENTS = 512
SOURCES = 32


def set_ends(array, own_key, smallest, largest):
    longest = array.shape.index(max(array.shape))
    spots = []
    for shift in (0, 1):
        where = [jax.random.randint(jax.random.fold_in(own_key, axis), (), 0, length) for axis, length in enumerate(array.shape)]
        where[longest] = (where[longest] + shift) % array.shape[longest]
        spots.append(tuple(where))
    return array.at[spots[0]].set(smallest).at[spots[1]].set(largest)


def block_levels(own_key, shape, shards, least, high):
    loudness = 1.0
    for dim, shards_of in shards:
        steps = jax.random.uniform(jax.random.fold_in(jax.random.fold_in(own_key, 6), dim), (shards_of,), jnp.float32, least / len(shards), high / len(shards))
        loudness = loudness * jnp.repeat(jnp.exp(steps), shape[dim] // shards_of).reshape((-1,) + (1,) * (len(shape) - 1 - dim))
    return loudness


def bell_draw(stream_key, dims, deviation, reach, cuts=(), kind=jnp.bfloat16):
    factor_of = block_levels(stream_key, dims, cuts, -0.22, 0.18) if cuts else 1.0
    drawn = jax.random.normal(stream_key, dims, jnp.float32) * deviation * factor_of
    return jnp.minimum(jnp.maximum(drawn, -reach), reach).astype(kind)


def setup_inputs(seed: int = 0) -> dict:
    splits = jax.random.split(jax.random.key(seed), 11)
    return {
        "observed": bell_draw(splits[0], (2, BLOCK_CHANNELS, BASELINE_TOTAL), 1.0, 6.0, ((1, 4), (2, 32)), jnp.float32),
        "weights": jnp.clip(jnp.exp(math.log(3.0) - 2.3025851 * jax.random.uniform(splits[1], (BLOCK_CHANNELS, BASELINE_TOTAL), jnp.float32) ** block_levels(splits[1], (BLOCK_CHANNELS, BASELINE_TOTAL), ((0, 4), (1, 32)), -0.2, 0.2)), 0.3, 3.0),
        "pairs": set_ends(jax.random.randint(splits[2], (2, BASELINE_TOTAL), 0, STATION_COUNT), jax.random.fold_in(splits[2], 1), 0, STATION_COUNT - 1).astype(jnp.int32),
        "positions": jnp.clip(jax.random.uniform(splits[3], (STATION_COUNT, 2), jnp.float32, -1.0, 1.0) * block_levels(splits[3], (STATION_COUNT, 2), ((0, 32),), -0.4, 0.0), -1.0, 1.0),
        "centres": jnp.clip(jax.random.uniform(splits[4], (2, SOURCES), jnp.float32, -0.6, 0.6), -0.6, 0.6),
        "assign": set_ends(jax.random.randint(splits[5], (COMPONENTS,), 0, SOURCES), jax.random.fold_in(splits[5], 1), 0, SOURCES - 1).astype(jnp.int32),
        "amplitude": jnp.clip(jnp.exp(math.log(0.1) - 2.3025851 * jax.random.uniform(splits[6], (COMPONENTS,), jnp.float32) ** block_levels(splits[6], (COMPONENTS,), ((0, 2),), -0.2, 0.2)), 0.01, 0.1),
        "offsets": bell_draw(splits[7], (2, COMPONENTS), 0.15, 2.0, ((1, 2),), jnp.float32),
        "widths": jnp.clip(jnp.exp(math.log(0.1) - 1.609438 * jax.random.uniform(splits[8], (COMPONENTS,), jnp.float32) ** block_levels(splits[8], (COMPONENTS,), ((0, 2),), -0.2, 0.2)), 0.02, 0.1),
        "block_index": jax.random.randint(splits[9], (1,), 0, BLOCKS).astype(jnp.int32),
    }


TWO_PI = 2.0 * math.pi
ENV_COEF = 2.0 * math.pi * math.pi
NU_ZERO = 50000000.0
NU_STEP = 36621.09375
NU_REF = 100000000.0

def wave_numbers(block, start, count):
    index = block * BLOCK_CHANNELS + start + jnp.arange(count, dtype=jnp.int32)
    return (NU_ZERO + index.astype(jnp.float32) * NU_STEP) / NU_REF

def scale_terms(sums, amplitude, widths, residual_norm):
    grad_amp = -residual_norm * sums[0]
    grad_l = -residual_norm * TWO_PI * amplitude * sums[2]
    grad_m = -residual_norm * TWO_PI * amplitude * sums[3]
    grad_w = residual_norm * 2.0 * TWO_PI * math.pi * amplitude * widths * sums[1]
    return jnp.stack([grad_amp, grad_l, grad_m, grad_w])

def reference(observed, weights, pairs, positions, centres, assign, amplitude, offsets, widths, block_index):
    lpos = centres[0][assign] + offsets[0]
    mpos = centres[1][assign] + offsets[1]
    ks = wave_numbers(block_index[0], 0, BLOCK_CHANNELS)
    residual_norm = 1.0 / math.sqrt(BASELINE_TOTAL * BLOCK_CHANNELS)
    xs = positions[:, 0]
    ys = positions[:, 1]
    block_count = BASELINE_TOTAL // BASELINE_SHARD
    pidx = pairs[0].reshape(block_count, BASELINE_SHARD)
    qidx = pairs[1].reshape(block_count, BASELINE_SHARD)
    highest = lax.Precision.HIGHEST

    def channel(inputs):
        kval, obs, wts = inputs
        theta = (xs[:, None] * lpos[None, :] + ys[:, None] * mpos[None, :]) * (-TWO_PI * kval)
        gre = jnp.cos(theta)
        gim = jnp.sin(theta)
        obs_r = obs[0].reshape(block_count, BASELINE_SHARD)
        obs_i = obs[1].reshape(block_count, BASELINE_SHARD)
        wblk = wts.reshape(block_count, BASELINE_SHARD)

        def step(total, blk):
            pix, qix, orr, oii, wt = blk
            dx = xs[pix] - xs[qix]
            dy = ys[pix] - ys[qix]
            r2 = dx * dx + dy * dy
            gp_r = jnp.take(gre, pix, axis=0)
            gp_i = jnp.take(gim, pix, axis=0)
            gq_r = jnp.take(gre, qix, axis=0)
            gq_i = jnp.take(gim, qix, axis=0)
            env = jnp.exp(-(ENV_COEF * kval * kval) * r2[:, None] * (widths * widths)[None, :])
            ep_r = env * (gp_r * gq_r + gp_i * gq_i)
            ep_i = env * (gp_i * gq_r - gp_r * gq_i)
            vr = jnp.dot(ep_r, amplitude, precision=highest, preferred_element_type=jnp.float32)
            vi = jnp.dot(ep_i, amplitude, precision=highest, preferred_element_type=jnp.float32)
            rr = orr - vr
            ri = oii - vi
            wr = wt * rr
            wi = wt * ri
            k2r2 = kval * kval * r2
            kdx = kval * dx
            kdy = kval * dy
            left_r = jnp.stack([wr, k2r2 * wr, -kdx * wi, -kdy * wi])
            left_i = jnp.stack([wi, k2r2 * wi, kdx * wr, kdy * wr])
            term = jnp.dot(left_r, ep_r, precision=highest, preferred_element_type=jnp.float32)
            term = term + jnp.dot(left_i, ep_i, precision=highest, preferred_element_type=jnp.float32)
            return (total + term, jnp.stack([rr, ri]))
        start = jnp.zeros((4, COMPONENTS), jnp.float32)
        total, baseline_rows = lax.scan(step, start, (pidx, qidx, obs_r, obs_i, wblk))
        visibility_misfit = jnp.transpose(baseline_rows, (1, 0, 2)).reshape(2, BASELINE_TOTAL)
        return (total, visibility_misfit)
    totals, resids = lax.map(channel, (ks, jnp.transpose(observed, (1, 0, 2)), weights))
    sums = lax.optimization_barrier(jnp.sum(totals, axis=0))
    grad_comp = scale_terms(sums, amplitude, widths, residual_norm)
    grad_centre = jnp.stack([jax.ops.segment_sum(grad_comp[1], assign, num_segments=SOURCES), jax.ops.segment_sum(grad_comp[2], assign, num_segments=SOURCES)])
    residual = jnp.transpose(resids, (1, 0, 2))
    return (grad_comp, grad_centre, residual)
```

```python
import functools
import math

import jax
import jax.numpy as jnp
from jax import lax
from jax.experimental import pallas as pl
from jax.experimental.pallas import tpu as pltpu
from jax.sharding import PartitionSpec as P

F32 = jnp.float32
BF16 = jnp.bfloat16
LOGICAL = pl.DeviceIdType.LOGICAL
BLOCK_CHANNELS = 16
NU_ZERO = 50000000.0
NU_STEP = 36621.09375
NU_REF = 100000000.0
DK = NU_STEP / NU_REF
CHANS = 4
TWO_PI = 2.0 * math.pi
ENV_COEF = 2.0 * math.pi * math.pi

SIN_COEFS = (4.44288283, -7.30824115, 3.60628896, -0.8457636, 0.10920575)
COS_COEFS = (-1.4142135, 6.97885099, -5.73946117, 1.88356299, -0.31069819)

TERMS = (
    [(a, n - a, 0) for n in range(4) for a in range(n, -1, -1)]
    + [(a, n - a, 1) for n in range(3) for a in range(n, -1, -1)]
    + [(a, n - a, 2) for n in range(2) for a in range(n, -1, -1)]
)
ROWS = 24

Z_STEPS = (-2, 1, -1, 0)
STEPS = (2, 1, -1, 0)


def hops(off):
    return abs(off[0]) + abs(off[1]) + abs(off[2]) + 0.1 * off[3]


def far_first(offs):
    return sorted((o for o in offs if o != (0, 0, 0, 0)), key=lambda o: (hops(o), o), reverse=True)


GATHER = far_first([(dx, 0, dz, dc) for dx in STEPS for dz in Z_STEPS for dc in (0, 1)])
COLUMN = far_first([(0, 0, dz, dc) for dz in (4, 3, 2, 1, 0, -1, -2, -3) for dc in (0, 1)])
PLANE = far_first([(dx, dy, 0, 0) for dx in STEPS for dy in STEPS])
PARTNER = (0, 0, 4, 0)
SENDS_TO_ME = far_first(
    {((-dx + 1) % 4 - 1, (-dy + 1) % 4 - 1, (-dz + 3) % 8 - 3, dc) for dx, dy, dz, dc in GATHER + COLUMN + PLANE}
)


def here():
    bl = lax.axis_index("bl")
    src = lax.axis_index("src")
    return lax.div(bl, 8), lax.axis_index("ch"), src * 4 + lax.rem(lax.div(bl, 2), 4), lax.rem(bl, 2)


def device(me, off):
    x, y, z, core = me
    dx, dy, dz, dc = off
    x = lax.rem(x + (dx + 4), 4) if dx else x
    y = lax.rem(y + (dy + 4), 4) if dy else y
    z = lax.rem(z + (dz + 8), 8) if dz else z
    core = 1 - core if dc else core
    return lax.div(z, 4) * 128 + (x * 8 + lax.rem(z, 4) * 2 + core) * 4 + y


def slot_of(off):
    dx, _, dz, dc = off
    return (dx % 4) * 8 + (dz % 4) * 2 + dc


def rows_iota(shape):
    return lax.broadcasted_iota(jnp.int32, shape, 0)


def one_of(rows, wanted):
    mask = None
    for w in wanted:
        mask = (rows == w) if mask is None else (mask | (rows == w))
    return mask


def pick(rows, pairs, other=0.0):
    out = other
    for wanted, value in pairs:
        if wanted:
            out = jnp.where(one_of(rows, wanted), value, out)
    return out


def monomials(u, v, w, shape):
    rows = rows_iota(shape)

    def power(base, which, top):
        out = jnp.ones(shape, F32)
        p = base
        for n in range(1, top + 1):
            wanted = [j for j, t in enumerate(TERMS) if t[which] == n]
            out = jnp.where(one_of(rows, wanted), jnp.broadcast_to(p, shape), out)
            p = p * base
        return out

    prod = power(u, 0, 3) * power(v, 1, 3) * power(w, 2, 2)
    return jnp.where(rows < len(TERMS), prod, 0.0)


def channel_factors(k_mid, lanes):
    shape = (ROWS, lanes)
    rows = rows_iota(shape)
    consts = []
    for j, (a, b, e) in enumerate(TERMS):
        n = a + b
        sign = -1.0 if (n // 2) % 2 else 1.0
        consts.append(([j], sign * TWO_PI**n / (math.factorial(a) * math.factorial(b) * math.factorial(e))))
    base = pick(rows, consts) + jnp.zeros(shape, F32)
    out = []
    for f in range(CHANS):
        delta = (f - 0.5 * (CHANS - 1)) * DK
        kappa = (-ENV_COEF * delta) * (2.0 * k_mid + delta)
        phase = pick(
            rows,
            [([j for j, t in enumerate(TERMS) if t[0] + t[1] == n], delta**n) for n in range(1, 4)],
            1.0,
        )
        env = jnp.where(
            one_of(rows, [j for j, t in enumerate(TERMS) if t[2] == 1]),
            kappa,
            jnp.where(one_of(rows, [j for j, t in enumerate(TERMS) if t[2] == 2]), kappa * kappa, 1.0),
        )
        out.append(base * phase * env)
    return out


def split2(x):
    high = x.astype(BF16)
    return high, (x - high.astype(F32)).astype(BF16)


def split3(x):
    high = x.astype(BF16)
    rest = x - high.astype(F32)
    mid = rest.astype(BF16)
    return high, mid, (rest - mid.astype(F32)).astype(BF16)


def kernel(
    obs_h, wts_h, pairs_h, pos_h, cen_h, asg_h, amp_h, off_h, wid_h, blk_s,
    comp_o, centre_o, res_o,
    obs_v, wts_v, pairs_v, pos_v, cen_v, asg_v, amp_v, off_v, wid_v,
    table, comp, lcol, mcol, wcol, ep, part, recv_a, part_b, recv_b, resid,
    in_sem, gat_s, gat_r, cmp_s, cmp_r, res_s, res_r, a_s, a_r, b_s, b_r,
):
    me = here()
    x_me, y_me, z_me, core_me = me
    src = lax.axis_index("src")
    z_low = lax.rem(z_me, 4)
    half = src * 256
    barrier = pltpu.get_barrier_semaphore()
    for off in SENDS_TO_ME:
        pl.semaphore_signal(barrier, 1, device_id=device(me, off), device_id_type=LOGICAL)

    halves = pl.ds(pl.multiple_of(half, 256), 256)
    loads = [
        pltpu.make_async_copy(a, b, in_sem.at[i])
        for i, (a, b) in enumerate(
            [
                (pos_h, pos_v), (cen_h, cen_v), (asg_h, asg_v), (amp_h, amp_v), (off_h, off_v), (wid_h, wid_v),
                (pairs_h.at[:, halves], pairs_v), (obs_h.at[:, :, halves], obs_v), (wts_h.at[:, halves], wts_v),
            ]
        )
    ]
    for load in loads:
        load.start()

    loads[0].wait()
    lane = lax.broadcasted_iota(jnp.int32, (16, 128), 1)
    sub = rows_iota((16, 128))
    spread = jnp.where(lane == sub, pos_v[:, 0:1], 0.0) + jnp.where(lane == sub + 16, pos_v[:, 1:2], 0.0)
    table[0] = jnp.sum(spread, axis=0, keepdims=True)

    for load in loads[1:6]:
        load.wait()
    assign = asg_v[...]
    onehot = (jnp.broadcast_to(assign, (32, 256)) == rows_iota((32, 256))).astype(BF16)
    cen_parts = split3(cen_v[...])
    centre = sum(jnp.dot(p, onehot, preferred_element_type=F32) for p in cen_parts)
    lm = centre + off_v[...]
    width = wid_v[...]
    rows8 = rows_iota((8, 256))
    comp[src] = pick(
        rows8,
        [
            ([0], lm[0:1, :]), ([1], lm[1:2, :]), ([2], width * width), ([3], amp_v[...]), ([4], width),
            ([5], assign.astype(F32)),
        ],
    )

    pl.semaphore_wait(barrier, len(SENDS_TO_ME))

    send_comp = pltpu.make_async_remote_copy(
        src_ref=comp.at[src], dst_ref=comp.at[src], send_sem=cmp_s, recv_sem=cmp_r,
        device_id=device(me, PARTNER), device_id_type=LOGICAL,
    )
    send_comp.start()
    for off in GATHER:
        pltpu.make_async_remote_copy(
            src_ref=table.at[0], dst_ref=table.at[slot_of(off)], send_sem=gat_s, recv_sem=gat_r,
            device_id=device(me, off), device_id_type=LOGICAL,
        ).start()

    first = blk_s[0] * BLOCK_CHANNELS + lax.axis_index("ch") * CHANS
    k_mid = (NU_ZERO + (first.astype(F32) + 0.5 * (CHANS - 1)) * NU_STEP) / NU_REF
    ks = [(NU_ZERO + (first + f).astype(F32) * NU_STEP) / NU_REF for f in range(CHANS)]
    gs = channel_factors(k_mid, 256)
    loads[6].wait()
    ant = pairs_v[...]
    shard = lax.shift_right_logical(ant, 4)
    slot = (
        ((x_me - lax.shift_right_logical(shard, 3)) & 3) * 8
        + ((z_low - lax.shift_right_logical(shard, 1)) & 3) * 2
        + ((core_me - shard) & 1)
    )
    inner = ant & 15
    rows32 = rows_iota((32, 128))

    send_comp.wait_recv()
    both = jnp.concatenate([comp[0], comp[1]], axis=1)
    l_row, m_row, w2_row = both[0:1, :], both[1:2, :], both[2:3, :]
    amp_row, w_row = both[3:4, :], both[4:5, :]
    mono = monomials(l_row, m_row, w2_row, (ROWS, 512))
    amp_high, amp_low = split2(mono * amp_row)
    mono_amp = jnp.concatenate([amp_high, amp_low], axis=0)
    cols = jnp.transpose(both)
    lcol[...] = jnp.broadcast_to(cols[:, 0:1], (512, 128))
    mcol[...] = jnp.broadcast_to(cols[:, 1:2], (512, 128))
    wcol[...] = jnp.broadcast_to(cols[:, 2:3], (512, 128))

    pltpu.make_async_copy(table.at[pl.ds(1, 31)], table.at[pl.ds(1, 31)], gat_r).wait()
    sites = table[:, 0, :]
    delta_x, delta_y = [], []
    for t in range(2):
        lanes = slice(128 * t, 128 * t + 128)
        got = []
        for shift in (0, 16):
            total = 0.0
            for a in range(2):
                idx = jnp.broadcast_to(inner[a : a + 1, lanes] + shift, (32, 128))
                val = jnp.take_along_axis(sites, idx, axis=1, mode="promise_in_bounds")
                val = jnp.where(jnp.broadcast_to(slot[a : a + 1, lanes], (32, 128)) == rows32, val, 0.0)
                total = total + val if a == 0 else total - val
            got.append(jnp.sum(total, axis=0, keepdims=True))
        delta_x.append(got[0])
        delta_y.append(got[1])
    dx = jnp.concatenate(delta_x, axis=1)
    dy = jnp.concatenate(delta_y, axis=1)
    r2 = dx * dx + dy * dy

    kx = [k_mid * d for d in delta_x]
    ky = [k_mid * d for d in delta_y]
    er = [
        (-ENV_COEF * math.log2(math.e)) * (k_mid * k_mid) * (delta_x[t] * delta_x[t] + delta_y[t] * delta_y[t])
        for t in range(2)
    ]

    for i in range(32):
        rows = slice(16 * i, 16 * i + 16)
        lc, mc, wc = lcol[rows, :], mcol[rows, :], wcol[rows, :]
        for t in range(2):
            turns = lc * kx[t] + mc * ky[t]
            env = jnp.exp2(wc * er[t])
            r = turns - jnp.round(turns)
            y = r * r
            s = SIN_COEFS[-1]
            for coef in SIN_COEFS[-2::-1]:
                s = s * y + coef
            s = s * r
            c = COS_COEFS[-1]
            for coef in COS_COEFS[-2::-1]:
                c = c * y + coef
            ep_r = env * (1.0 - s * s)
            ep_i = env * (s * c)
            lo = 128 * t
            high, low = split2(ep_r)
            ep[rows, lo : lo + 128] = high
            ep[rows, 256 + lo : 384 + lo] = low
            high, low = split2(ep_i)
            ep[rows, 512 + lo : 640 + lo] = high
            ep[rows, 768 + lo : 896 + lo] = low

    m_all = jnp.dot(mono_amp, ep[...], preferred_element_type=F32)
    m_all = m_all[0:ROWS] + m_all[ROWS:]
    m_r = m_all[:, 0:256] + m_all[:, 256:512]
    m_i = m_all[:, 512:768] + m_all[:, 768:1024]
    rows24 = rows_iota((ROWS, 256))
    odd = one_of(rows24, [j for j, t in enumerate(TERMS) if (t[0] + t[1]) % 2])
    base = monomials(dx, dy, r2, (ROWS, 256))
    n_r = base * jnp.where(odd, m_i, m_r)
    n_i = base * jnp.where(odd, -m_r, m_i)
    loads[7].wait()
    loads[8].wait()
    zero = jnp.zeros((ROWS, 256), F32)
    a0, d0, a1, d1, a2, d2 = zero, zero, zero, zero, zero, zero
    resids = []
    for f in range(CHANS):
        v_r = jnp.sum(gs[f] * n_r, axis=0, keepdims=True)
        v_i = jnp.sum(gs[f] * n_i, axis=0, keepdims=True)
        rr = obs_v[0, f : f + 1, :] - v_r
        ri = obs_v[1, f : f + 1, :] - v_i
        resids.append((rr, ri))
        wr = wts_v[f : f + 1, :] * rr
        wi = wts_v[f : f + 1, :] * ri
        k = ks[f]
        a0 += gs[f] * wr
        d0 += gs[f] * wi
        a1 += gs[f] * (k * wr)
        d1 += gs[f] * (k * wi)
        a2 += gs[f] * (k * k * wr)
        d2 += gs[f] * (k * k * wi)
    resid[src] = pick(
        rows8, [([f], resids[f][0]) for f in range(CHANS)] + [([4 + f], resids[f][1]) for f in range(CHANS)]
    )
    send_resid = pltpu.make_async_remote_copy(
        src_ref=resid.at[src], dst_ref=resid.at[src], send_sem=res_s, recv_sem=res_r,
        device_id=device(me, PARTNER), device_id_type=LOGICAL,
    )
    send_resid.start()

    def sides(a, d):
        return jnp.where(odd, -d, a) * base, jnp.where(odd, a, d) * base

    c0, s0 = sides(a0, d0)
    c1, s1 = sides(a1, d1)
    c2, s2 = sides(a2, d2)
    left_r = jnp.concatenate([c0, c2 * r2, -s1 * dx, -s1 * dy], axis=0)
    left_i = jnp.concatenate([s0, s2 * r2, c1 * dx, c1 * dy], axis=0)
    lr = jnp.concatenate(split2(left_r), axis=0)
    li = jnp.concatenate(split2(left_i), axis=0)
    left = jnp.concatenate([lr, lr, li, li], axis=1)
    y_all = lax.dot_general(left, ep[...], (((1,), (1,)), ((), ())), preferred_element_type=F32)
    y_all = y_all[0 : 4 * ROWS] + y_all[4 * ROWS :]
    sums = [
        jnp.sum(y_all[q * ROWS : (q + 1) * ROWS] * mono, axis=0, keepdims=True) for q in range(4)
    ]
    norm = 1.0 / math.sqrt(16384 * BLOCK_CHANNELS)
    grads = [
        -norm * sums[0],
        (-norm * TWO_PI) * amp_row * sums[2],
        (-norm * TWO_PI) * amp_row * sums[3],
        (norm * 2.0 * TWO_PI * math.pi) * amp_row * w_row * sums[1],
    ]

    onehot_all = (jnp.broadcast_to(both[5:6, :], (32, 512)) == rows_iota((32, 512)).astype(F32)).astype(BF16)
    gl, gm = split3(grads[1]), split3(grads[2])
    wide = lax.dot_general(
        jnp.concatenate(list(gl) + list(gm), axis=0), onehot_all, (((1,), (1,)), ((), ())),
        preferred_element_type=F32,
    )
    cen_l = wide[0:1, :] + wide[1:2, :] + wide[2:3, :]
    cen_m = wide[3:4, :] + wide[4:5, :] + wide[5:6, :]
    cen_rows = jnp.concatenate([cen_l, cen_m, jnp.zeros((1, 64), F32)], axis=1)
    for s in range(2):
        rows = rows_iota((8, 128))
        tile = 0.0
        for h in range(2):
            lo = 256 * s + 128 * h
            for q in range(4):
                tile = jnp.where(rows == 4 * h + q, grads[q][:, lo : lo + 128], tile)
        part[s, 0:8, :] = tile
        part[s, 8:16, :] = jnp.broadcast_to(cen_rows, (8, 128))

    for i, off in enumerate(COLUMN):
        to = lax.div(lax.rem(z_me + (off[2] + 8), 8), 4)
        pltpu.make_async_remote_copy(
            src_ref=part.at[to], dst_ref=recv_a.at[i], send_sem=a_s, recv_sem=a_r,
            device_id=device(me, off), device_id_type=LOGICAL,
        ).start()
    pltpu.make_async_copy(recv_a, recv_a, a_r).wait()
    total = part[src]
    for i in range(15):
        total = total + recv_a[i]
    part_b[...] = total
    for i, off in enumerate(PLANE):
        pltpu.make_async_remote_copy(
            src_ref=part_b, dst_ref=recv_b.at[i], send_sem=b_s, recv_sem=b_r,
            device_id=device(me, off), device_id_type=LOGICAL,
        ).start()
    send_resid.wait_recv()
    for h in range(2):
        res_o[0, :, 256 * h : 256 * h + 256] = resid[h, 0:4, :]
        res_o[1, :, 256 * h : 256 * h + 256] = resid[h, 4:8, :]
    pltpu.make_async_copy(recv_b, recv_b, b_r).wait()
    for i in range(15):
        total = total + recv_b[i]
    comp_o[:, 0:128] = total[0:4, :]
    comp_o[:, 128:256] = total[4:8, :]
    centre_o[0:1, :] = total[8:9, 0:32]
    centre_o[1:2, :] = total[8:9, 32:64]

    send_comp.wait_send()
    send_resid.wait_send()
    pltpu.make_async_copy(table.at[pl.ds(1, 31)], table.at[pl.ds(1, 31)], gat_s).wait()
    pltpu.make_async_copy(recv_a, recv_a, a_s).wait()
    pltpu.make_async_copy(recv_b, recv_b, b_s).wait()


def on_device(observed, weights, pairs, positions, centres, assign, amplitude, offsets, widths, block_index):
    dma = pltpu.SemaphoreType.DMA
    return pl.pallas_call(
        kernel,
        out_shape=(
            jax.ShapeDtypeStruct((4, 256), F32),
            jax.ShapeDtypeStruct((2, 32), F32),
            jax.ShapeDtypeStruct((2, 4, 512), F32),
        ),
        in_specs=[pl.BlockSpec(memory_space=pl.ANY)] * 9 + [pl.BlockSpec(memory_space=pltpu.SMEM)],
        out_specs=tuple([pl.BlockSpec(memory_space=pltpu.VMEM)] * 3),
        scratch_shapes=[
            pltpu.VMEM((2, 4, 256), F32),
            pltpu.VMEM((4, 256), F32),
            pltpu.VMEM((2, 256), jnp.int32),
            pltpu.VMEM((16, 2), F32),
            pltpu.VMEM((2, 32), F32),
            pltpu.VMEM((1, 256), jnp.int32),
            pltpu.VMEM((1, 256), F32),
            pltpu.VMEM((2, 256), F32),
            pltpu.VMEM((1, 256), F32),
            pltpu.VMEM((32, 1, 128), F32),
            pltpu.VMEM((2, 8, 256), F32),
            pltpu.VMEM((512, 128), F32),
            pltpu.VMEM((512, 128), F32),
            pltpu.VMEM((512, 128), F32),
            pltpu.VMEM((512, 1024), BF16),
            pltpu.VMEM((2, 16, 128), F32),
            pltpu.VMEM((15, 16, 128), F32),
            pltpu.VMEM((16, 128), F32),
            pltpu.VMEM((15, 16, 128), F32),
            pltpu.VMEM((2, 8, 256), F32),
            dma((9,)),
        ]
        + [dma(())] * 10,
        compiler_params=pltpu.CompilerParams(
            collective_id=0, has_side_effects=True, vmem_limit_bytes=32 * 1024 * 1024
        ),
        name="refit",
    )(
        observed, weights, pairs, positions, centres, assign.reshape(1, 256), amplitude.reshape(1, 256), offsets,
        widths.reshape(1, 256), block_index,
    )


def solution(mesh):
    placed = (
        P(None, "ch", "bl"),
        P("ch", "bl"),
        P(None, "bl"),
        P("bl", None),
        P(),
        P("src"),
        P("src"),
        P(None, "src"),
        P("src"),
        P(),
    )
    return jax.shard_map(
        on_device,
        mesh=mesh,
        in_specs=placed,
        out_specs=(P(None, "src"), P(), P(None, "ch", "bl")),
        check_vma=False,
    )
```

```python
import functools
import math

import jax
import jax.numpy as jnp
from jax import lax
from jax.experimental import pallas as pl
from jax.experimental.pallas import tpu as pltpu
from jax.sharding import PartitionSpec as P

F32 = jnp.float32
BF16 = jnp.bfloat16
LOGICAL = pl.DeviceIdType.LOGICAL
BLOCK_CHANNELS = 16
NU_ZERO = 50000000.0
NU_STEP = 36621.09375
NU_REF = 100000000.0
DK = NU_STEP / NU_REF
CHANS = 4
TWO_PI = 2.0 * math.pi
ENV_COEF = 2.0 * math.pi * math.pi

SIN_COEFS = (4.44288283, -7.30824115, 3.60628896, -0.8457636, 0.10920575)
COS_COEFS = (-1.4142135, 6.97885099, -5.73946117, 1.88356299, -0.31069819)

TERMS = (
    [(a, n - a, 0) for n in range(4) for a in range(n, -1, -1)]
    + [(a, n - a, 1) for n in range(3) for a in range(n, -1, -1)]
    + [(a, n - a, 2) for n in range(2) for a in range(n, -1, -1)]
)
ROWS = 24

Z_STEPS = (-2, 1, -1, 0)
STEPS = (2, 1, -1, 0)


def hops(off):
    return abs(off[0]) + abs(off[1]) + abs(off[2]) + 0.1 * off[3]


def far_first(offs):
    return sorted((o for o in offs if o != (0, 0, 0, 0)), key=lambda o: (hops(o), o), reverse=True)


GATHER = far_first([(dx, 0, dz, dc) for dx in STEPS for dz in Z_STEPS for dc in (0, 1)])
COLUMN = far_first([(0, 0, dz, dc) for dz in (4, 3, 2, 1, 0, -1, -2, -3) for dc in (0, 1)])
PLANE = far_first([(dx, dy, 0, 0) for dx in STEPS for dy in STEPS])
PARTNER = (0, 0, 4, 0)
SENDS_TO_ME = far_first(
    {((-dx + 1) % 4 - 1, (-dy + 1) % 4 - 1, (-dz + 3) % 8 - 3, dc) for dx, dy, dz, dc in GATHER + COLUMN + PLANE}
)


def here():
    bl = lax.axis_index("bl")
    src = lax.axis_index("src")
    return lax.div(bl, 8), lax.axis_index("ch"), src * 4 + lax.rem(lax.div(bl, 2), 4), lax.rem(bl, 2)


def device(me, off):
    x, y, z, core = me
    dx, dy, dz, dc = off
    x = lax.rem(x + (dx + 4), 4) if dx else x
    y = lax.rem(y + (dy + 4), 4) if dy else y
    z = lax.rem(z + (dz + 8), 8) if dz else z
    core = 1 - core if dc else core
    return lax.div(z, 4) * 128 + (x * 8 + lax.rem(z, 4) * 2 + core) * 4 + y


def slot_of(off):
    dx, _, dz, dc = off
    return (dx % 4) * 8 + (dz % 4) * 2 + dc


def rows_iota(shape):
    return lax.broadcasted_iota(jnp.int32, shape, 0)


def one_of(rows, wanted):
    mask = None
    for w in wanted:
        mask = (rows == w) if mask is None else (mask | (rows == w))
    return mask


def pick(rows, pairs, other=0.0):
    out = other
    for wanted, value in pairs:
        if wanted:
            out = jnp.where(one_of(rows, wanted), value, out)
    return out


def monomials(u, v, w, shape):
    rows = rows_iota(shape)

    def power(base, which, top):
        out = jnp.ones(shape, F32)
        p = base
        for n in range(1, top + 1):
            wanted = [j for j, t in enumerate(TERMS) if t[which] == n]
            out = jnp.where(one_of(rows, wanted), jnp.broadcast_to(p, shape), out)
            p = p * base
        return out

    prod = power(u, 0, 3) * power(v, 1, 3) * power(w, 2, 2)
    return jnp.where(rows < len(TERMS), prod, 0.0)


def channel_factors(k_mid, lanes):
    shape = (ROWS, lanes)
    rows = rows_iota(shape)
    consts = []
    for j, (a, b, e) in enumerate(TERMS):
        n = a + b
        sign = -1.0 if (n // 2) % 2 else 1.0
        consts.append(([j], sign * TWO_PI**n / (math.factorial(a) * math.factorial(b) * math.factorial(e))))
    base = pick(rows, consts) + jnp.zeros(shape, F32)
    out = []
    for f in range(CHANS):
        delta = (f - 0.5 * (CHANS - 1)) * DK
        kappa = (-ENV_COEF * delta) * (2.0 * k_mid + delta)
        phase = pick(
            rows,
            [([j for j, t in enumerate(TERMS) if t[0] + t[1] == n], delta**n) for n in range(1, 4)],
            1.0,
        )
        env = jnp.where(
            one_of(rows, [j for j, t in enumerate(TERMS) if t[2] == 1]),
            kappa,
            jnp.where(one_of(rows, [j for j, t in enumerate(TERMS) if t[2] == 2]), kappa * kappa, 1.0),
        )
        out.append(base * phase * env)
    return out


def split2(x):
    high = x.astype(BF16)
    return high, (x - high.astype(F32)).astype(BF16)


def split3(x):
    high = x.astype(BF16)
    rest = x - high.astype(F32)
    mid = rest.astype(BF16)
    return high, mid, (rest - mid.astype(F32)).astype(BF16)


def kernel(
    obs_h, wts_h, pairs_h, pos_h, cen_h, asg_h, amp_h, off_h, wid_h, blk_s,
    comp_o, centre_o, res_o,
    obs_v, wts_v, pairs_v, pos_v, cen_v, asg_v, amp_v, off_v, wid_v,
    table, comp, lcol, mcol, wcol, ep, part, recv_a, part_b, recv_b, resid,
    in_sem, gat_s, gat_r, cmp_s, cmp_r, res_s, res_r, a_s, a_r, b_s, b_r,
):
    me = here()
    x_me, y_me, z_me, core_me = me
    src = lax.axis_index("src")
    z_low = lax.rem(z_me, 4)
    half = src * 256
    barrier = pltpu.get_barrier_semaphore()
    for off in SENDS_TO_ME:
        pl.semaphore_signal(barrier, 1, device_id=device(me, off), device_id_type=LOGICAL)

    halves = pl.ds(pl.multiple_of(half, 256), 256)
    loads = [
        pltpu.make_async_copy(a, b, in_sem.at[i])
        for i, (a, b) in enumerate(
            [
                (pos_h, pos_v), (cen_h, cen_v), (asg_h, asg_v), (amp_h, amp_v), (off_h, off_v), (wid_h, wid_v),
                (pairs_h.at[:, halves], pairs_v), (obs_h.at[:, :, halves], obs_v), (wts_h.at[:, halves], wts_v),
            ]
        )
    ]
    for load in loads:
        load.start()

    loads[0].wait()
    table[0] = jnp.concatenate([pos_v[0:1, :], pos_v[1:2, :], jnp.zeros((1, 96), F32)], axis=1)

    for load in loads[1:6]:
        load.wait()
    assign = asg_v[...]
    onehot = (jnp.broadcast_to(assign, (32, 256)) == rows_iota((32, 256))).astype(BF16)
    cen_parts = split3(cen_v[...])
    centre = sum(jnp.dot(p, onehot, preferred_element_type=F32) for p in cen_parts)
    lm = centre + off_v[...]
    width = wid_v[...]
    rows8 = rows_iota((8, 256))
    comp[src] = pick(
        rows8,
        [
            ([0], lm[0:1, :]), ([1], lm[1:2, :]), ([2], width * width), ([3], amp_v[...]), ([4], width),
            ([5], assign.astype(F32)),
        ],
    )

    pl.semaphore_wait(barrier, len(SENDS_TO_ME))

    send_comp = pltpu.make_async_remote_copy(
        src_ref=comp.at[src], dst_ref=comp.at[src], send_sem=cmp_s, recv_sem=cmp_r,
        device_id=device(me, PARTNER), device_id_type=LOGICAL,
    )
    send_comp.start()
    for off in GATHER:
        pltpu.make_async_remote_copy(
            src_ref=table.at[0], dst_ref=table.at[slot_of(off)], send_sem=gat_s, recv_sem=gat_r,
            device_id=device(me, off), device_id_type=LOGICAL,
        ).start()

    first = blk_s[0] * BLOCK_CHANNELS + lax.axis_index("ch") * CHANS
    k_mid = (NU_ZERO + (first.astype(F32) + 0.5 * (CHANS - 1)) * NU_STEP) / NU_REF
    ks = [(NU_ZERO + (first + f).astype(F32) * NU_STEP) / NU_REF for f in range(CHANS)]
    gs = channel_factors(k_mid, 256)
    loads[6].wait()
    ant = pairs_v[...]
    shard = lax.shift_right_logical(ant, 4)
    slot = (
        ((x_me - lax.shift_right_logical(shard, 3)) & 3) * 8
        + ((z_low - lax.shift_right_logical(shard, 1)) & 3) * 2
        + ((core_me - shard) & 1)
    )
    inner = ant & 15
    rows32 = rows_iota((32, 128))

    send_comp.wait_recv()
    both = jnp.concatenate([comp[0], comp[1]], axis=1)
    l_row, m_row, w2_row = both[0:1, :], both[1:2, :], both[2:3, :]
    amp_row, w_row = both[3:4, :], both[4:5, :]
    mono = monomials(l_row, m_row, w2_row, (ROWS, 512))
    amp_high, amp_low = split2(mono * amp_row)
    mono_amp = jnp.concatenate([amp_high, amp_low], axis=0)
    cols = jnp.transpose(both)
    lcol[...] = jnp.broadcast_to(cols[:, 0:1], (512, 128))
    mcol[...] = jnp.broadcast_to(cols[:, 1:2], (512, 128))
    wcol[...] = jnp.broadcast_to(cols[:, 2:3], (512, 128))

    pltpu.make_async_copy(table.at[pl.ds(1, 31)], table.at[pl.ds(1, 31)], gat_r).wait()
    sites = table[:, 0, :]
    delta_x, delta_y = [], []
    for t in range(2):
        lanes = slice(128 * t, 128 * t + 128)
        got = []
        for shift in (0, 16):
            total = 0.0
            for a in range(2):
                idx = jnp.broadcast_to(inner[a : a + 1, lanes] + shift, (32, 128))
                val = jnp.take_along_axis(sites, idx, axis=1, mode="promise_in_bounds")
                val = jnp.where(jnp.broadcast_to(slot[a : a + 1, lanes], (32, 128)) == rows32, val, 0.0)
                total = total + val if a == 0 else total - val
            got.append(jnp.sum(total, axis=0, keepdims=True))
        delta_x.append(got[0])
        delta_y.append(got[1])
    dx = jnp.concatenate(delta_x, axis=1)
    dy = jnp.concatenate(delta_y, axis=1)
    r2 = dx * dx + dy * dy

    kx = [k_mid * d for d in delta_x]
    ky = [k_mid * d for d in delta_y]
    er = [
        (-ENV_COEF * math.log2(math.e)) * (k_mid * k_mid) * (delta_x[t] * delta_x[t] + delta_y[t] * delta_y[t])
        for t in range(2)
    ]

    for i in range(32):
        rows = slice(16 * i, 16 * i + 16)
        lc, mc, wc = lcol[rows, :], mcol[rows, :], wcol[rows, :]
        for t in range(2):
            turns = lc * kx[t] + mc * ky[t]
            env = jnp.exp2(wc * er[t])
            r = turns - jnp.round(turns)
            y = r * r
            s = SIN_COEFS[-1]
            for coef in SIN_COEFS[-2::-1]:
                s = s * y + coef
            s = s * r
            c = COS_COEFS[-1]
            for coef in COS_COEFS[-2::-1]:
                c = c * y + coef
            ep_r = env * (1.0 - s * s)
            ep_i = env * (s * c)
            lo = 128 * t
            high, low = split2(ep_r)
            ep[rows, lo : lo + 128] = high
            ep[rows, 256 + lo : 384 + lo] = low
            high, low = split2(ep_i)
            ep[rows, 512 + lo : 640 + lo] = high
            ep[rows, 768 + lo : 896 + lo] = low

    m_all = jnp.dot(mono_amp, ep[...], preferred_element_type=F32)
    m_all = m_all[0:ROWS] + m_all[ROWS:]
    m_r = m_all[:, 0:256] + m_all[:, 256:512]
    m_i = m_all[:, 512:768] + m_all[:, 768:1024]
    rows24 = rows_iota((ROWS, 256))
    odd = one_of(rows24, [j for j, t in enumerate(TERMS) if (t[0] + t[1]) % 2])
    base = monomials(dx, dy, r2, (ROWS, 256))
    n_r = base * jnp.where(odd, m_i, m_r)
    n_i = base * jnp.where(odd, -m_r, m_i)
    loads[7].wait()
    loads[8].wait()
    zero = jnp.zeros((ROWS, 256), F32)
    a0, d0, a1, d1, a2, d2 = zero, zero, zero, zero, zero, zero
    resids = []
    for f in range(CHANS):
        v_r = jnp.sum(gs[f] * n_r, axis=0, keepdims=True)
        v_i = jnp.sum(gs[f] * n_i, axis=0, keepdims=True)
        rr = obs_v[0, f : f + 1, :] - v_r
        ri = obs_v[1, f : f + 1, :] - v_i
        resids.append((rr, ri))
        wr = wts_v[f : f + 1, :] * rr
        wi = wts_v[f : f + 1, :] * ri
        k = ks[f]
        a0 += gs[f] * wr
        d0 += gs[f] * wi
        a1 += gs[f] * (k * wr)
        d1 += gs[f] * (k * wi)
        a2 += gs[f] * (k * k * wr)
        d2 += gs[f] * (k * k * wi)
    resid[src] = pick(
        rows8, [([f], resids[f][0]) for f in range(CHANS)] + [([4 + f], resids[f][1]) for f in range(CHANS)]
    )
    send_resid = pltpu.make_async_remote_copy(
        src_ref=resid.at[src], dst_ref=resid.at[src], send_sem=res_s, recv_sem=res_r,
        device_id=device(me, PARTNER), device_id_type=LOGICAL,
    )
    send_resid.start()

    def sides(a, d):
        return jnp.where(odd, -d, a) * base, jnp.where(odd, a, d) * base

    c0, s0 = sides(a0, d0)
    c1, s1 = sides(a1, d1)
    c2, s2 = sides(a2, d2)
    left_r = jnp.concatenate([c0, c2 * r2, -s1 * dx, -s1 * dy], axis=0)
    left_i = jnp.concatenate([s0, s2 * r2, c1 * dx, c1 * dy], axis=0)
    lr = jnp.concatenate(split2(left_r), axis=0)
    li = jnp.concatenate(split2(left_i), axis=0)
    left = jnp.concatenate([lr, lr, li, li], axis=1)
    y_all = lax.dot_general(left, ep[...], (((1,), (1,)), ((), ())), preferred_element_type=F32)
    y_all = y_all[0 : 4 * ROWS] + y_all[4 * ROWS :]
    sums = [
        jnp.sum(y_all[q * ROWS : (q + 1) * ROWS] * mono, axis=0, keepdims=True) for q in range(4)
    ]
    norm = 1.0 / math.sqrt(16384 * BLOCK_CHANNELS)
    grads = [
        -norm * sums[0],
        (-norm * TWO_PI) * amp_row * sums[2],
        (-norm * TWO_PI) * amp_row * sums[3],
        (norm * 2.0 * TWO_PI * math.pi) * amp_row * w_row * sums[1],
    ]

    onehot_all = (jnp.broadcast_to(both[5:6, :], (32, 512)) == rows_iota((32, 512)).astype(F32)).astype(BF16)
    gl, gm = split3(grads[1]), split3(grads[2])
    wide = lax.dot_general(
        jnp.concatenate(list(gl) + list(gm), axis=0), onehot_all, (((1,), (1,)), ((), ())),
        preferred_element_type=F32,
    )
    cen_l = wide[0:1, :] + wide[1:2, :] + wide[2:3, :]
    cen_m = wide[3:4, :] + wide[4:5, :] + wide[5:6, :]
    cen_rows = jnp.concatenate([cen_l, cen_m, jnp.zeros((1, 64), F32)], axis=1)
    for s in range(2):
        rows = rows_iota((8, 128))
        tile = 0.0
        for h in range(2):
            lo = 256 * s + 128 * h
            for q in range(4):
                tile = jnp.where(rows == 4 * h + q, grads[q][:, lo : lo + 128], tile)
        part[s, 0:8, :] = tile
        part[s, 8:16, :] = jnp.broadcast_to(cen_rows, (8, 128))

    for i, off in enumerate(COLUMN):
        to = lax.div(lax.rem(z_me + (off[2] + 8), 8), 4)
        pltpu.make_async_remote_copy(
            src_ref=part.at[to], dst_ref=recv_a.at[i], send_sem=a_s, recv_sem=a_r,
            device_id=device(me, off), device_id_type=LOGICAL,
        ).start()
    pltpu.make_async_copy(recv_a, recv_a, a_r).wait()
    total = part[src]
    for i in range(15):
        total = total + recv_a[i]
    part_b[...] = total
    for i, off in enumerate(PLANE):
        pltpu.make_async_remote_copy(
            src_ref=part_b, dst_ref=recv_b.at[i], send_sem=b_s, recv_sem=b_r,
            device_id=device(me, off), device_id_type=LOGICAL,
        ).start()
    send_resid.wait_recv()
    for h in range(2):
        res_o[0, :, 256 * h : 256 * h + 256] = resid[h, 0:4, :]
        res_o[1, :, 256 * h : 256 * h + 256] = resid[h, 4:8, :]
    pltpu.make_async_copy(recv_b, recv_b, b_r).wait()
    for i in range(15):
        total = total + recv_b[i]
    comp_o[:, 0:128] = total[0:4, :]
    comp_o[:, 128:256] = total[4:8, :]
    centre_o[0:1, :] = total[8:9, 0:32]
    centre_o[1:2, :] = total[8:9, 32:64]

    send_comp.wait_send()
    send_resid.wait_send()
    pltpu.make_async_copy(table.at[pl.ds(1, 31)], table.at[pl.ds(1, 31)], gat_s).wait()
    pltpu.make_async_copy(recv_a, recv_a, a_s).wait()
    pltpu.make_async_copy(recv_b, recv_b, b_s).wait()


def deliver(*refs):
    sem = refs[6]
    moves = [pltpu.make_async_copy(refs[i], refs[3 + i], sem.at[i]) for i in range(3)]
    for move in moves:
        move.start()
    for move in moves:
        move.wait()


def on_device(observed, weights, pairs, positions, centres, assign, amplitude, offsets, widths, block_index):
    dma = pltpu.SemaphoreType.DMA
    operands = [
        pltpu.with_memory_space_constraint(v, pltpu.HBM)
        for v in (
            observed, weights, pairs, positions.T, centres, assign.reshape(1, 256), amplitude.reshape(1, 256), offsets,
            widths.reshape(1, 256),
        )
    ]
    sums = pl.pallas_call(
        kernel,
        out_shape=(
            jax.ShapeDtypeStruct((4, 256), F32),
            jax.ShapeDtypeStruct((2, 32), F32),
            jax.ShapeDtypeStruct((2, 4, 512), F32),
        ),
        in_specs=[pl.BlockSpec(memory_space=pltpu.HBM)] * 9 + [pl.BlockSpec(memory_space=pltpu.SMEM)],
        out_specs=tuple([pl.BlockSpec(memory_space=pltpu.VMEM)] * 3),
        scratch_shapes=[
            pltpu.VMEM((2, 4, 256), F32),
            pltpu.VMEM((4, 256), F32),
            pltpu.VMEM((2, 256), jnp.int32),
            pltpu.VMEM((2, 16), F32),
            pltpu.VMEM((2, 32), F32),
            pltpu.VMEM((1, 256), jnp.int32),
            pltpu.VMEM((1, 256), F32),
            pltpu.VMEM((2, 256), F32),
            pltpu.VMEM((1, 256), F32),
            pltpu.VMEM((32, 1, 128), F32),
            pltpu.VMEM((2, 8, 256), F32),
            pltpu.VMEM((512, 128), F32),
            pltpu.VMEM((512, 128), F32),
            pltpu.VMEM((512, 128), F32),
            pltpu.VMEM((512, 1024), BF16),
            pltpu.VMEM((2, 16, 128), F32),
            pltpu.VMEM((15, 16, 128), F32),
            pltpu.VMEM((16, 128), F32),
            pltpu.VMEM((15, 16, 128), F32),
            pltpu.VMEM((2, 8, 256), F32),
            dma((9,)),
        ]
        + [dma(())] * 10,
        compiler_params=pltpu.CompilerParams(
            collective_id=0, has_side_effects=True, vmem_limit_bytes=32 * 1024 * 1024
        ),
        name="refit",
    )(*operands, block_index)
    return pl.pallas_call(
        deliver,
        out_shape=tuple(jax.ShapeDtypeStruct(v.shape, F32) for v in sums),
        in_specs=[pl.BlockSpec(memory_space=pltpu.VMEM)] * 3,
        out_specs=tuple([pl.BlockSpec(memory_space=pltpu.HBM)] * 3),
        scratch_shapes=[dma((3,))],
        name="deliver",
    )(*(pltpu.with_memory_space_constraint(v, pltpu.VMEM) for v in sums))


def solution(mesh):
    placed = (
        P(None, "ch", "bl"),
        P("ch", "bl"),
        P(None, "bl"),
        P("bl", None),
        P(),
        P("src"),
        P("src"),
        P(None, "src"),
        P("src"),
        P(),
    )
    return jax.shard_map(
        on_device,
        mesh=mesh,
        in_specs=placed,
        out_specs=(P(None, "src"), P(), P(None, "ch", "bl")),
        check_vma=False,
    )
```

```python
import functools
import math

import jax
import jax.numpy as jnp
from jax import lax
from jax.experimental import pallas as pl
from jax.experimental.pallas import tpu as pltpu
from jax.sharding import PartitionSpec as P

F32 = jnp.float32
BF16 = jnp.bfloat16
LOGICAL = pl.DeviceIdType.LOGICAL
BLOCK_CHANNELS = 16
NU_ZERO = 50000000.0
NU_STEP = 36621.09375
NU_REF = 100000000.0
DK = NU_STEP / NU_REF
CHANS = 4
TWO_PI = 2.0 * math.pi
ENV_COEF = 2.0 * math.pi * math.pi

SIN_COEFS = (4.44288283, -7.30824115, 3.60628896, -0.8457636, 0.10920575)
COS_COEFS = (-1.4142135, 6.97885099, -5.73946117, 1.88356299, -0.31069819)

TERMS = (
    [(a, n - a, 0) for n in range(4) for a in range(n, -1, -1)]
    + [(a, n - a, 1) for n in range(3) for a in range(n, -1, -1)]
    + [(a, n - a, 2) for n in range(2) for a in range(n, -1, -1)]
)
ROWS = 24

STEPS = (2, 1, -1, 0)
Z_STEPS = (-2, 1, -1, 0)


def far_first(offs):
    return sorted((o for o in offs if o != (0, 0, 0)), key=lambda o: (sum(map(abs, o)), o), reverse=True)


GATHER = far_first([(dx, 0, dz) for dx in STEPS for dz in Z_STEPS])
COLUMN = far_first([(0, 0, dz) for dz in (4, 3, 2, 1, 0, -1, -2, -3)])
PLANE = far_first([(dx, dy, 0) for dx in STEPS for dy in STEPS])
PARTNER = (0, 0, 4)
GREET = far_first(
    {((-dx + 1) % 4 - 1, (-dy + 1) % 4 - 1, (-dz + 3) % 8 - 3) for dx, dy, dz in GATHER + COLUMN + PLANE}
)


def here():
    bl = lax.axis_index("bl")
    src = lax.axis_index("src")
    return lax.div(bl, 8), lax.axis_index("ch"), src * 4 + lax.rem(lax.div(bl, 2), 4), lax.rem(bl, 2)


def device(me, off, core):
    x, y, z, _ = me
    dx, dy, dz = off
    x = lax.rem(x + (dx + 4), 4) if dx else x
    y = lax.rem(y + (dy + 4), 4) if dy else y
    z = lax.rem(z + (dz + 8), 8) if dz else z
    return lax.div(z, 4) * 128 + (x * 8 + lax.rem(z, 4) * 2 + core) * 4 + y


def slot_of(off):
    return (off[0] % 4) * 4 + off[2] % 4


def send(src_ref, dst_ref, send_sem, recv_sem, to):
    return pltpu.make_async_remote_copy(
        src_ref=src_ref, dst_ref=dst_ref, send_sem=send_sem, recv_sem=recv_sem, device_id=to, device_id_type=LOGICAL
    )


def drain(ref, sem):
    pltpu.make_async_copy(ref, ref, sem).wait()


def rows_iota(shape):
    return lax.broadcasted_iota(jnp.int32, shape, 0)


def one_of(rows, wanted):
    mask = None
    for w in wanted:
        mask = (rows == w) if mask is None else (mask | (rows == w))
    return mask


def pick(rows, pairs, other=0.0):
    out = other
    for wanted, value in pairs:
        if wanted:
            out = jnp.where(one_of(rows, wanted), value, out)
    return out


def monomials(u, v, w, shape):
    rows = rows_iota(shape)

    def power(base, which, top):
        out = jnp.ones(shape, F32)
        p = base
        for n in range(1, top + 1):
            wanted = [j for j, t in enumerate(TERMS) if t[which] == n]
            out = jnp.where(one_of(rows, wanted), jnp.broadcast_to(p, shape), out)
            p = p * base
        return out

    prod = power(u, 0, 3) * power(v, 1, 3) * power(w, 2, 2)
    return jnp.where(rows < len(TERMS), prod, 0.0)


def channel_factors(k_mid, lanes):
    shape = (ROWS, lanes)
    rows = rows_iota(shape)
    consts = []
    for j, (a, b, e) in enumerate(TERMS):
        n = a + b
        sign = -1.0 if (n // 2) % 2 else 1.0
        consts.append(([j], sign * TWO_PI**n / (math.factorial(a) * math.factorial(b) * math.factorial(e))))
    base = pick(rows, consts) + jnp.zeros(shape, F32)
    out = []
    for f in range(CHANS):
        delta = (f - 0.5 * (CHANS - 1)) * DK
        kappa = (-ENV_COEF * delta) * (2.0 * k_mid + delta)
        phase = pick(
            rows,
            [([j for j, t in enumerate(TERMS) if t[0] + t[1] == n], delta**n) for n in range(1, 4)],
            1.0,
        )
        env = jnp.where(
            one_of(rows, [j for j, t in enumerate(TERMS) if t[2] == 1]),
            kappa,
            jnp.where(one_of(rows, [j for j, t in enumerate(TERMS) if t[2] == 2]), kappa * kappa, 1.0),
        )
        out.append(base * phase * env)
    return out


def split2(x):
    high = x.astype(BF16)
    return high, (x - high.astype(F32)).astype(BF16)


def split3(x):
    high = x.astype(BF16)
    rest = x - high.astype(F32)
    mid = rest.astype(BF16)
    return high, mid, (rest - mid.astype(F32)).astype(BF16)


def kernel(
    obs_h, wts_h, pairs_h, pos_h, cen_h, asg_h, amp_h, off_h, wid_h, blk_h,
    comp_o, centre_o, res_o,
    obs_v, wts_v, pairs_v, pos_v, cen_v, asg_v, amp_v, off_v, wid_v, blk_s,
    sibling, table, comp, lcol, mcol, wcol, ep, part, recv_a, recv_b, resid,
    in_sem, sib_s, sib_r, gat_s, gat_r, cmp_s, cmp_r, res_s, res_r, a_s, a_r, b_s, b_r,
):
    me = here()
    x_me, y_me, z_me, core_me = me
    src = lax.axis_index("src")
    z_low = lax.rem(z_me, 4)
    half = src * 256
    here0, here1 = device(me, (0, 0, 0), 0), device(me, (0, 0, 0), 1)
    is0, is1 = core_me == 0, core_me == 1
    barrier = pltpu.get_barrier_semaphore()
    pl.semaphore_signal(barrier, 1, device_id=jnp.where(is0, here1, here0), device_id_type=LOGICAL)
    for off in GREET:
        pl.semaphore_signal(barrier, 1, device_id=device(me, off, 1), device_id_type=LOGICAL)

    halves = pl.ds(pl.multiple_of(half, 256), 256)
    loads = [
        pltpu.make_async_copy(a, b, in_sem.at[i])
        for i, (a, b) in enumerate(
            [
                (pos_h, pos_v), (cen_h, cen_v), (asg_h, asg_v), (amp_h, amp_v), (off_h, off_v), (wid_h, wid_v),
                (pairs_h.at[:, halves], pairs_v), (obs_h.at[:, :, halves], obs_v), (wts_h.at[:, halves], wts_v), (blk_h, blk_s),
            ]
        )
    ]
    for load in loads:
        load.start()

    loads[0].wait()
    gap = jnp.zeros((1, 16), F32)
    xs, ys = pos_v[0:1, :], pos_v[1:2, :]
    tail = jnp.zeros((1, 64), F32)

    @pl.when(is0)
    def _():
        sibling[...] = jnp.concatenate([xs, gap, ys, gap, tail], axis=1)
        pl.semaphore_wait(barrier, 1)
        send(sibling, table.at[0], sib_s, sib_r, here1).start()

    @pl.when(is1)
    def _():
        sibling[...] = jnp.concatenate([gap, xs, gap, ys, tail], axis=1)

    for load in loads[1:6]:
        load.wait()
    assign = asg_v[...]
    onehot = (jnp.broadcast_to(assign, (32, 256)) == rows_iota((32, 256))).astype(BF16)
    cen_parts = split3(cen_v[...])
    centre = sum(jnp.dot(p, onehot, preferred_element_type=F32) for p in cen_parts)
    lm = centre + off_v[...]
    width = wid_v[...]
    rows8 = rows_iota((8, 256))
    comp[src] = pick(
        rows8,
        [
            ([0], lm[0:1, :]), ([1], lm[1:2, :]), ([2], width * width), ([3], amp_v[...]), ([4], width),
            ([5], assign.astype(F32)),
        ],
    )

    @pl.when(is1)
    def _():
        drain(table.at[0], sib_r)
        table[0] = table[0] + sibling[...]
        pl.semaphore_wait(barrier, 2 * len(GREET) + 1)
        for core in (0, 1):
            send(comp.at[src], comp.at[src], cmp_s.at[core], cmp_r, device(me, PARTNER, core)).start()
        for off in GATHER:
            for core in (0, 1):
                send(table.at[0], table.at[slot_of(off)], gat_s.at[core], gat_r, device(me, off, core)).start()
        send(table.at[0], table.at[0], gat_s.at[0], gat_r, here0).start()

    loads[6].wait()
    loads[9].wait()
    first = blk_s[0] * BLOCK_CHANNELS + lax.axis_index("ch") * CHANS
    k_mid = (NU_ZERO + (first.astype(F32) + 0.5 * (CHANS - 1)) * NU_STEP) / NU_REF
    ks = [(NU_ZERO + (first + f).astype(F32) * NU_STEP) / NU_REF for f in range(CHANS)]
    gs = channel_factors(k_mid, 256)
    ant = pairs_v[...]
    chip = lax.shift_right_logical(ant, 5)
    slot = ((x_me - lax.shift_right_logical(chip, 2)) & 3) * 4 + ((z_low - chip) & 3)
    inner = ant & 31
    rows16 = rows_iota((16, 128))

    drain(comp.at[0], cmp_r)
    both = jnp.concatenate([comp[0], comp[1]], axis=1)
    l_row, m_row, w2_row = both[0:1, :], both[1:2, :], both[2:3, :]
    amp_row, w_row = both[3:4, :], both[4:5, :]
    mono = monomials(l_row, m_row, w2_row, (ROWS, 512))
    amp_high, amp_low = split2(mono * amp_row)
    mono_amp = jnp.concatenate([amp_high, amp_low], axis=0)
    cols = jnp.transpose(both)
    lcol[...] = jnp.broadcast_to(cols[:, 0:1], (512, 128))
    mcol[...] = jnp.broadcast_to(cols[:, 1:2], (512, 128))
    wcol[...] = jnp.broadcast_to(cols[:, 2:3], (512, 128))

    @pl.when(is0)
    def _():
        drain(table, gat_r)

    @pl.when(is1)
    def _():
        drain(table.at[pl.ds(1, 15)], gat_r)

    sites = table[:, 0, :]
    delta_x, delta_y = [], []
    for t in range(2):
        lanes = slice(128 * t, 128 * t + 128)
        got = []
        for shift in (0, 32):
            total = 0.0
            for a in range(2):
                idx = jnp.broadcast_to(inner[a : a + 1, lanes] + shift, (16, 128))
                val = jnp.take_along_axis(sites, idx, axis=1, mode="promise_in_bounds")
                val = jnp.where(jnp.broadcast_to(slot[a : a + 1, lanes], (16, 128)) == rows16, val, 0.0)
                total = total + val if a == 0 else total - val
            got.append(jnp.sum(total, axis=0, keepdims=True))
        delta_x.append(got[0])
        delta_y.append(got[1])
    dx = jnp.concatenate(delta_x, axis=1)
    dy = jnp.concatenate(delta_y, axis=1)
    r2 = dx * dx + dy * dy

    kx = [k_mid * d for d in delta_x]
    ky = [k_mid * d for d in delta_y]
    er = [
        (-ENV_COEF * math.log2(math.e)) * (k_mid * k_mid) * (delta_x[t] * delta_x[t] + delta_y[t] * delta_y[t])
        for t in range(2)
    ]

    for i in range(32):
        rows = slice(16 * i, 16 * i + 16)
        lc, mc, wc = lcol[rows, :], mcol[rows, :], wcol[rows, :]
        for t in range(2):
            turns = lc * kx[t] + mc * ky[t]
            env = jnp.exp2(wc * er[t])
            r = turns - jnp.round(turns)
            y = r * r
            s = SIN_COEFS[-1]
            for coef in SIN_COEFS[-2::-1]:
                s = s * y + coef
            s = s * r
            c = COS_COEFS[-1]
            for coef in COS_COEFS[-2::-1]:
                c = c * y + coef
            ep_r = env * (1.0 - s * s)
            ep_i = env * (s * c)
            lo = 128 * t
            high, low = split2(ep_r)
            ep[rows, lo : lo + 128] = high
            ep[rows, 256 + lo : 384 + lo] = low
            high, low = split2(ep_i)
            ep[rows, 512 + lo : 640 + lo] = high
            ep[rows, 768 + lo : 896 + lo] = low

    m_all = jnp.dot(mono_amp, ep[...], preferred_element_type=F32)
    m_all = m_all[0:ROWS] + m_all[ROWS:]
    m_r = m_all[:, 0:256] + m_all[:, 256:512]
    m_i = m_all[:, 512:768] + m_all[:, 768:1024]
    rows24 = rows_iota((ROWS, 256))
    odd = one_of(rows24, [j for j, t in enumerate(TERMS) if (t[0] + t[1]) % 2])
    base = monomials(dx, dy, r2, (ROWS, 256))
    n_r = base * jnp.where(odd, m_i, m_r)
    n_i = base * jnp.where(odd, -m_r, m_i)
    loads[7].wait()
    loads[8].wait()
    zero = jnp.zeros((ROWS, 256), F32)
    a0, d0, a1, d1, a2, d2 = zero, zero, zero, zero, zero, zero
    resids = []
    for f in range(CHANS):
        v_r = jnp.sum(gs[f] * n_r, axis=0, keepdims=True)
        v_i = jnp.sum(gs[f] * n_i, axis=0, keepdims=True)
        rr = obs_v[0, f : f + 1, :] - v_r
        ri = obs_v[1, f : f + 1, :] - v_i
        resids.append((rr, ri))
        wr = wts_v[f : f + 1, :] * rr
        wi = wts_v[f : f + 1, :] * ri
        k = ks[f]
        a0 += gs[f] * wr
        d0 += gs[f] * wi
        a1 += gs[f] * (k * wr)
        d1 += gs[f] * (k * wi)
        a2 += gs[f] * (k * k * wr)
        d2 += gs[f] * (k * k * wi)
    resid[src] = pick(
        rows8, [([f], resids[f][0]) for f in range(CHANS)] + [([4 + f], resids[f][1]) for f in range(CHANS)]
    )
    send_resid = send(
        resid.at[src], resid.at[src], res_s, res_r, jnp.where(is0, device(me, PARTNER, 0), device(me, PARTNER, 1))
    )
    send_resid.start()

    def sides(a, d):
        return jnp.where(odd, -d, a) * base, jnp.where(odd, a, d) * base

    c0, s0 = sides(a0, d0)
    c1, s1 = sides(a1, d1)
    c2, s2 = sides(a2, d2)
    left_r = jnp.concatenate([c0, c2 * r2, -s1 * dx, -s1 * dy], axis=0)
    left_i = jnp.concatenate([s0, s2 * r2, c1 * dx, c1 * dy], axis=0)
    lr = jnp.concatenate(split2(left_r), axis=0)
    li = jnp.concatenate(split2(left_i), axis=0)
    left = jnp.concatenate([lr, lr, li, li], axis=1)
    y_all = lax.dot_general(left, ep[...], (((1,), (1,)), ((), ())), preferred_element_type=F32)
    y_all = y_all[0 : 4 * ROWS] + y_all[4 * ROWS :]
    sums = [
        jnp.sum(y_all[q * ROWS : (q + 1) * ROWS] * mono, axis=0, keepdims=True) for q in range(4)
    ]
    norm = 1.0 / math.sqrt(16384 * BLOCK_CHANNELS)
    grads = [
        -norm * sums[0],
        (-norm * TWO_PI) * amp_row * sums[2],
        (-norm * TWO_PI) * amp_row * sums[3],
        (norm * 2.0 * TWO_PI * math.pi) * amp_row * w_row * sums[1],
    ]

    onehot_all = (jnp.broadcast_to(both[5:6, :], (32, 512)) == rows_iota((32, 512)).astype(F32)).astype(BF16)
    gl, gm = split3(grads[1]), split3(grads[2])
    wide = lax.dot_general(
        jnp.concatenate(list(gl) + list(gm), axis=0), onehot_all, (((1,), (1,)), ((), ())),
        preferred_element_type=F32,
    )
    cen_l = wide[0:1, :] + wide[1:2, :] + wide[2:3, :]
    cen_m = wide[3:4, :] + wide[4:5, :] + wide[5:6, :]
    cen_rows = jnp.concatenate([cen_l, cen_m, jnp.zeros((1, 64), F32)], axis=1)
    for s in range(2):
        rows = rows_iota((8, 128))
        tile = 0.0
        for h in range(2):
            lo = 256 * s + 128 * h
            for q in range(4):
                tile = jnp.where(rows == 4 * h + q, grads[q][:, lo : lo + 128], tile)
        part[s, 0:8, :] = tile
        part[s, 8:16, :] = jnp.broadcast_to(cen_rows, (8, 128))

    def column(core):
        for i, off in enumerate(COLUMN):
            to = lax.div(lax.rem(z_me + (off[2] + 8), 8), 4)
            send(part.at[to], recv_a.at[2 * i + core], a_s, a_r, device(me, off, 1)).start()

    @pl.when(is0)
    def _():
        column(0)
        send(part.at[src], recv_a.at[14], a_s, a_r, here1).start()

    @pl.when(is1)
    def _():
        column(1)
        drain(recv_a, a_r)
        total = part[src]
        for i in range(15):
            total = total + recv_a[i]
        recv_b[0] = total
        for i, off in enumerate(PLANE):
            for core in (0, 1):
                send(recv_b.at[0], recv_b.at[i + 1], b_s.at[core], b_r, device(me, off, core)).start()
        send(recv_b.at[0], recv_b.at[0], b_s.at[0], b_r, here0).start()

    send_resid.wait_recv()
    for h in range(2):
        res_o[0, :, 256 * h : 256 * h + 256] = resid[h, 0:4, :]
        res_o[1, :, 256 * h : 256 * h + 256] = resid[h, 4:8, :]

    @pl.when(is0)
    def _():
        drain(recv_b, b_r)

    @pl.when(is1)
    def _():
        drain(recv_b.at[pl.ds(1, 15)], b_r)

    total = recv_b[0]
    for i in range(1, 16):
        total = total + recv_b[i]
    comp_o[:, 0:128] = total[0:4, :]
    comp_o[:, 128:256] = total[4:8, :]
    centre_o[0:1, :] = total[8:9, 0:32]
    centre_o[1:2, :] = total[8:9, 32:64]

    send_resid.wait_send()

    @pl.when(is0)
    def _():
        drain(sibling, sib_s)
        drain(recv_a.at[pl.ds(0, 8)], a_s)

    @pl.when(is1)
    def _():
        for core in (0, 1):
            drain(comp.at[0], cmp_s.at[core])
        drain(table, gat_s.at[0])
        drain(table.at[pl.ds(1, 15)], gat_s.at[1])
        drain(recv_a.at[pl.ds(0, 7)], a_s)
        drain(recv_b, b_s.at[0])
        drain(recv_b.at[pl.ds(1, 15)], b_s.at[1])


def deliver(*refs):
    sem = refs[6]
    moves = [pltpu.make_async_copy(refs[i], refs[3 + i], sem.at[i]) for i in range(3)]
    for move in moves:
        move.start()
    for move in moves:
        move.wait()


def on_device(observed, weights, pairs, positions, centres, assign, amplitude, offsets, widths, block_index):
    dma = pltpu.SemaphoreType.DMA
    operands = [
        pltpu.with_memory_space_constraint(v, pltpu.HBM)
        for v in (
            observed, weights, pairs, positions.T, centres, assign.reshape(1, 256), amplitude.reshape(1, 256), offsets,
            widths.reshape(1, 256),
        )
    ]
    sums = pl.pallas_call(
        kernel,
        out_shape=(
            jax.ShapeDtypeStruct((4, 256), F32),
            jax.ShapeDtypeStruct((2, 32), F32),
            jax.ShapeDtypeStruct((2, 4, 512), F32),
        ),
        in_specs=[pl.BlockSpec(memory_space=pltpu.HBM)] * 9 + [pl.BlockSpec(memory_space=pl.ANY)],
        out_specs=tuple([pl.BlockSpec(memory_space=pltpu.VMEM)] * 3),
        scratch_shapes=[
            pltpu.VMEM((2, 4, 256), F32),
            pltpu.VMEM((4, 256), F32),
            pltpu.VMEM((2, 256), jnp.int32),
            pltpu.VMEM((2, 16), F32),
            pltpu.VMEM((2, 32), F32),
            pltpu.VMEM((1, 256), jnp.int32),
            pltpu.VMEM((1, 256), F32),
            pltpu.VMEM((2, 256), F32),
            pltpu.VMEM((1, 256), F32),
            pltpu.SMEM((1,), jnp.int32),
            pltpu.VMEM((1, 128), F32),
            pltpu.VMEM((16, 1, 128), F32),
            pltpu.VMEM((2, 8, 256), F32),
            pltpu.VMEM((512, 128), F32),
            pltpu.VMEM((512, 128), F32),
            pltpu.VMEM((512, 128), F32),
            pltpu.VMEM((512, 1024), BF16),
            pltpu.VMEM((2, 16, 128), F32),
            pltpu.VMEM((15, 16, 128), F32),
            pltpu.VMEM((16, 16, 128), F32),
            pltpu.VMEM((2, 8, 256), F32),
            dma((10,)), dma(()), dma(()), dma((2,)), dma(()), dma((2,)), dma(()), dma(()), dma(()), dma(()), dma(()),
            dma((2,)), dma(()),
        ],
        compiler_params=pltpu.CompilerParams(
            collective_id=0, has_side_effects=True, vmem_limit_bytes=32 * 1024 * 1024
        ),
        name="refit",
    )(*operands, block_index)
    return pl.pallas_call(
        deliver,
        out_shape=tuple(jax.ShapeDtypeStruct(v.shape, F32) for v in sums),
        in_specs=[pl.BlockSpec(memory_space=pltpu.VMEM)] * 3,
        out_specs=tuple([pl.BlockSpec(memory_space=pltpu.HBM)] * 3),
        scratch_shapes=[dma((3,))],
        name="deliver",
    )(*(pltpu.with_memory_space_constraint(v, pltpu.VMEM) for v in sums))


def solution(mesh):
    placed = (
        P(None, "ch", "bl"),
        P("ch", "bl"),
        P(None, "bl"),
        P("bl", None),
        P(),
        P("src"),
        P("src"),
        P(None, "src"),
        P("src"),
        P(),
    )
    return jax.shard_map(
        on_device,
        mesh=mesh,
        in_specs=placed,
        out_specs=(P(None, "src"), P(), P(None, "ch", "bl")),
        check_vma=False,
    )
```

```python
import functools
import math

import jax
import jax.numpy as jnp
from jax import lax
from jax.experimental import pallas as pl
from jax.experimental.pallas import tpu as pltpu
from jax.sharding import PartitionSpec as P

F32 = jnp.float32
BF16 = jnp.bfloat16
LOGICAL = pl.DeviceIdType.LOGICAL
BLOCK_CHANNELS = 16
NU_ZERO = 50000000.0
NU_STEP = 36621.09375
NU_REF = 100000000.0
DK = NU_STEP / NU_REF
CHANS = 4
TWO_PI = 2.0 * math.pi
ENV_COEF = 2.0 * math.pi * math.pi

SIN_COEFS = (4.44288283, -7.30824115, 3.60628896, -0.8457636, 0.10920575)
COS_COEFS = (-1.4142135, 6.97885099, -5.73946117, 1.88356299, -0.31069819)

TERMS = (
    [(a, n - a, 0) for n in range(4) for a in range(n, -1, -1)]
    + [(a, n - a, 1) for n in range(3) for a in range(n, -1, -1)]
    + [(a, n - a, 2) for n in range(2) for a in range(n, -1, -1)]
)
ROWS = 24

STEPS = (2, 1, -1, 0)
Z_STEPS = (-2, 1, -1, 0)


def far_first(offs):
    return sorted((o for o in offs if o != (0, 0, 0)), key=lambda o: (sum(map(abs, o)), o), reverse=True)


GATHER = far_first([(dx, 0, dz) for dx in STEPS for dz in Z_STEPS])
COLUMN = far_first([(0, 0, dz) for dz in (4, 3, 2, 1, 0, -1, -2, -3)])
PLANE = far_first([(dx, dy, 0) for dx in STEPS for dy in STEPS])
PARTNER = (0, 0, 4)
GREET = far_first(
    {((-dx + 1) % 4 - 1, (-dy + 1) % 4 - 1, (-dz + 3) % 8 - 3) for dx, dy, dz in GATHER + COLUMN + PLANE}
)


def here():
    bl = lax.axis_index("bl")
    src = lax.axis_index("src")
    return lax.div(bl, 8), lax.axis_index("ch"), src * 4 + lax.rem(lax.div(bl, 2), 4), lax.rem(bl, 2)


def device(me, off, core):
    x, y, z, _ = me
    dx, dy, dz = off
    x = lax.rem(x + (dx + 4), 4) if dx else x
    y = lax.rem(y + (dy + 4), 4) if dy else y
    z = lax.rem(z + (dz + 8), 8) if dz else z
    return lax.div(z, 4) * 128 + (x * 8 + lax.rem(z, 4) * 2 + core) * 4 + y


def slot_of(off):
    return (off[0] % 4) * 4 + off[2] % 4


def send(src_ref, dst_ref, send_sem, recv_sem, to):
    return pltpu.make_async_remote_copy(
        src_ref=src_ref, dst_ref=dst_ref, send_sem=send_sem, recv_sem=recv_sem, device_id=to, device_id_type=LOGICAL
    )


def drain(ref, sem):
    pltpu.make_async_copy(ref, ref, sem).wait()


def rows_iota(shape):
    return lax.broadcasted_iota(jnp.int32, shape, 0)


def one_of(rows, wanted):
    mask = None
    for w in wanted:
        mask = (rows == w) if mask is None else (mask | (rows == w))
    return mask


def pick(rows, pairs, other=0.0):
    out = other
    for wanted, value in pairs:
        if wanted:
            out = jnp.where(one_of(rows, wanted), value, out)
    return out


def monomials(u, v, w, shape):
    rows = rows_iota(shape)

    def power(base, which, top):
        out = jnp.ones(shape, F32)
        p = base
        for n in range(1, top + 1):
            wanted = [j for j, t in enumerate(TERMS) if t[which] == n]
            out = jnp.where(one_of(rows, wanted), jnp.broadcast_to(p, shape), out)
            p = p * base
        return out

    prod = power(u, 0, 3) * power(v, 1, 3) * power(w, 2, 2)
    return jnp.where(rows < len(TERMS), prod, 0.0)


def channel_factors(k_mid, lanes):
    shape = (ROWS, lanes)
    rows = rows_iota(shape)
    consts = []
    for j, (a, b, e) in enumerate(TERMS):
        n = a + b
        sign = -1.0 if (n // 2) % 2 else 1.0
        consts.append(([j], sign * TWO_PI**n / (math.factorial(a) * math.factorial(b) * math.factorial(e))))
    base = pick(rows, consts) + jnp.zeros(shape, F32)
    out = []
    for f in range(CHANS):
        delta = (f - 0.5 * (CHANS - 1)) * DK
        kappa = (-ENV_COEF * delta) * (2.0 * k_mid + delta)
        phase = pick(
            rows,
            [([j for j, t in enumerate(TERMS) if t[0] + t[1] == n], delta**n) for n in range(1, 4)],
            1.0,
        )
        env = jnp.where(
            one_of(rows, [j for j, t in enumerate(TERMS) if t[2] == 1]),
            kappa,
            jnp.where(one_of(rows, [j for j, t in enumerate(TERMS) if t[2] == 2]), kappa * kappa, 1.0),
        )
        out.append(base * phase * env)
    return out


def split2(x):
    high = x.astype(BF16)
    return high, (x - high.astype(F32)).astype(BF16)


def split3(x):
    high = x.astype(BF16)
    rest = x - high.astype(F32)
    mid = rest.astype(BF16)
    return high, mid, (rest - mid.astype(F32)).astype(BF16)


def kernel(
    obs_h, wts_h, pairs_h, pos_h, cen_h, asg_h, amp_h, off_h, wid_h, blk_h,
    comp_o, centre_o, res_o,
    obs_v, wts_v, pairs_v, pos_v, cen_v, asg_v, amp_v, off_v, wid_v, blk_s,
    sibling, table, comp, lcol, mcol, wcol, ep, part, recv_a, recv_b, resid,
    in_sem, sib_s, sib_r, gat_s, gat_r, cmp_s, cmp_r, res_s, res_r, a_s, a_r, b_s, b_r,
):
    me = here()
    x_me, y_me, z_me, core_me = me
    src = lax.axis_index("src")
    z_low = lax.rem(z_me, 4)
    half = src * 256
    here0, here1 = device(me, (0, 0, 0), 0), device(me, (0, 0, 0), 1)
    is0, is1 = core_me == 0, core_me == 1
    barrier = pltpu.get_barrier_semaphore()
    pl.semaphore_signal(barrier, 1, device_id=jnp.where(is0, here1, here0), device_id_type=LOGICAL)
    for off in GREET:
        pl.semaphore_signal(barrier, 1, device_id=device(me, off, 1), device_id_type=LOGICAL)

    halves = pl.ds(pl.multiple_of(half, 256), 256)
    loads = [
        pltpu.make_async_copy(a, b, in_sem.at[i])
        for i, (a, b) in enumerate(
            [
                (pos_h, pos_v), (cen_h, cen_v), (asg_h, asg_v), (amp_h, amp_v), (off_h, off_v), (wid_h, wid_v),
                (pairs_h.at[:, halves], pairs_v), (obs_h.at[:, :, halves], obs_v), (wts_h.at[:, halves], wts_v), (blk_h, blk_s),
            ]
        )
    ]
    for load in loads:
        load.start()

    loads[0].wait()
    gap = jnp.zeros((1, 16), F32)
    xs, ys = pos_v[0:1, :], pos_v[1:2, :]
    tail = jnp.zeros((1, 64), F32)

    @pl.when(is0)
    def _():
        sibling[...] = jnp.concatenate([xs, gap, ys, gap, tail], axis=1)
        pl.semaphore_wait(barrier, 1)
        send(sibling, table.at[0], sib_s, sib_r, here1).start()

    @pl.when(is1)
    def _():
        sibling[...] = jnp.concatenate([gap, xs, gap, ys, tail], axis=1)

    for load in loads[1:6]:
        load.wait()
    assign = asg_v[...]
    onehot = (jnp.broadcast_to(assign, (32, 256)) == rows_iota((32, 256))).astype(BF16)
    cen_parts = split3(cen_v[...])
    centre = sum(jnp.dot(p, onehot, preferred_element_type=F32) for p in cen_parts)
    lm = centre + off_v[...]
    width = wid_v[...]
    rows8 = rows_iota((8, 256))
    comp[src] = pick(
        rows8,
        [
            ([0], lm[0:1, :]), ([1], lm[1:2, :]), ([2], width * width), ([3], amp_v[...]), ([4], width),
            ([5], assign.astype(F32)),
        ],
    )

    @pl.when(is1)
    def _():
        drain(table.at[0], sib_r)
        table[0] = table[0] + sibling[...]
        pl.semaphore_wait(barrier, 2 * len(GREET) + 1)
        for core in (0, 1):
            send(comp.at[src], comp.at[src], cmp_s.at[core], cmp_r, device(me, PARTNER, core)).start()
        for off in GATHER:
            for core in (0, 1):
                send(table.at[0], table.at[slot_of(off)], gat_s.at[core], gat_r, device(me, off, core)).start()
        send(table.at[0], table.at[0], gat_s.at[0], gat_r, here0).start()

    loads[6].wait()
    loads[9].wait()
    first = blk_s[0] * BLOCK_CHANNELS + lax.axis_index("ch") * CHANS
    k_mid = (NU_ZERO + (first.astype(F32) + 0.5 * (CHANS - 1)) * NU_STEP) / NU_REF
    ks = [(NU_ZERO + (first + f).astype(F32) * NU_STEP) / NU_REF for f in range(CHANS)]
    gs = channel_factors(k_mid, 256)
    ant = pairs_v[...]
    chip = lax.shift_right_logical(ant, 5)
    slot = ((x_me - lax.shift_right_logical(chip, 2)) & 3) * 4 + ((z_low - chip) & 3)
    inner = ant & 31
    rows16 = rows_iota((16, 128))

    drain(comp.at[0], cmp_r)
    both = jnp.concatenate([comp[0], comp[1]], axis=1)
    l_row, m_row, w2_row = both[0:1, :], both[1:2, :], both[2:3, :]
    amp_row, w_row = both[3:4, :], both[4:5, :]
    mono = monomials(l_row, m_row, w2_row, (ROWS, 512))
    amp_high, amp_low = split2(mono * amp_row)
    mono_amp = jnp.concatenate([amp_high, amp_low], axis=0)
    cols = jnp.transpose(both)
    lcol[...] = jnp.broadcast_to(cols[:, 0:1], (512, 128))
    mcol[...] = jnp.broadcast_to(cols[:, 1:2], (512, 128))
    wcol[...] = jnp.broadcast_to(cols[:, 2:3], (512, 128))

    @pl.when(is0)
    def _():
        drain(table, gat_r)

    @pl.when(is1)
    def _():
        drain(table.at[pl.ds(1, 15)], gat_r)

    sites = table[:, 0, :]
    delta_x, delta_y = [], []
    for t in range(2):
        lanes = slice(128 * t, 128 * t + 128)
        got = []
        for shift in (0, 32):
            total = 0.0
            for a in range(2):
                idx = jnp.broadcast_to(inner[a : a + 1, lanes] + shift, (16, 128))
                val = jnp.take_along_axis(sites, idx, axis=1, mode="promise_in_bounds")
                val = jnp.where(jnp.broadcast_to(slot[a : a + 1, lanes], (16, 128)) == rows16, val, 0.0)
                total = total + val if a == 0 else total - val
            got.append(jnp.sum(total, axis=0, keepdims=True))
        delta_x.append(got[0])
        delta_y.append(got[1])
    dx = jnp.concatenate(delta_x, axis=1)
    dy = jnp.concatenate(delta_y, axis=1)
    r2 = dx * dx + dy * dy

    kx = [k_mid * d for d in delta_x]
    ky = [k_mid * d for d in delta_y]
    er = [
        (-ENV_COEF * math.log2(math.e)) * (k_mid * k_mid) * (delta_x[t] * delta_x[t] + delta_y[t] * delta_y[t])
        for t in range(2)
    ]

    for i in range(32):
        rows = slice(16 * i, 16 * i + 16)
        lc, mc, wc = lcol[rows, :], mcol[rows, :], wcol[rows, :]
        for t in range(2):
            turns = lc * kx[t] + mc * ky[t]
            env = jnp.exp2(wc * er[t])
            r = turns - jnp.round(turns)
            y = r * r
            s = SIN_COEFS[-1]
            for coef in SIN_COEFS[-2::-1]:
                s = s * y + coef
            s = s * r
            c = COS_COEFS[-1]
            for coef in COS_COEFS[-2::-1]:
                c = c * y + coef
            ep_r = env * (1.0 - s * s)
            ep_i = env * (s * c)
            lo = 128 * t
            high, low = split2(ep_r)
            ep[rows, lo : lo + 128] = high
            ep[rows, 256 + lo : 384 + lo] = low
            high, low = split2(ep_i)
            ep[rows, 512 + lo : 640 + lo] = high
            ep[rows, 768 + lo : 896 + lo] = low

    m_all = jnp.dot(mono_amp, ep[...], preferred_element_type=F32)
    m_all = m_all[0:ROWS] + m_all[ROWS:]
    m_r = m_all[:, 0:256] + m_all[:, 256:512]
    m_i = m_all[:, 512:768] + m_all[:, 768:1024]
    rows24 = rows_iota((ROWS, 256))
    odd = one_of(rows24, [j for j, t in enumerate(TERMS) if (t[0] + t[1]) % 2])
    base = monomials(dx, dy, r2, (ROWS, 256))
    n_r = base * jnp.where(odd, m_i, m_r)
    n_i = base * jnp.where(odd, -m_r, m_i)
    loads[7].wait()
    loads[8].wait()
    zero = jnp.zeros((ROWS, 256), F32)
    a0, d0, a1, d1, a2, d2 = zero, zero, zero, zero, zero, zero
    resids = []
    for f in range(CHANS):
        v_r = jnp.sum(gs[f] * n_r, axis=0, keepdims=True)
        v_i = jnp.sum(gs[f] * n_i, axis=0, keepdims=True)
        rr = obs_v[0, f : f + 1, :] - v_r
        ri = obs_v[1, f : f + 1, :] - v_i
        resids.append((rr, ri))
        wr = wts_v[f : f + 1, :] * rr
        wi = wts_v[f : f + 1, :] * ri
        k = ks[f]
        a0 += gs[f] * wr
        d0 += gs[f] * wi
        a1 += gs[f] * (k * wr)
        d1 += gs[f] * (k * wi)
        a2 += gs[f] * (k * k * wr)
        d2 += gs[f] * (k * k * wi)
    resid[src] = pick(
        rows8, [([f], resids[f][0]) for f in range(CHANS)] + [([4 + f], resids[f][1]) for f in range(CHANS)]
    )
    send_resid = send(
        resid.at[src], resid.at[src], res_s, res_r, jnp.where(is0, device(me, PARTNER, 0), device(me, PARTNER, 1))
    )
    send_resid.start()

    def sides(a, d):
        return jnp.where(odd, -d, a) * base, jnp.where(odd, a, d) * base

    c0, s0 = sides(a0, d0)
    c1, s1 = sides(a1, d1)
    c2, s2 = sides(a2, d2)
    left_r = jnp.concatenate([c0, c2 * r2, -s1 * dx, -s1 * dy], axis=0)
    left_i = jnp.concatenate([s0, s2 * r2, c1 * dx, c1 * dy], axis=0)
    lr = jnp.concatenate(split2(left_r), axis=0)
    li = jnp.concatenate(split2(left_i), axis=0)
    left = jnp.concatenate([lr, lr, li, li], axis=1)
    y_all = lax.dot_general(left, ep[...], (((1,), (1,)), ((), ())), preferred_element_type=F32)
    y_all = y_all[0 : 4 * ROWS] + y_all[4 * ROWS :]
    sums = [
        jnp.sum(y_all[q * ROWS : (q + 1) * ROWS] * mono, axis=0, keepdims=True) for q in range(4)
    ]
    norm = 1.0 / math.sqrt(16384 * BLOCK_CHANNELS)
    grads = [
        -norm * sums[0],
        (-norm * TWO_PI) * amp_row * sums[2],
        (-norm * TWO_PI) * amp_row * sums[3],
        (norm * 2.0 * TWO_PI * math.pi) * amp_row * w_row * sums[1],
    ]

    onehot_all = (jnp.broadcast_to(both[5:6, :], (32, 512)) == rows_iota((32, 512)).astype(F32)).astype(BF16)
    gl, gm = split3(grads[1]), split3(grads[2])
    wide = lax.dot_general(
        jnp.concatenate(list(gl) + list(gm), axis=0), onehot_all, (((1,), (1,)), ((), ())),
        preferred_element_type=F32,
    )
    cen_l = wide[0:1, :] + wide[1:2, :] + wide[2:3, :]
    cen_m = wide[3:4, :] + wide[4:5, :] + wide[5:6, :]
    cen_rows = jnp.concatenate([cen_l, cen_m, jnp.zeros((1, 64), F32)], axis=1)
    for s in range(2):
        rows = rows_iota((8, 128))
        tile = 0.0
        for h in range(2):
            lo = 256 * s + 128 * h
            for q in range(4):
                tile = jnp.where(rows == 4 * h + q, grads[q][:, lo : lo + 128], tile)
        part[s, 0:8, :] = tile
        part[s, 8:9, :] = cen_rows

    def column(core):
        for i, off in enumerate(COLUMN):
            to = lax.div(lax.rem(z_me + (off[2] + 8), 8), 4)
            send(part.at[to], recv_a.at[2 * i + core], a_s, a_r, device(me, off, 1)).start()

    @pl.when(is0)
    def _():
        column(0)
        send(part.at[src], recv_a.at[14], a_s, a_r, here1).start()

    @pl.when(is1)
    def _():
        column(1)
        drain(recv_a, a_r)
        total = part[src]
        for i in range(15):
            total = total + recv_a[i]
        recv_b[0] = total
        for i, off in enumerate(PLANE):
            for core in (0, 1):
                send(recv_b.at[0], recv_b.at[i + 1], b_s.at[core], b_r, device(me, off, core)).start()
        send(recv_b.at[0], recv_b.at[0], b_s.at[0], b_r, here0).start()

    send_resid.wait_recv()
    for h in range(2):
        res_o[0, :, 256 * h : 256 * h + 256] = resid[h, 0:4, :]
        res_o[1, :, 256 * h : 256 * h + 256] = resid[h, 4:8, :]

    @pl.when(is0)
    def _():
        drain(recv_b, b_r)

    @pl.when(is1)
    def _():
        drain(recv_b.at[pl.ds(1, 15)], b_r)

    total = recv_b[0]
    for i in range(1, 16):
        total = total + recv_b[i]
    comp_o[:, 0:128] = total[0:4, :]
    comp_o[:, 128:256] = total[4:8, :]
    centre_o[0:1, :] = total[8:9, 0:32]
    centre_o[1:2, :] = total[8:9, 32:64]

    send_resid.wait_send()

    @pl.when(is0)
    def _():
        drain(sibling, sib_s)
        drain(recv_a.at[pl.ds(0, 8)], a_s)

    @pl.when(is1)
    def _():
        for core in (0, 1):
            drain(comp.at[0], cmp_s.at[core])
        drain(table, gat_s.at[0])
        drain(table.at[pl.ds(1, 15)], gat_s.at[1])
        drain(recv_a.at[pl.ds(0, 7)], a_s)
        drain(recv_b, b_s.at[0])
        drain(recv_b.at[pl.ds(1, 15)], b_s.at[1])


def deliver(*refs):
    sem = refs[6]
    moves = [pltpu.make_async_copy(refs[i], refs[3 + i], sem.at[i]) for i in range(3)]
    for move in moves:
        move.start()
    for move in moves:
        move.wait()


def on_device(observed, weights, pairs, positions, centres, assign, amplitude, offsets, widths, block_index):
    dma = pltpu.SemaphoreType.DMA
    operands = [
        pltpu.with_memory_space_constraint(v, pltpu.HBM)
        for v in (
            observed, weights, pairs, positions.T, centres, assign.reshape(1, 256), amplitude.reshape(1, 256), offsets,
            widths.reshape(1, 256),
        )
    ]
    sums = pl.pallas_call(
        kernel,
        out_shape=(
            jax.ShapeDtypeStruct((4, 256), F32),
            jax.ShapeDtypeStruct((2, 32), F32),
            jax.ShapeDtypeStruct((2, 4, 512), F32),
        ),
        in_specs=[pl.BlockSpec(memory_space=pltpu.HBM)] * 9 + [pl.BlockSpec(memory_space=pl.ANY)],
        out_specs=tuple([pl.BlockSpec(memory_space=pltpu.VMEM)] * 3),
        scratch_shapes=[
            pltpu.VMEM((2, 4, 256), F32),
            pltpu.VMEM((4, 256), F32),
            pltpu.VMEM((2, 256), jnp.int32),
            pltpu.VMEM((2, 16), F32),
            pltpu.VMEM((2, 32), F32),
            pltpu.VMEM((1, 256), jnp.int32),
            pltpu.VMEM((1, 256), F32),
            pltpu.VMEM((2, 256), F32),
            pltpu.VMEM((1, 256), F32),
            pltpu.SMEM((1,), jnp.int32),
            pltpu.VMEM((1, 128), F32),
            pltpu.VMEM((16, 1, 128), F32),
            pltpu.VMEM((2, 8, 256), F32),
            pltpu.VMEM((512, 128), F32),
            pltpu.VMEM((512, 128), F32),
            pltpu.VMEM((512, 128), F32),
            pltpu.VMEM((512, 1024), BF16),
            pltpu.VMEM((2, 9, 128), F32),
            pltpu.VMEM((15, 9, 128), F32),
            pltpu.VMEM((16, 9, 128), F32),
            pltpu.VMEM((2, 8, 256), F32),
            dma((10,)), dma(()), dma(()), dma((2,)), dma(()), dma((2,)), dma(()), dma(()), dma(()), dma(()), dma(()),
            dma((2,)), dma(()),
        ],
        compiler_params=pltpu.CompilerParams(
            collective_id=0, has_side_effects=True, vmem_limit_bytes=32 * 1024 * 1024
        ),
        name="refit",
    )(*operands, block_index)
    return pl.pallas_call(
        deliver,
        out_shape=tuple(jax.ShapeDtypeStruct(v.shape, F32) for v in sums),
        in_specs=[pl.BlockSpec(memory_space=pltpu.VMEM)] * 3,
        out_specs=tuple([pl.BlockSpec(memory_space=pltpu.HBM)] * 3),
        scratch_shapes=[dma((3,))],
        name="deliver",
    )(*(pltpu.with_memory_space_constraint(v, pltpu.VMEM) for v in sums))


def solution(mesh):
    placed = (
        P(None, "ch", "bl"),
        P("ch", "bl"),
        P(None, "bl"),
        P("bl", None),
        P(),
        P("src"),
        P("src"),
        P(None, "src"),
        P("src"),
        P(),
    )
    return jax.shard_map(
        on_device,
        mesh=mesh,
        in_specs=placed,
        out_specs=(P(None, "src"), P(), P(None, "ch", "bl")),
        check_vma=False,
    )
```

```python
import functools
import math

import jax
import jax.numpy as jnp
from jax import lax
from jax.experimental import pallas as pl
from jax.experimental.pallas import tpu as pltpu
from jax.sharding import PartitionSpec as P

F32 = jnp.float32
BF16 = jnp.bfloat16
LOGICAL = pl.DeviceIdType.LOGICAL
BLOCK_CHANNELS = 16
NU_ZERO = 50000000.0
NU_STEP = 36621.09375
NU_REF = 100000000.0
DK = NU_STEP / NU_REF
CHANS = 4
TWO_PI = 2.0 * math.pi
ENV_COEF = 2.0 * math.pi * math.pi

SIN_COEFS = (4.44288283, -7.30824115, 3.60628896, -0.8457636, 0.10920575)
COS_COEFS = (-1.4142135, 6.97885099, -5.73946117, 1.88356299, -0.31069819)

ROUNDER = 12582912.0
NT = (((1,), (1,)), ((), ()))

TERMS = (
    [(a, n - a, 0) for n in range(4) for a in range(n, -1, -1)]
    + [(a, n - a, 1) for n in range(3) for a in range(n, -1, -1)]
    + [(a, n - a, 2) for n in range(2) for a in range(n, -1, -1)]
)
ROWS = 24
ODD = [j for j, t in enumerate(TERMS) if (t[0] + t[1]) % 2]

STEPS = (2, 1, -1, 0)
Z_STEPS = (-2, 1, -1, 0)


def far_first(offs):
    return sorted((o for o in offs if o != (0, 0, 0)), key=lambda o: (sum(map(abs, o)), o), reverse=True)


GATHER = far_first([(dx, 0, dz) for dx in STEPS for dz in Z_STEPS])
COLUMN = far_first([(0, 0, dz) for dz in (4, 3, 2, 1, 0, -1, -2, -3)])
PLANE = far_first([(dx, dy, 0) for dx in STEPS for dy in STEPS])
PARTNER = (0, 0, 4)
GREET = far_first(
    {((-dx + 1) % 4 - 1, (-dy + 1) % 4 - 1, (-dz + 3) % 8 - 3) for dx, dy, dz in GATHER + COLUMN + PLANE}
)


def here():
    bl = lax.axis_index("bl")
    src = lax.axis_index("src")
    return lax.div(bl, 8), lax.axis_index("ch"), src * 4 + lax.rem(lax.div(bl, 2), 4), lax.rem(bl, 2)


def device(me, off, core):
    x, y, z, _ = me
    dx, dy, dz = off
    x = lax.rem(x + (dx + 4), 4) if dx else x
    y = lax.rem(y + (dy + 4), 4) if dy else y
    z = lax.rem(z + (dz + 8), 8) if dz else z
    return lax.div(z, 4) * 128 + (x * 8 + lax.rem(z, 4) * 2 + core) * 4 + y


def slot_of(off):
    return (off[0] % 4) * 4 + off[2] % 4


def send(src_ref, dst_ref, send_sem, recv_sem, to):
    return pltpu.make_async_remote_copy(
        src_ref=src_ref, dst_ref=dst_ref, send_sem=send_sem, recv_sem=recv_sem, device_id=to, device_id_type=LOGICAL
    )


def drain(ref, sem):
    pltpu.make_async_copy(ref, ref, sem).wait()


def rows_iota(shape):
    return lax.broadcasted_iota(jnp.int32, shape, 0)


def one_of(rows, wanted):
    mask = None
    for w in wanted:
        mask = (rows == w) if mask is None else (mask | (rows == w))
    return mask


def pick(rows, pairs, other=0.0):
    out = other
    for wanted, value in pairs:
        if wanted:
            out = jnp.where(one_of(rows, wanted), value, out)
    return out


def selectors(shape):
    rows = rows_iota(shape)
    out = []
    for which, top in ((0, 3), (1, 3), (2, 2)):
        for n in range(top + 1):
            wanted = [j for j, t in enumerate(TERMS) if t[which] == n]
            out.append(jnp.where(one_of(rows, wanted), 1.0, 0.0) + jnp.zeros(shape, F32))
    return out


def monomials(u, v, w, sel):
    u2, v2 = u * u, v * v
    p = sel[0] + sel[1] * u + sel[2] * u2 + sel[3] * (u2 * u)
    q = sel[4] + sel[5] * v + sel[6] * v2 + sel[7] * (v2 * v)
    return p * q * (sel[8] + sel[9] * w + sel[10] * (w * w))


def channel_factors(k_mid, lanes):
    shape = (ROWS, lanes)
    rows = rows_iota(shape)
    consts = []
    for j, (a, b, e) in enumerate(TERMS):
        n = a + b
        sign = -1.0 if (n // 2) % 2 else 1.0
        consts.append(([j], sign * TWO_PI**n / (math.factorial(a) * math.factorial(b) * math.factorial(e))))
    base = pick(rows, consts) + jnp.zeros(shape, F32)
    out = []
    for f in range(CHANS):
        delta = (f - 0.5 * (CHANS - 1)) * DK
        kappa = (-ENV_COEF * delta) * (2.0 * k_mid + delta)
        phase = pick(
            rows,
            [([j for j, t in enumerate(TERMS) if t[0] + t[1] == n], delta**n) for n in range(1, 4)],
            1.0,
        )
        env = jnp.where(
            one_of(rows, [j for j, t in enumerate(TERMS) if t[2] == 1]),
            kappa,
            jnp.where(one_of(rows, [j for j, t in enumerate(TERMS) if t[2] == 2]), kappa * kappa, 1.0),
        )
        out.append(base * phase * env)
    return out


def split2(x):
    wide = x * 65537.0
    high = wide - (wide - x)
    return high.astype(BF16), (x - high).astype(BF16)


def split3(x):
    high = x.astype(BF16)
    rest = x - high.astype(F32)
    mid = rest.astype(BF16)
    return high, mid, (rest - mid.astype(F32)).astype(BF16)


def kernel(
    obs_h, wts_h, pairs_h, pos_h, cen_h, asg_h, amp_h, off_h, wid_h, blk_h,
    comp_o, centre_o, res_o,
    obs_v, wts_v, pairs_v, pos_v, cen_v, asg_v, amp_v, off_v, wid_v, blk_s,
    sibling, table, comp, lcol, mcol, wcol, ep_a, ep_b, ep_c, ep_d, part, recv_a, recv_b, resid, gs_v, sel_v, hot_v,
    in_sem, sib_s, sib_r, gat_s, gat_r, cmp_s, cmp_r, res_s, res_r, a_s, a_r, b_s, b_r,
):
    me = here()
    x_me, y_me, z_me, core_me = me
    src = lax.axis_index("src")
    z_low = lax.rem(z_me, 4)
    at_end = (z_low == 0) | (z_low == 3)
    half = src * 256
    here0, here1 = device(me, (0, 0, 0), 0), device(me, (0, 0, 0), 1)
    is0, is1 = core_me == 0, core_me == 1
    barrier = pltpu.get_barrier_semaphore()
    pl.semaphore_signal(barrier, 1, device_id=jnp.where(is0, here1, here0), device_id_type=LOGICAL)
    for off in GREET:
        pl.semaphore_signal(barrier, 1, device_id=device(me, off, 1), device_id_type=LOGICAL)

    halves = pl.ds(pl.multiple_of(half, 256), 256)
    loads = [
        pltpu.make_async_copy(a, b, in_sem.at[i])
        for i, (a, b) in enumerate(
            [
                (pos_h, pos_v), (cen_h, cen_v), (asg_h, asg_v), (amp_h, amp_v), (off_h, off_v), (wid_h, wid_v),
                (pairs_h.at[:, halves], pairs_v), (obs_h.at[:, :, halves], obs_v), (wts_h.at[:, halves], wts_v), (blk_h, blk_s),
            ]
        )
    ]
    for load in loads:
        load.start()

    loads[0].wait()
    gap = jnp.zeros((1, 16), F32)
    xs, ys = pos_v[0:1, :], pos_v[1:2, :]
    tail = jnp.zeros((1, 64), F32)

    @pl.when(is0)
    def _():
        sibling[...] = jnp.concatenate([xs, gap, ys, gap, tail], axis=1)
        pl.semaphore_wait(barrier, 1)
        send(sibling, table.at[0], sib_s, sib_r, here1).start()

    @pl.when(is1)
    def _():
        sibling[...] = jnp.concatenate([gap, xs, gap, ys, tail], axis=1)

    for load in loads[1:6]:
        load.wait()
    assign = asg_v[...]
    onehot = (jnp.broadcast_to(assign, (32, 256)) == rows_iota((32, 256))).astype(BF16)
    cen_parts = split3(cen_v[...])
    centre = sum(jnp.dot(p, onehot, preferred_element_type=F32) for p in cen_parts)
    lm = centre + off_v[...]
    width = wid_v[...]
    rows8 = rows_iota((8, 256))
    comp[src] = pick(
        rows8,
        [
            ([0], lm[0:1, :]), ([1], lm[1:2, :]), ([2], width * width), ([3], amp_v[...]), ([4], width),
            ([5], assign.astype(F32)),
        ],
    )

    @pl.when(is1)
    def _():
        drain(table.at[0], sib_r)
        table[0] = table[0] + sibling[...]
        pl.semaphore_wait(barrier, 2 * len(GREET) + 1)

        def positions(chips):
            for off in chips:
                for core in (0, 1):
                    send(table.at[0], table.at[slot_of(off)], gat_s.at[core], gat_r, device(me, off, core)).start()

        positions(GATHER[:5])

        @pl.when(at_end)
        def _():
            for step in (1, 2):
                far = lax.rem(z_me + jnp.where(z_low == 0, 8 - step, step), 8)
                for core in (0, 1):
                    to = lax.div(far, 4) * 128 + (x_me * 8 + lax.rem(far, 4) * 2 + core) * 4 + y_me
                    send(comp.at[src], comp.at[src], cmp_s.at[core], cmp_r, to).start()

        positions(GATHER[5:])
        send(table.at[0], table.at[0], gat_s.at[0], gat_r, here0).start()

    loads[6].wait()
    loads[9].wait()
    first = blk_s[0] * BLOCK_CHANNELS + lax.axis_index("ch") * CHANS
    k_mid = (NU_ZERO + (first.astype(F32) + 0.5 * (CHANS - 1)) * NU_STEP) / NU_REF
    ks = [(NU_ZERO + (first + f).astype(F32) * NU_STEP) / NU_REF for f in range(CHANS)]
    for f, factor in enumerate(channel_factors(k_mid, 128)):
        gs_v[f] = factor
    choose = selectors((ROWS, 128))
    for n, one in enumerate(choose):
        sel_v[n] = one
    sel_v[11] = jnp.where(one_of(rows_iota((ROWS, 128)), ODD), 1.0, 0.0)
    ant = pairs_v[...]
    chip = lax.shift_right_logical(ant, 5)
    slot = ((x_me - lax.shift_right_logical(chip, 2)) & 3) * 4 + ((z_low - chip) & 3)
    inner = ant & 31
    rows16 = rows_iota((16, 128))

    drain(comp.at[0], cmp_r)
    both = jnp.concatenate([comp[0], comp[1]], axis=1)
    l_row, m_row, w2_row = both[0:1, :], both[1:2, :], both[2:3, :]
    amp_row, w_row = both[3:4, :], both[4:5, :]
    mono = monomials(l_row, m_row, w2_row, [jnp.concatenate([one] * 4, axis=1) for one in choose])
    amp_high, amp_low = split2(mono * amp_row)
    mono_amp = jnp.concatenate([amp_high, amp_low], axis=0)
    source = jnp.broadcast_to(both[5:6, :], (128, 512))
    rows128 = rows_iota((128, 512)).astype(F32)
    hot_v[:, 0:512] = (source == rows128).astype(BF16)
    hot_v[:, 512:1024] = (source + 32.0 == rows128).astype(BF16)
    cols = jnp.transpose(both)
    lcol[...] = jnp.broadcast_to(cols[:, 0:1], (512, 128))
    mcol[...] = jnp.broadcast_to(cols[:, 1:2], (512, 128))
    wcol[...] = jnp.broadcast_to(cols[:, 2:3], (512, 128))

    @pl.when(is0)
    def _():
        drain(table, gat_r)

    @pl.when(is1)
    def _():
        drain(table.at[pl.ds(1, 15)], gat_r)

    sites = table[:, 0, :]
    delta_x, delta_y = [], []
    for t in range(2):
        lanes = slice(128 * t, 128 * t + 128)
        got = []
        for shift in (0, 32):
            total = 0.0
            for a in range(2):
                idx = jnp.broadcast_to(inner[a : a + 1, lanes] + shift, (16, 128))
                val = jnp.take_along_axis(sites, idx, axis=1, mode="promise_in_bounds")
                val = jnp.where(jnp.broadcast_to(slot[a : a + 1, lanes], (16, 128)) == rows16, val, 0.0)
                total = total + val if a == 0 else total - val
            got.append(jnp.sum(total, axis=0, keepdims=True))
        delta_x.append(got[0])
        delta_y.append(got[1])
    dist = [delta_x[t] * delta_x[t] + delta_y[t] * delta_y[t] for t in range(2)]
    sel = [sel_v[n] for n in range(11)]
    bases = [monomials(delta_x[t], delta_y[t], dist[t], sel) for t in range(2)]

    kx = [k_mid * d for d in delta_x]
    ky = [k_mid * d for d in delta_y]
    er = [
        (-ENV_COEF) * (k_mid * k_mid) * dist[t]
        for t in range(2)
    ]

    loads[7].wait()
    loads[8].wait()
    odd = sel_v[11] > 0.5
    gs = [gs_v[f] for f in range(CHANS)]

    eps = (ep_a, ep_b, ep_c, ep_d)

    def terms(t, first, last):
        for i in range(first, last):
            rows = slice(16 * i, 16 * i + 16)
            lc, mc, wc = lcol[rows, :], mcol[rows, :], wcol[rows, :]
            turns = lc * kx[t] + mc * ky[t]
            env = jnp.exp(wc * er[t])
            r = turns - ((turns + ROUNDER) - ROUNDER)
            y = r * r
            s = SIN_COEFS[-1]
            for coef in SIN_COEFS[-2::-1]:
                s = s * y + coef
            s = s * r
            c = COS_COEFS[-1]
            for coef in COS_COEFS[-2::-1]:
                c = c * y + coef
            here_ep = eps[2 * t + i // 16]
            inner_rows = slice(16 * (i % 16), 16 * (i % 16) + 16)
            high, low = split2(env * (1.0 - s * s))
            here_ep[inner_rows, 0:128] = high
            here_ep[inner_rows, 256:384] = low
            high, low = split2(env * (s * c))
            here_ep[inner_rows, 128:256] = high
            here_ep[inner_rows, 384:512] = low

    def moments(t, h):
        part_c = slice(256 * h, 256 * h + 256)
        here_ep = eps[2 * t + h]
        high = jnp.dot(mono_amp[:, part_c], here_ep[:, 0:256], preferred_element_type=F32)
        low = jnp.dot(mono_amp[0:ROWS, part_c], here_ep[:, 256:512], preferred_element_type=F32)
        return high[0:ROWS] + high[ROWS:] + low

    def misfit(t, m_all):
        m_r, m_i = m_all[:, 0:128], m_all[:, 128:256]
        lanes = slice(128 * t, 128 * t + 128)
        dx, dy, r2, base = delta_x[t], delta_y[t], dist[t], bases[t]
        n_r = base * jnp.where(odd, m_i, m_r)
        n_i = base * jnp.where(odd, -m_r, m_i)
        zero = jnp.zeros((ROWS, 128), F32)
        a0, d0, a1, d1, a2, d2 = zero, zero, zero, zero, zero, zero
        tile = jnp.zeros((8, 128), F32)
        rows8 = rows_iota((8, 128))
        for f in range(CHANS):
            v_r = jnp.sum(gs[f] * n_r, axis=0, keepdims=True)
            v_i = jnp.sum(gs[f] * n_i, axis=0, keepdims=True)
            rr = obs_v[0, f : f + 1, lanes] - v_r
            ri = obs_v[1, f : f + 1, lanes] - v_i
            tile = jnp.where(rows8 == f, rr, jnp.where(rows8 == CHANS + f, ri, tile))
            wr = wts_v[f : f + 1, lanes] * rr
            wi = wts_v[f : f + 1, lanes] * ri
            k = ks[f]
            a0 += gs[f] * wr
            d0 += gs[f] * wi
            a1 += gs[f] * (k * wr)
            d1 += gs[f] * (k * wi)
            a2 += gs[f] * (k * k * wr)
            d2 += gs[f] * (k * k * wi)
        resid[src, :, lanes] = tile

        def sides(a, d):
            return jnp.where(odd, -d, a) * base, jnp.where(odd, a, d) * base

        c0, s0 = sides(a0, d0)
        c1, s1 = sides(a1, d1)
        c2, s2 = sides(a2, d2)
        left_r = jnp.concatenate([c0, c2 * r2, -s1 * dx, -s1 * dy], axis=0)
        left_i = jnp.concatenate([s0, s2 * r2, c1 * dx, c1 * dy], axis=0)
        high, low = split2(jnp.concatenate([left_r, left_i], axis=1))
        return high, jnp.concatenate([high, low], axis=0)

    def adjoint(t, left_high, left_both):
        out = []
        for h in range(2):
            here_ep = eps[2 * t + h]
            high = lax.dot_general(left_both, here_ep[:, 0:256], NT, preferred_element_type=F32)
            low = lax.dot_general(left_high, here_ep[:, 256:512], NT, preferred_element_type=F32)
            out.append(high[0 : 4 * ROWS] + high[4 * ROWS :] + low)
        return jnp.concatenate(out, axis=1)

    terms(0, 0, 32)
    m0 = moments(0, 0) + moments(0, 1)
    terms(1, 0, 32)
    m1 = moments(1, 0) + moments(1, 1)
    left0 = misfit(0, m0)
    y_all = adjoint(0, *left0)
    left1 = misfit(1, m1)
    send_resid = send(
        resid.at[src], resid.at[src], res_s, res_r, jnp.where(is0, device(me, PARTNER, 0), device(me, PARTNER, 1))
    )
    send_resid.start()
    y_all += adjoint(1, *left1)
    sums = [jnp.sum(y_all[q * ROWS : (q + 1) * ROWS] * mono, axis=0, keepdims=True) for q in range(4)]
    norm = 1.0 / math.sqrt(16384 * BLOCK_CHANNELS)
    grads = [
        -norm * sums[0],
        (-norm * TWO_PI) * amp_row * sums[2],
        (-norm * TWO_PI) * amp_row * sums[3],
        (norm * 2.0 * TWO_PI * math.pi) * amp_row * w_row * sums[1],
    ]

    scaled = (-norm * TWO_PI) * (mono * amp_row)
    to_l, to_m = split2(y_all[2 * ROWS : 3 * ROWS] * scaled), split2(y_all[3 * ROWS : 4 * ROWS] * scaled)
    left = jnp.concatenate([jnp.concatenate([to_l[n], to_m[n]], axis=1) for n in range(2)], axis=0)
    wide = lax.dot_general(left, hot_v[...], NT, preferred_element_type=F32)
    cen_rows = jnp.sum(wide, axis=0, keepdims=True)
    for s in range(2):
        rows = rows_iota((8, 128))
        tile = 0.0
        for h in range(2):
            lo = 256 * s + 128 * h
            for q in range(4):
                tile = jnp.where(rows == 4 * h + q, grads[q][:, lo : lo + 128], tile)
        part[s, 0:8, :] = tile
        part[s, 8:9, :] = cen_rows

    def column(core):
        for i, off in enumerate(COLUMN):
            to = lax.div(lax.rem(z_me + (off[2] + 8), 8), 4)
            send(part.at[to], recv_a.at[2 * i + core], a_s, a_r, device(me, off, 1)).start()

    @pl.when(is0)
    def _():
        column(0)
        send(part.at[src], recv_a.at[14], a_s, a_r, here1).start()

    @pl.when(is1)
    def _():
        column(1)
        drain(recv_a, a_r)
        total = part[src]
        for i in range(15):
            total = total + recv_a[i]
        recv_b[0] = total
        for i, off in enumerate(PLANE):
            for core in (0, 1):
                send(recv_b.at[0], recv_b.at[i + 1], b_s.at[core], b_r, device(me, off, core)).start()
        send(recv_b.at[0], recv_b.at[0], b_s.at[0], b_r, here0).start()

    send_resid.wait_recv()
    for h in range(2):
        res_o[0, :, 256 * h : 256 * h + 256] = resid[h, 0:4, :]
        res_o[1, :, 256 * h : 256 * h + 256] = resid[h, 4:8, :]

    @pl.when(is0)
    def _():
        drain(recv_b, b_r)

    @pl.when(is1)
    def _():
        drain(recv_b.at[pl.ds(1, 15)], b_r)

    total = recv_b[0]
    for i in range(1, 16):
        total = total + recv_b[i]
    comp_o[:, 0:128] = total[0:4, :]
    comp_o[:, 128:256] = total[4:8, :]
    centre_o[0:1, :] = total[8:9, 0:32]
    centre_o[1:2, :] = total[8:9, 32:64]

    send_resid.wait_send()

    @pl.when(is0)
    def _():
        drain(sibling, sib_s)
        drain(recv_a.at[pl.ds(0, 8)], a_s)

    @pl.when(is1)
    def _():
        @pl.when(at_end)
        def _():
            for core in (0, 1):
                drain(comp, cmp_s.at[core])

        drain(table, gat_s.at[0])
        drain(table.at[pl.ds(1, 15)], gat_s.at[1])
        drain(recv_a.at[pl.ds(0, 7)], a_s)
        drain(recv_b, b_s.at[0])
        drain(recv_b.at[pl.ds(1, 15)], b_s.at[1])


def deliver(*refs):
    sem = refs[6]
    moves = [pltpu.make_async_copy(refs[i], refs[3 + i], sem.at[i]) for i in range(3)]
    for move in moves:
        move.start()
    for move in moves:
        move.wait()


def on_device(observed, weights, pairs, positions, centres, assign, amplitude, offsets, widths, block_index):
    dma = pltpu.SemaphoreType.DMA
    operands = [
        pltpu.with_memory_space_constraint(v, pltpu.HBM)
        for v in (
            observed, weights, pairs, positions.T, centres, assign.reshape(1, 256), amplitude.reshape(1, 256), offsets,
            widths.reshape(1, 256),
        )
    ]
    sums = pl.pallas_call(
        kernel,
        out_shape=(
            jax.ShapeDtypeStruct((4, 256), F32),
            jax.ShapeDtypeStruct((2, 32), F32),
            jax.ShapeDtypeStruct((2, 4, 512), F32),
        ),
        in_specs=[pl.BlockSpec(memory_space=pltpu.HBM)] * 9 + [pl.BlockSpec(memory_space=pl.ANY)],
        out_specs=tuple([pl.BlockSpec(memory_space=pltpu.VMEM)] * 3),
        scratch_shapes=[
            pltpu.VMEM((2, 4, 256), F32),
            pltpu.VMEM((4, 256), F32),
            pltpu.VMEM((2, 256), jnp.int32),
            pltpu.VMEM((2, 16), F32),
            pltpu.VMEM((2, 32), F32),
            pltpu.VMEM((1, 256), jnp.int32),
            pltpu.VMEM((1, 256), F32),
            pltpu.VMEM((2, 256), F32),
            pltpu.VMEM((1, 256), F32),
            pltpu.SMEM((1,), jnp.int32),
            pltpu.VMEM((1, 128), F32),
            pltpu.VMEM((16, 1, 128), F32),
            pltpu.VMEM((2, 8, 256), F32),
            pltpu.VMEM((512, 128), F32),
            pltpu.VMEM((512, 128), F32),
            pltpu.VMEM((512, 128), F32),
            pltpu.VMEM((256, 512), BF16),
            pltpu.VMEM((256, 512), BF16),
            pltpu.VMEM((256, 512), BF16),
            pltpu.VMEM((256, 512), BF16),
            pltpu.VMEM((2, 9, 128), F32),
            pltpu.VMEM((15, 9, 128), F32),
            pltpu.VMEM((16, 9, 128), F32),
            pltpu.VMEM((2, 8, 256), F32),
            pltpu.VMEM((4, ROWS, 128), F32),
            pltpu.VMEM((12, ROWS, 128), F32),
            pltpu.VMEM((128, 1024), BF16),
            dma((10,)), dma(()), dma(()), dma((2,)), dma(()), dma((2,)), dma(()), dma(()), dma(()), dma(()), dma(()),
            dma((2,)), dma(()),
        ],
        compiler_params=pltpu.CompilerParams(
            collective_id=0, has_side_effects=True, vmem_limit_bytes=32 * 1024 * 1024
        ),
        name="refit",
    )(*operands, block_index)
    return pl.pallas_call(
        deliver,
        out_shape=tuple(jax.ShapeDtypeStruct(v.shape, F32) for v in sums),
        in_specs=[pl.BlockSpec(memory_space=pltpu.VMEM)] * 3,
        out_specs=tuple([pl.BlockSpec(memory_space=pltpu.HBM)] * 3),
        scratch_shapes=[dma((3,))],
        name="deliver",
    )(*(pltpu.with_memory_space_constraint(v, pltpu.VMEM) for v in sums))


def solution(mesh):
    placed = (
        P(None, "ch", "bl"),
        P("ch", "bl"),
        P(None, "bl"),
        P("bl", None),
        P(),
        P("src"),
        P("src"),
        P(None, "src"),
        P("src"),
        P(),
    )
    return jax.shard_map(
        on_device,
        mesh=mesh,
        in_specs=placed,
        out_specs=(P(None, "src"), P(), P(None, "ch", "bl")),
        check_vma=False,
    )
```

```python
import functools
import math

import jax
import jax.numpy as jnp
from jax import lax
from jax.experimental import pallas as pl
from jax.experimental.pallas import tpu as pltpu
from jax.sharding import PartitionSpec as P

F32 = jnp.float32
BF16 = jnp.bfloat16
LOGICAL = pl.DeviceIdType.LOGICAL
BLOCK_CHANNELS = 16
NU_ZERO = 50000000.0
NU_STEP = 36621.09375
NU_REF = 100000000.0
DK = NU_STEP / NU_REF
CHANS = 4
TWO_PI = 2.0 * math.pi
ENV_COEF = 2.0 * math.pi * math.pi

SIN_COEFS = (4.44288283, -7.30824115, 3.60628896, -0.8457636, 0.10920575)
COS_COEFS = (-1.4142135, 6.97885099, -5.73946117, 1.88356299, -0.31069819)

ROUNDER = 12582912.0
NT = (((1,), (1,)), ((), ()))

TERMS = (
    [(a, n - a, 0) for n in range(4) for a in range(n, -1, -1)]
    + [(a, n - a, 1) for n in range(3) for a in range(n, -1, -1)]
    + [(a, n - a, 2) for n in range(2) for a in range(n, -1, -1)]
)
ROWS = 24
ODD = [j for j, t in enumerate(TERMS) if (t[0] + t[1]) % 2]

STEPS = (2, 1, -1, 0)
Z_STEPS = (-2, 1, -1, 0)


def far_first(offs):
    return sorted((o for o in offs if o != (0, 0, 0)), key=lambda o: (sum(map(abs, o)), o), reverse=True)


GATHER = far_first([(dx, 0, dz) for dx in STEPS for dz in Z_STEPS])
COLUMN = far_first([(0, 0, dz) for dz in (4, 3, 2, 1, 0, -1, -2, -3)])
PLANE = far_first([(dx, dy, 0) for dx in STEPS for dy in STEPS])
PARTNER = (0, 0, 4)
GREET = far_first(
    {((-dx + 1) % 4 - 1, (-dy + 1) % 4 - 1, (-dz + 3) % 8 - 3) for dx, dy, dz in GATHER + COLUMN + PLANE}
)


def here():
    bl = lax.axis_index("bl")
    src = lax.axis_index("src")
    return lax.div(bl, 8), lax.axis_index("ch"), src * 4 + lax.rem(lax.div(bl, 2), 4), lax.rem(bl, 2)


def device(me, off, core):
    x, y, z, _ = me
    dx, dy, dz = off
    x = lax.rem(x + (dx + 4), 4) if dx else x
    y = lax.rem(y + (dy + 4), 4) if dy else y
    z = lax.rem(z + (dz + 8), 8) if dz else z
    return lax.div(z, 4) * 128 + (x * 8 + lax.rem(z, 4) * 2 + core) * 4 + y


def slot_of(off):
    return (off[0] % 4) * 4 + off[2] % 4


def send(src_ref, dst_ref, send_sem, recv_sem, to):
    return pltpu.make_async_remote_copy(
        src_ref=src_ref, dst_ref=dst_ref, send_sem=send_sem, recv_sem=recv_sem, device_id=to, device_id_type=LOGICAL
    )


def drain(ref, sem):
    pltpu.make_async_copy(ref, ref, sem).wait()


def rows_iota(shape):
    return lax.broadcasted_iota(jnp.int32, shape, 0)


def one_of(rows, wanted):
    mask = None
    for w in wanted:
        mask = (rows == w) if mask is None else (mask | (rows == w))
    return mask


def pick(rows, pairs, other=0.0):
    out = other
    for wanted, value in pairs:
        if wanted:
            out = jnp.where(one_of(rows, wanted), value, out)
    return out


def selectors(shape):
    rows = rows_iota(shape)
    out = []
    for which, top in ((0, 3), (1, 3), (2, 2)):
        for n in range(top + 1):
            wanted = [j for j, t in enumerate(TERMS) if t[which] == n]
            out.append(jnp.where(one_of(rows, wanted), 1.0, 0.0) + jnp.zeros(shape, F32))
    return out


def monomials(u, v, w, sel):
    u2, v2 = u * u, v * v
    p = sel[0] + sel[1] * u + sel[2] * u2 + sel[3] * (u2 * u)
    q = sel[4] + sel[5] * v + sel[6] * v2 + sel[7] * (v2 * v)
    return p * q * (sel[8] + sel[9] * w + sel[10] * (w * w))


def channel_factors(k_mid, lanes):
    shape = (ROWS, lanes)
    rows = rows_iota(shape)
    consts = []
    for j, (a, b, e) in enumerate(TERMS):
        n = a + b
        sign = -1.0 if (n // 2) % 2 else 1.0
        consts.append(([j], sign * TWO_PI**n / (math.factorial(a) * math.factorial(b) * math.factorial(e))))
    base = pick(rows, consts) + jnp.zeros(shape, F32)
    out = []
    for f in range(CHANS):
        delta = (f - 0.5 * (CHANS - 1)) * DK
        kappa = (-ENV_COEF * delta) * (2.0 * k_mid + delta)
        phase = pick(
            rows,
            [([j for j, t in enumerate(TERMS) if t[0] + t[1] == n], delta**n) for n in range(1, 4)],
            1.0,
        )
        env = jnp.where(
            one_of(rows, [j for j, t in enumerate(TERMS) if t[2] == 1]),
            kappa,
            jnp.where(one_of(rows, [j for j, t in enumerate(TERMS) if t[2] == 2]), kappa * kappa, 1.0),
        )
        out.append(base * phase * env)
    return out


def split2(x):
    wide = x * 65537.0
    high = wide - (wide - x)
    return high.astype(BF16), (x - high).astype(BF16)


def split3(x):
    high = x.astype(BF16)
    rest = x - high.astype(F32)
    mid = rest.astype(BF16)
    return high, mid, (rest - mid.astype(F32)).astype(BF16)


def kernel(
    obs_h, wts_h, pairs_h, pos_h, cen_h, asg_h, amp_h, off_h, wid_h, blk_h,
    comp_o, centre_o, res_o,
    obs_v, wts_v, pairs_v, pos_v, cen_v, asg_v, amp_v, off_v, wid_v, blk_s,
    sibling, table, comp, lcol, mcol, wcol, ep_a, ep_b, ep_c, ep_d, part, recv_a, recv_b, resid, gs_v, sel_v, hot_v, y_v, pairs_x, obs_x, wts_x, extra,
    in_sem, sib_s, sib_r, gat_s, gat_r, cmp_s, cmp_r, res_s, res_r, x_s, x_r, a_s, a_r, b_s, b_r,
):
    me = here()
    x_me, y_me, z_me, core_me = me
    src = lax.axis_index("src")
    z_low = lax.rem(z_me, 4)
    half = src * 256
    here0, here1 = device(me, (0, 0, 0), 0), device(me, (0, 0, 0), 1)
    is0, is1 = core_me == 0, core_me == 1
    late0 = is0 & (src == 1)
    early0 = is0 & (src == 0)
    early1 = is1 & (src == 0)
    at_end = (z_low == 0) | (z_low == 3)
    barrier = pltpu.get_barrier_semaphore()
    pl.semaphore_signal(barrier, 1, device_id=jnp.where(is0, here1, here0), device_id_type=LOGICAL)
    for off in GREET:
        pl.semaphore_signal(barrier, 1, device_id=device(me, off, 1), device_id_type=LOGICAL)

    halves = pl.ds(pl.multiple_of(half, 256), 256)
    loads = [
        pltpu.make_async_copy(a, b, in_sem.at[i])
        for i, (a, b) in enumerate(
            [
                (pos_h, pos_v), (cen_h, cen_v), (asg_h, asg_v), (amp_h, amp_v), (off_h, off_v), (wid_h, wid_v),
                (pairs_h.at[:, halves], pairs_v), (obs_h.at[:, :, halves], obs_v), (wts_h.at[:, halves], wts_v), (blk_h, blk_s),
            ]
        )
    ]
    for load in loads:
        load.start()

    def hand_over():
        third = slice(256, 384)
        return [
            send(pairs_h.at[:, third], pairs_x, x_s.at[0], x_r.at[0], here1),
            send(obs_h.at[:, :, third], obs_x, x_s.at[1], x_r.at[1], here1),
            send(wts_h.at[:, third], wts_x, x_s.at[2], x_r.at[2], here1),
        ]

    loads[0].wait()
    gap = jnp.zeros((1, 16), F32)
    xs, ys = pos_v[0:1, :], pos_v[1:2, :]
    tail = jnp.zeros((1, 64), F32)

    @pl.when(is0)
    def _():
        sibling[...] = jnp.concatenate([xs, gap, ys, gap, tail], axis=1)
        pl.semaphore_wait(barrier, 1)
        send(sibling, table.at[0], sib_s, sib_r, here1).start()

        @pl.when(early0)
        def _():
            for move in hand_over():
                move.start()

    @pl.when(is1)
    def _():
        sibling[...] = jnp.concatenate([gap, xs, gap, ys, tail], axis=1)

    for load in loads[1:6]:
        load.wait()
    assign = asg_v[...]
    onehot = (jnp.broadcast_to(assign, (32, 256)) == rows_iota((32, 256))).astype(BF16)
    cen_parts = split3(cen_v[...])
    centre = sum(jnp.dot(p, onehot, preferred_element_type=F32) for p in cen_parts)
    lm = centre + off_v[...]
    width = wid_v[...]
    rows8 = rows_iota((8, 256))
    comp[src] = pick(
        rows8,
        [
            ([0], lm[0:1, :]), ([1], lm[1:2, :]), ([2], width * width), ([3], amp_v[...]), ([4], width),
            ([5], assign.astype(F32)),
        ],
    )

    @pl.when(is1)
    def _():
        drain(table.at[0], sib_r)
        table[0] = table[0] + sibling[...]
        pl.semaphore_wait(barrier, 2 * len(GREET) + 1)

        def positions(chips):
            for off in chips:
                for core in (0, 1):
                    send(table.at[0], table.at[slot_of(off)], gat_s.at[core], gat_r, device(me, off, core)).start()

        positions(GATHER[:5])

        @pl.when(at_end)
        def _():
            for step in (1, 2):
                far = lax.rem(z_me + jnp.where(z_low == 0, 8 - step, step), 8)
                for core in (0, 1):
                    to = lax.div(far, 4) * 128 + (x_me * 8 + lax.rem(far, 4) * 2 + core) * 4 + y_me
                    send(comp.at[src], comp.at[src], cmp_s.at[core], cmp_r, to).start()

        positions(GATHER[5:])
        send(table.at[0], table.at[0], gat_s.at[0], gat_r, here0).start()

    loads[6].wait()
    loads[9].wait()
    first = blk_s[0] * BLOCK_CHANNELS + lax.axis_index("ch") * CHANS
    k_mid = (NU_ZERO + (first.astype(F32) + 0.5 * (CHANS - 1)) * NU_STEP) / NU_REF
    ks = [(NU_ZERO + (first + f).astype(F32) * NU_STEP) / NU_REF for f in range(CHANS)]
    for f, factor in enumerate(channel_factors(k_mid, 128)):
        gs_v[f] = factor
    choose = selectors((ROWS, 128))
    for n, one in enumerate(choose):
        sel_v[n] = one
    sel_v[11] = jnp.where(one_of(rows_iota((ROWS, 128)), ODD), 1.0, 0.0)

    def places(ant):
        chip = lax.shift_right_logical(ant, 5)
        return ((x_me - lax.shift_right_logical(chip, 2)) & 3) * 4 + ((z_low - chip) & 3), ant & 31

    slot, inner = places(pairs_v[...])
    rows16 = rows_iota((16, 128))

    drain(comp.at[0], cmp_r)
    both = jnp.concatenate([comp[0], comp[1]], axis=1)
    l_row, m_row, w2_row = both[0:1, :], both[1:2, :], both[2:3, :]
    amp_row, w_row = both[3:4, :], both[4:5, :]
    mono = monomials(l_row, m_row, w2_row, [jnp.concatenate([one] * 4, axis=1) for one in choose])
    amp_high, amp_low = split2(mono * amp_row)
    mono_amp = jnp.concatenate([amp_high, amp_low], axis=0)
    source = jnp.broadcast_to(both[5:6, :], (128, 512))
    rows128 = rows_iota((128, 512)).astype(F32)
    hot_v[:, 0:512] = (source == rows128).astype(BF16)
    hot_v[:, 512:1024] = (source + 32.0 == rows128).astype(BF16)
    cols = jnp.transpose(both)
    lcol[...] = jnp.broadcast_to(cols[:, 0:1], (512, 128))
    mcol[...] = jnp.broadcast_to(cols[:, 1:2], (512, 128))
    wcol[...] = jnp.broadcast_to(cols[:, 2:3], (512, 128))

    @pl.when(is0)
    def _():
        drain(table, gat_r)

    @pl.when(is1)
    def _():
        drain(table.at[pl.ds(1, 15)], gat_r)

    sites = table[:, 0, :]

    def offsets(slot, inner):
        got = []
        for shift in (0, 32):
            total = 0.0
            for a in range(2):
                idx = jnp.broadcast_to(inner[a : a + 1, :] + shift, (16, 128))
                val = jnp.take_along_axis(sites, idx, axis=1, mode="promise_in_bounds")
                val = jnp.where(jnp.broadcast_to(slot[a : a + 1, :], (16, 128)) == rows16, val, 0.0)
                total = total + val if a == 0 else total - val
            got.append(jnp.sum(total, axis=0, keepdims=True))
        return got[0], got[1]

    loads[7].wait()
    loads[8].wait()
    odd = sel_v[11] > 0.5
    gs = [gs_v[f] for f in range(CHANS)]
    sel = [sel_v[n] for n in range(11)]

    eps = (ep_a, ep_b, ep_c, ep_d)

    def terms(t, h, kx, ky, er):
        for i in range(16 * h, 16 * h + 16):
            rows = slice(16 * i, 16 * i + 16)
            lc, mc, wc = lcol[rows, :], mcol[rows, :], wcol[rows, :]
            turns = lc * kx + mc * ky
            env = jnp.exp(wc * er)
            r = turns - ((turns + ROUNDER) - ROUNDER)
            y = r * r
            s = SIN_COEFS[-1]
            for coef in SIN_COEFS[-2::-1]:
                s = s * y + coef
            s = s * r
            c = COS_COEFS[-1]
            for coef in COS_COEFS[-2::-1]:
                c = c * y + coef
            here_ep = eps[2 * t + i // 16]
            inner_rows = slice(16 * (i % 16), 16 * (i % 16) + 16)
            high, low = split2(env * (1.0 - s * s))
            here_ep[inner_rows, 0:128] = high
            here_ep[inner_rows, 256:384] = low
            high, low = split2(env * (s * c))
            here_ep[inner_rows, 128:256] = high
            here_ep[inner_rows, 384:512] = low

    def moments(t, h):
        part_c = slice(256 * h, 256 * h + 256)
        here_ep = eps[2 * t + h]
        high = jnp.dot(mono_amp[:, part_c], here_ep[:, 0:256], preferred_element_type=F32)
        low = jnp.dot(mono_amp[0:ROWS, part_c], here_ep[:, 256:512], preferred_element_type=F32)
        return high[0:ROWS] + high[ROWS:] + low

    def misfit(n, m_all, obs, wts, dx, dy, r2):
        m_r, m_i = m_all[:, 0:128], m_all[:, 128:256]
        base = monomials(dx, dy, r2, sel)
        n_r = base * jnp.where(odd, m_i, m_r)
        n_i = base * jnp.where(odd, -m_r, m_i)
        zero = jnp.zeros((ROWS, 128), F32)
        a0, d0, a1, d1, a2, d2 = zero, zero, zero, zero, zero, zero
        found = jnp.zeros((8, 128), F32)
        rows8 = rows_iota((8, 128))
        for f in range(CHANS):
            v_r = jnp.sum(gs[f] * n_r, axis=0, keepdims=True)
            v_i = jnp.sum(gs[f] * n_i, axis=0, keepdims=True)
            rr = obs[0, f : f + 1, :] - v_r
            ri = obs[1, f : f + 1, :] - v_i
            found = jnp.where(rows8 == f, rr, jnp.where(rows8 == CHANS + f, ri, found))
            wr = wts[f : f + 1, :] * rr
            wi = wts[f : f + 1, :] * ri
            k = ks[f]
            a0 += gs[f] * wr
            d0 += gs[f] * wi
            a1 += gs[f] * (k * wr)
            d1 += gs[f] * (k * wi)
            a2 += gs[f] * (k * k * wr)
            d2 += gs[f] * (k * k * wi)
        (extra if n is None else resid.at[n])[...] = found

        def sides(a, d):
            return jnp.where(odd, -d, a) * base, jnp.where(odd, a, d) * base

        c0, s0 = sides(a0, d0)
        c1, s1 = sides(a1, d1)
        c2, s2 = sides(a2, d2)
        left_r = jnp.concatenate([c0, c2 * r2, -s1 * dx, -s1 * dy], axis=0)
        left_i = jnp.concatenate([s0, s2 * r2, c1 * dx, c1 * dy], axis=0)
        high, low = split2(jnp.concatenate([left_r, left_i], axis=1))
        return high, jnp.concatenate([high, low], axis=0)

    def adjoint(t, left_high, left_both):
        out = []
        for h in range(2):
            here_ep = eps[2 * t + h]
            high = lax.dot_general(left_both, here_ep[:, 0:256], NT, preferred_element_type=F32)
            low = lax.dot_general(left_high, here_ep[:, 256:512], NT, preferred_element_type=F32)
            out.append(high[0 : 4 * ROWS] + high[4 * ROWS :] + low)
        return jnp.concatenate(out, axis=1)

    def tile(n, t, slot, inner, obs, wts):
        dx, dy = offsets(slot, inner)
        r2 = dx * dx + dy * dy
        scales = k_mid * dx, k_mid * dy, (-ENV_COEF * (k_mid * k_mid)) * r2
        terms(t, 0, *scales)
        m_all = moments(t, 0)
        terms(t, 1, *scales)
        m_all += moments(t, 1)
        return adjoint(t, *misfit(n, m_all, obs, wts, dx, dy, r2))

    partner = jnp.where(is0, device(me, PARTNER, 0), device(me, PARTNER, 1))

    def pass_on(n, t):
        return send(resid.at[n], resid.at[n], res_s.at[t], res_r.at[t], partner)

    far, near = slice(128, 256), slice(0, 128)
    y_v[...] = tile(2 * src + 1, 1, slot[:, far], inner[:, far], obs_v[:, :, far], wts_v[:, far])
    pass_on(2 * src + 1, 1).start()

    @pl.when(jnp.logical_not(late0))
    def _():
        y_v[...] += tile(2 * src, 0, slot[:, near], inner[:, near], obs_v[:, :, near], wts_v[:, near])
        pass_on(2 * src, 0).start()

    def spread():
        return [
            send(extra, resid.at[2], x_s.at[3], x_r.at[3], here0),
            send(extra, resid.at[2], x_s.at[4], x_r.at[3], device(me, PARTNER, 0)),
        ]

    @pl.when(early1)
    def _():
        for n, ref in enumerate((pairs_x, obs_x, wts_x)):
            drain(ref, x_r.at[n])
        y_v[...] += tile(None, 0, *places(pairs_x[...]), obs_x, wts_x)
        for move in spread():
            move.start()

    y_all = y_v[...]
    sums = [jnp.sum(y_all[q * ROWS : (q + 1) * ROWS] * mono, axis=0, keepdims=True) for q in range(4)]
    norm = 1.0 / math.sqrt(16384 * BLOCK_CHANNELS)
    grads = [
        -norm * sums[0],
        (-norm * TWO_PI) * amp_row * sums[2],
        (-norm * TWO_PI) * amp_row * sums[3],
        (norm * 2.0 * TWO_PI * math.pi) * amp_row * w_row * sums[1],
    ]

    scaled = (-norm * TWO_PI) * (mono * amp_row)
    to_l, to_m = split2(y_all[2 * ROWS : 3 * ROWS] * scaled), split2(y_all[3 * ROWS : 4 * ROWS] * scaled)
    left = jnp.concatenate([jnp.concatenate([to_l[n], to_m[n]], axis=1) for n in range(2)], axis=0)
    wide = lax.dot_general(left, hot_v[...], NT, preferred_element_type=F32)
    cen_rows = jnp.sum(wide, axis=0, keepdims=True)
    for s in range(2):
        rows = rows_iota((8, 128))
        block = 0.0
        for h in range(2):
            lo = 256 * s + 128 * h
            for q in range(4):
                block = jnp.where(rows == 4 * h + q, grads[q][:, lo : lo + 128], block)
        part[s, 0:8, :] = block
        part[s, 8:9, :] = cen_rows

    def column(core):
        for i, off in enumerate(COLUMN):
            to = lax.div(lax.rem(z_me + (off[2] + 8), 8), 4)
            send(part.at[to], recv_a.at[2 * i + core], a_s, a_r, device(me, off, 1)).start()

    @pl.when(is0)
    def _():
        column(0)
        send(part.at[src], recv_a.at[14], a_s, a_r, here1).start()

    @pl.when(is1)
    def _():
        column(1)
        drain(recv_a, a_r)
        total = part[src]
        for i in range(15):
            total = total + recv_a[i]
        recv_b[0] = total
        for core in (1, 0):
            for i, off in enumerate(PLANE):
                send(recv_b.at[0], recv_b.at[i + 1], b_s.at[core], b_r, device(me, off, core)).start()
        send(recv_b.at[0], recv_b.at[0], b_s.at[0], b_r, here0).start()

    drain(resid.at[0], res_r.at[1])

    @pl.when(jnp.logical_not(early0))
    def _():
        drain(resid.at[0], res_r.at[0])

    @pl.when(is0)
    def _():
        drain(extra, x_r.at[3])

    for n in range(4):
        res_o[0, :, 128 * n : 128 * n + 128] = resid[n, 0:4, :]
        res_o[1, :, 128 * n : 128 * n + 128] = resid[n, 4:8, :]

    @pl.when(is0)
    def _():
        drain(recv_b, b_r)

    @pl.when(is1)
    def _():
        drain(recv_b.at[pl.ds(1, 15)], b_r)

    total = recv_b[0]
    for i in range(1, 16):
        total = total + recv_b[i]
    comp_o[:, 0:128] = total[0:4, :]
    comp_o[:, 128:256] = total[4:8, :]
    centre_o[0:1, :] = total[8:9, 0:32]
    centre_o[1:2, :] = total[8:9, 32:64]

    drain(resid.at[0], res_s.at[1])

    @pl.when(jnp.logical_not(late0))
    def _():
        drain(resid.at[0], res_s.at[0])

    @pl.when(early0)
    def _():
        for move in hand_over():
            move.wait_send()

    @pl.when(early1)
    def _():
        for move in spread():
            move.wait_send()

    @pl.when(is0)
    def _():
        drain(sibling, sib_s)
        drain(recv_a.at[pl.ds(0, 8)], a_s)

    @pl.when(is1)
    def _():
        @pl.when(at_end)
        def _():
            for core in (0, 1):
                drain(comp, cmp_s.at[core])

        drain(table, gat_s.at[0])
        drain(table.at[pl.ds(1, 15)], gat_s.at[1])
        drain(recv_a.at[pl.ds(0, 7)], a_s)
        drain(recv_b, b_s.at[0])
        drain(recv_b.at[pl.ds(1, 15)], b_s.at[1])


def deliver(*refs):
    sem = refs[6]
    moves = [pltpu.make_async_copy(refs[i], refs[3 + i], sem.at[i]) for i in range(3)]
    for move in moves:
        move.start()
    for move in moves:
        move.wait()


def on_device(observed, weights, pairs, positions, centres, assign, amplitude, offsets, widths, block_index):
    dma = pltpu.SemaphoreType.DMA
    operands = [
        pltpu.with_memory_space_constraint(v, pltpu.HBM)
        for v in (
            observed, weights, pairs, positions.T, centres, assign.reshape(1, 256), amplitude.reshape(1, 256), offsets,
            widths.reshape(1, 256),
        )
    ]
    sums = pl.pallas_call(
        kernel,
        out_shape=(
            jax.ShapeDtypeStruct((4, 256), F32),
            jax.ShapeDtypeStruct((2, 32), F32),
            jax.ShapeDtypeStruct((2, 4, 512), F32),
        ),
        in_specs=[pl.BlockSpec(memory_space=pltpu.HBM)] * 9 + [pl.BlockSpec(memory_space=pl.ANY)],
        out_specs=tuple([pl.BlockSpec(memory_space=pltpu.VMEM)] * 3),
        scratch_shapes=[
            pltpu.VMEM((2, 4, 256), F32),
            pltpu.VMEM((4, 256), F32),
            pltpu.VMEM((2, 256), jnp.int32),
            pltpu.VMEM((2, 16), F32),
            pltpu.VMEM((2, 32), F32),
            pltpu.VMEM((1, 256), jnp.int32),
            pltpu.VMEM((1, 256), F32),
            pltpu.VMEM((2, 256), F32),
            pltpu.VMEM((1, 256), F32),
            pltpu.SMEM((1,), jnp.int32),
            pltpu.VMEM((1, 128), F32),
            pltpu.VMEM((16, 1, 128), F32),
            pltpu.VMEM((2, 8, 256), F32),
            pltpu.VMEM((512, 128), F32),
            pltpu.VMEM((512, 128), F32),
            pltpu.VMEM((512, 128), F32),
            pltpu.VMEM((256, 512), BF16),
            pltpu.VMEM((256, 512), BF16),
            pltpu.VMEM((256, 512), BF16),
            pltpu.VMEM((256, 512), BF16),
            pltpu.VMEM((2, 9, 128), F32),
            pltpu.VMEM((15, 9, 128), F32),
            pltpu.VMEM((16, 9, 128), F32),
            pltpu.VMEM((4, 8, 128), F32),
            pltpu.VMEM((4, ROWS, 128), F32),
            pltpu.VMEM((12, ROWS, 128), F32),
            pltpu.VMEM((128, 1024), BF16),
            pltpu.VMEM((4 * ROWS, 512), F32),
            pltpu.VMEM((2, 128), jnp.int32),
            pltpu.VMEM((2, 4, 128), F32),
            pltpu.VMEM((4, 128), F32),
            pltpu.VMEM((8, 128), F32),
            dma((10,)), dma(()), dma(()), dma((2,)), dma(()), dma((2,)), dma(()), dma((2,)), dma((2,)), dma((5,)), dma((4,)), dma(()), dma(()),
            dma((2,)), dma(()),
        ],
        compiler_params=pltpu.CompilerParams(
            collective_id=0, has_side_effects=True, vmem_limit_bytes=32 * 1024 * 1024
        ),
        name="refit",
    )(*operands, block_index)
    return pl.pallas_call(
        deliver,
        out_shape=tuple(jax.ShapeDtypeStruct(v.shape, F32) for v in sums),
        in_specs=[pl.BlockSpec(memory_space=pltpu.VMEM)] * 3,
        out_specs=tuple([pl.BlockSpec(memory_space=pltpu.HBM)] * 3),
        scratch_shapes=[dma((3,))],
        name="deliver",
    )(*(pltpu.with_memory_space_constraint(v, pltpu.VMEM) for v in sums))


def solution(mesh):
    placed = (
        P(None, "ch", "bl"),
        P("ch", "bl"),
        P(None, "bl"),
        P("bl", None),
        P(),
        P("src"),
        P("src"),
        P(None, "src"),
        P("src"),
        P(),
    )
    return jax.shard_map(
        on_device,
        mesh=mesh,
        in_specs=placed,
        out_specs=(P(None, "src"), P(), P(None, "ch", "bl")),
        check_vma=False,
    )
```

```python
import functools
import math

import jax
import jax.numpy as jnp
from jax import lax
from jax.experimental import pallas as pl
from jax.experimental.pallas import tpu as pltpu
from jax.sharding import PartitionSpec as P

F32 = jnp.float32
BF16 = jnp.bfloat16
LOGICAL = pl.DeviceIdType.LOGICAL
BLOCK_CHANNELS = 16
NU_ZERO = 50000000.0
NU_STEP = 36621.09375
NU_REF = 100000000.0
DK = NU_STEP / NU_REF
CHANS = 4
TWO_PI = 2.0 * math.pi
ENV_COEF = 2.0 * math.pi * math.pi

SIN_COEFS = (4.44288283, -7.30824115, 3.60628896, -0.8457636, 0.10920575)
COS_COEFS = (-1.4142135, 6.97885099, -5.73946117, 1.88356299, -0.31069819)

ROUNDER = 12582912.0
NT = (((1,), (1,)), ((), ()))

TERMS = (
    [(a, n - a, 0) for n in range(4) for a in range(n, -1, -1)]
    + [(a, n - a, 1) for n in range(3) for a in range(n, -1, -1)]
    + [(a, n - a, 2) for n in range(2) for a in range(n, -1, -1)]
)
ROWS = 24
ODD = [j for j, t in enumerate(TERMS) if (t[0] + t[1]) % 2]

STEPS = (2, 1, -1, 0)
Z_STEPS = (-2, 1, -1, 0)


def far_first(offs):
    return sorted((o for o in offs if o != (0, 0, 0)), key=lambda o: (sum(map(abs, o)), o), reverse=True)


GATHER = far_first([(dx, 0, dz) for dx in STEPS for dz in Z_STEPS])
COLUMN = far_first([(0, 0, dz) for dz in (4, 3, 2, 1, 0, -1, -2, -3)])
PLANE = far_first([(dx, dy, 0) for dx in STEPS for dy in STEPS])
PARTNER = (0, 0, 4)
GREET = far_first(
    {((-dx + 1) % 4 - 1, (-dy + 1) % 4 - 1, (-dz + 3) % 8 - 3) for dx, dy, dz in GATHER + COLUMN + PLANE}
)


def here():
    bl = lax.axis_index("bl")
    src = lax.axis_index("src")
    return lax.div(bl, 8), lax.axis_index("ch"), src * 4 + lax.rem(lax.div(bl, 2), 4), lax.rem(bl, 2)


def device(me, off, core):
    x, y, z, _ = me
    dx, dy, dz = off
    x = lax.rem(x + (dx + 4), 4) if dx else x
    y = lax.rem(y + (dy + 4), 4) if dy else y
    z = lax.rem(z + (dz + 8), 8) if dz else z
    return lax.div(z, 4) * 128 + (x * 8 + lax.rem(z, 4) * 2 + core) * 4 + y


def slot_of(off):
    return (off[0] % 4) * 4 + off[2] % 4


def send(src_ref, dst_ref, send_sem, recv_sem, to):
    return pltpu.make_async_remote_copy(
        src_ref=src_ref, dst_ref=dst_ref, send_sem=send_sem, recv_sem=recv_sem, device_id=to, device_id_type=LOGICAL
    )


def drain(ref, sem):
    pltpu.make_async_copy(ref, ref, sem).wait()


def rows_iota(shape):
    return lax.broadcasted_iota(jnp.int32, shape, 0)


def one_of(rows, wanted):
    mask = None
    for w in wanted:
        mask = (rows == w) if mask is None else (mask | (rows == w))
    return mask


def pick(rows, pairs, other=0.0):
    out = other
    for wanted, value in pairs:
        if wanted:
            out = jnp.where(one_of(rows, wanted), value, out)
    return out


def selectors(shape):
    rows = rows_iota(shape)
    out = []
    for which, top in ((0, 3), (1, 3), (2, 2)):
        for n in range(top + 1):
            wanted = [j for j, t in enumerate(TERMS) if t[which] == n]
            out.append(jnp.where(one_of(rows, wanted), 1.0, 0.0) + jnp.zeros(shape, F32))
    return out


def monomials(u, v, w, sel):
    u2, v2 = u * u, v * v
    p = sel[0] + sel[1] * u + sel[2] * u2 + sel[3] * (u2 * u)
    q = sel[4] + sel[5] * v + sel[6] * v2 + sel[7] * (v2 * v)
    return p * q * (sel[8] + sel[9] * w + sel[10] * (w * w))


def channel_factors(k_mid, lanes):
    shape = (ROWS, lanes)
    rows = rows_iota(shape)
    consts = []
    for j, (a, b, e) in enumerate(TERMS):
        n = a + b
        sign = -1.0 if (n // 2) % 2 else 1.0
        consts.append(([j], sign * TWO_PI**n / (math.factorial(a) * math.factorial(b) * math.factorial(e))))
    base = pick(rows, consts) + jnp.zeros(shape, F32)
    out = []
    for f in range(CHANS):
        delta = (f - 0.5 * (CHANS - 1)) * DK
        kappa = (-ENV_COEF * delta) * (2.0 * k_mid + delta)
        phase = pick(
            rows,
            [([j for j, t in enumerate(TERMS) if t[0] + t[1] == n], delta**n) for n in range(1, 4)],
            1.0,
        )
        env = jnp.where(
            one_of(rows, [j for j, t in enumerate(TERMS) if t[2] == 1]),
            kappa,
            jnp.where(one_of(rows, [j for j, t in enumerate(TERMS) if t[2] == 2]), kappa * kappa, 1.0),
        )
        out.append(base * phase * env)
    return out


def split2(x):
    wide = x * 65537.0
    high = wide - (wide - x)
    return high.astype(BF16), (x - high).astype(BF16)


def split3(x):
    high = x.astype(BF16)
    rest = x - high.astype(F32)
    mid = rest.astype(BF16)
    return high, mid, (rest - mid.astype(F32)).astype(BF16)


def kernel(
    obs_h, wts_h, pairs_h, pos_h, cen_h, asg_h, amp_h, off_h, wid_h, blk_h,
    comp_o, centre_o, res_o,
    obs_v, wts_v, pairs_v, pos_v, cen_v, asg_v, amp_v, off_v, wid_v, blk_s, row_s,
    sibling, table, comp, lcol, mcol, wcol, ep_a, ep_b, ep_c, ep_d, part, recv_a, recv_b, resid, gs_v, sel_v, hot_v, y_v, pairs_x, obs_x, wts_x, extra,
    in_sem, row_sem, sib_s, sib_r, gat_s, gat_r, cmp_s, cmp_r, res_s, res_r, x_s, x_r, a_s, a_r, b_s, b_r,
):
    me = here()
    x_me, y_me, z_me, core_me = me
    src = lax.axis_index("src")
    z_low = lax.rem(z_me, 4)
    half = src * 256
    here0, here1 = device(me, (0, 0, 0), 0), device(me, (0, 0, 0), 1)
    is0, is1 = core_me == 0, core_me == 1
    late0 = is0 & (src == 1)
    early0 = is0 & (src == 0)
    early1 = is1 & (src == 0)
    at_end = (z_low == 0) | (z_low == 3)
    barrier = pltpu.get_barrier_semaphore()
    pl.semaphore_signal(barrier, 1, device_id=jnp.where(is0, here1, here0), device_id_type=LOGICAL)
    for off in GREET:
        pl.semaphore_signal(barrier, 1, device_id=device(me, off, 1), device_id_type=LOGICAL)

    halves = pl.ds(pl.multiple_of(half, 256), 256)
    loads = [
        pltpu.make_async_copy(a, b, in_sem.at[i])
        for i, (a, b) in enumerate(
            [
                (pos_h, pos_v), (cen_h, cen_v), (asg_h, asg_v), (amp_h, amp_v), (off_h, off_v), (wid_h, wid_v),
                (pairs_h.at[:, halves], pairs_v), (obs_h.at[:, :, halves], obs_v), (wts_h.at[:, halves], wts_v), (blk_h, blk_s),
            ]
        )
    ]
    for load in loads:
        load.start()

    def hand_over():
        third = slice(256, 384)
        return [
            send(pairs_h.at[:, third], pairs_x, x_s.at[0], x_r.at[0], here1),
            send(obs_h.at[:, :, third], obs_x, x_s.at[1], x_r.at[1], here1),
            send(wts_h.at[:, third], wts_x, x_s.at[2], x_r.at[2], here1),
        ]

    loads[0].wait()
    gap = jnp.zeros((1, 16), F32)
    xs, ys = pos_v[0:1, :], pos_v[1:2, :]
    tail = jnp.zeros((1, 64), F32)

    @pl.when(is0)
    def _():
        sibling[...] = jnp.concatenate([xs, gap, ys, gap, tail], axis=1)
        pl.semaphore_wait(barrier, 1)
        send(sibling, table.at[0], sib_s, sib_r, here1).start()

        @pl.when(early0)
        def _():
            for move in hand_over():
                move.start()

    @pl.when(is1)
    def _():
        sibling[...] = jnp.concatenate([gap, xs, gap, ys, tail], axis=1)

    for load in loads[1:6]:
        load.wait()
    assign = asg_v[...]
    onehot = (jnp.broadcast_to(assign, (32, 256)) == rows_iota((32, 256))).astype(BF16)
    cen_parts = split3(cen_v[...])
    centre = sum(jnp.dot(p, onehot, preferred_element_type=F32) for p in cen_parts)
    lm = centre + off_v[...]
    width = wid_v[...]
    rows8 = rows_iota((8, 256))
    comp[src] = pick(
        rows8,
        [
            ([0], lm[0:1, :]), ([1], lm[1:2, :]), ([2], width * width), ([3], amp_v[...]), ([4], width),
            ([5], assign.astype(F32)),
        ],
    )

    @pl.when(is1)
    def _():
        drain(table.at[0], sib_r)
        table[0] = table[0] + sibling[...]
        to_scalar = pltpu.make_async_copy(table.at[0], row_s, row_sem)
        to_scalar.start()
        to_scalar.wait()
        pl.semaphore_wait(barrier, 2 * len(GREET) + 1)

        def positions(chips):
            for off in chips:
                for core in (0, 1):
                    send(row_s, table.at[slot_of(off)], gat_s.at[core], gat_r, device(me, off, core)).start()

        positions(GATHER[:5])

        @pl.when(at_end)
        def _():
            for step in (1, 2):
                far = lax.rem(z_me + jnp.where(z_low == 0, 8 - step, step), 8)
                for core in (0, 1):
                    to = lax.div(far, 4) * 128 + (x_me * 8 + lax.rem(far, 4) * 2 + core) * 4 + y_me
                    send(comp.at[src], comp.at[src], cmp_s.at[core], cmp_r, to).start()

        positions(GATHER[5:])
        send(row_s, table.at[0], gat_s.at[0], gat_r, here0).start()

    loads[6].wait()
    loads[9].wait()
    first = blk_s[0] * BLOCK_CHANNELS + lax.axis_index("ch") * CHANS
    k_mid = (NU_ZERO + (first.astype(F32) + 0.5 * (CHANS - 1)) * NU_STEP) / NU_REF
    ks = [(NU_ZERO + (first + f).astype(F32) * NU_STEP) / NU_REF for f in range(CHANS)]
    for f, factor in enumerate(channel_factors(k_mid, 128)):
        gs_v[f] = factor
    choose = selectors((ROWS, 128))
    for n, one in enumerate(choose):
        sel_v[n] = one
    sel_v[11] = jnp.where(one_of(rows_iota((ROWS, 128)), ODD), 1.0, 0.0)

    def places(ant):
        chip = lax.shift_right_logical(ant, 5)
        return ((x_me - lax.shift_right_logical(chip, 2)) & 3) * 4 + ((z_low - chip) & 3), ant & 31

    slot, inner = places(pairs_v[...])
    rows16 = rows_iota((16, 128))

    drain(comp.at[0], cmp_r)
    both = jnp.concatenate([comp[0], comp[1]], axis=1)
    l_row, m_row, w2_row = both[0:1, :], both[1:2, :], both[2:3, :]
    amp_row, w_row = both[3:4, :], both[4:5, :]
    mono = monomials(l_row, m_row, w2_row, [jnp.concatenate([one] * 4, axis=1) for one in choose])
    amp_high, amp_low = split2(mono * amp_row)
    mono_amp = jnp.concatenate([amp_high, amp_low], axis=0)
    rows128 = rows_iota((128, 512))
    source = jnp.broadcast_to(both[5:6, :], (128, 512))
    hot_v[...] = ((source == (rows128 & 31).astype(F32)) & (rows128 < 64)).astype(BF16)
    cols = jnp.transpose(both)
    lcol[...] = jnp.broadcast_to(cols[:, 0:1], (512, 128))
    mcol[...] = jnp.broadcast_to(cols[:, 1:2], (512, 128))
    wcol[...] = jnp.broadcast_to(cols[:, 2:3], (512, 128))

    @pl.when(is0)
    def _():
        drain(table, gat_r)

    @pl.when(is1)
    def _():
        drain(table.at[pl.ds(1, 15)], gat_r)

    sites = table[:, 0, :]

    def offsets(slot, inner):
        got = []
        for shift in (0, 32):
            total = 0.0
            for a in range(2):
                idx = jnp.broadcast_to(inner[a : a + 1, :] + shift, (16, 128))
                val = jnp.take_along_axis(sites, idx, axis=1, mode="promise_in_bounds")
                val = jnp.where(jnp.broadcast_to(slot[a : a + 1, :], (16, 128)) == rows16, val, 0.0)
                total = total + val if a == 0 else total - val
            got.append(jnp.sum(total, axis=0, keepdims=True))
        return got[0], got[1]

    loads[7].wait()
    loads[8].wait()
    odd = sel_v[11] > 0.5
    gs = [gs_v[f] for f in range(CHANS)]
    sel = [sel_v[n] for n in range(11)]

    eps = (ep_a, ep_b, ep_c, ep_d)

    def terms(t, h, kx, ky, er):
        for i in range(16 * h, 16 * h + 16):
            rows = slice(16 * i, 16 * i + 16)
            lc, mc, wc = lcol[rows, :], mcol[rows, :], wcol[rows, :]
            turns = lc * kx + mc * ky
            env = jnp.exp(wc * er)
            r = turns - ((turns + ROUNDER) - ROUNDER)
            y = r * r
            s = SIN_COEFS[-1]
            for coef in SIN_COEFS[-2::-1]:
                s = s * y + coef
            s = s * r
            c = COS_COEFS[-1]
            for coef in COS_COEFS[-2::-1]:
                c = c * y + coef
            here_ep = eps[2 * t + i // 16]
            inner_rows = slice(16 * (i % 16), 16 * (i % 16) + 16)
            es = env * s
            high, low = split2(env - es * s)
            here_ep[inner_rows, 0:128] = high
            here_ep[inner_rows, 256:384] = low
            high, low = split2(es * c)
            here_ep[inner_rows, 128:256] = high
            here_ep[inner_rows, 384:512] = low

    def moments(t, h):
        part_c = slice(256 * h, 256 * h + 256)
        here_ep = eps[2 * t + h]
        high = jnp.dot(mono_amp[:, part_c], here_ep[:, 0:256], preferred_element_type=F32)
        low = jnp.dot(mono_amp[0:ROWS, part_c], here_ep[:, 256:512], preferred_element_type=F32)
        return high[0:ROWS] + high[ROWS:] + low

    def misfit(n, m_all, obs, wts, dx, dy, r2):
        m_r, m_i = m_all[:, 0:128], m_all[:, 128:256]
        base = monomials(dx, dy, r2, sel)
        n_r = base * jnp.where(odd, m_i, m_r)
        n_i = base * jnp.where(odd, -m_r, m_i)
        zero = jnp.zeros((ROWS, 128), F32)
        a0, d0, a1, d1, a2, d2 = zero, zero, zero, zero, zero, zero
        found = jnp.zeros((8, 128), F32)
        rows8 = rows_iota((8, 128))
        for f in range(CHANS):
            v_r = jnp.sum(gs[f] * n_r, axis=0, keepdims=True)
            v_i = jnp.sum(gs[f] * n_i, axis=0, keepdims=True)
            rr = obs[0, f : f + 1, :] - v_r
            ri = obs[1, f : f + 1, :] - v_i
            found = jnp.where(rows8 == f, rr, jnp.where(rows8 == CHANS + f, ri, found))
            wr = wts[f : f + 1, :] * rr
            wi = wts[f : f + 1, :] * ri
            k = ks[f]
            a0 += gs[f] * wr
            d0 += gs[f] * wi
            a1 += gs[f] * (k * wr)
            d1 += gs[f] * (k * wi)
            a2 += gs[f] * (k * k * wr)
            d2 += gs[f] * (k * k * wi)
        (extra if n is None else resid.at[n])[...] = found

        def sides(a, d):
            return jnp.where(odd, -d, a) * base, jnp.where(odd, a, d) * base

        c0, s0 = sides(a0, d0)
        c1, s1 = sides(a1, d1)
        c2, s2 = sides(a2, d2)
        left_r = jnp.concatenate([c0, c2 * r2, -s1 * dx, -s1 * dy], axis=0)
        left_i = jnp.concatenate([s0, s2 * r2, c1 * dx, c1 * dy], axis=0)
        high, low = split2(jnp.concatenate([left_r, left_i], axis=1))
        return high, jnp.concatenate([high, low], axis=0)

    def adjoint(t, left_high, left_both):
        out = []
        for h in range(2):
            here_ep = eps[2 * t + h]
            high = lax.dot_general(left_both, here_ep[:, 0:256], NT, preferred_element_type=F32)
            low = lax.dot_general(left_high, here_ep[:, 256:512], NT, preferred_element_type=F32)
            out.append(high[0 : 4 * ROWS] + high[4 * ROWS :] + low)
        return jnp.concatenate(out, axis=1)

    def tile(n, t, slot, inner, obs, wts):
        dx, dy = offsets(slot, inner)
        r2 = dx * dx + dy * dy
        scales = k_mid * dx, k_mid * dy, (-ENV_COEF * (k_mid * k_mid)) * r2
        terms(t, 0, *scales)
        m_all = moments(t, 0)
        terms(t, 1, *scales)
        m_all += moments(t, 1)
        return adjoint(t, *misfit(n, m_all, obs, wts, dx, dy, r2))

    partner = jnp.where(is0, device(me, PARTNER, 0), device(me, PARTNER, 1))

    def pass_on(n, t):
        return send(resid.at[n], resid.at[n], res_s.at[t], res_r.at[t], partner)

    far, near = slice(128, 256), slice(0, 128)
    y_v[...] = tile(2 * src + 1, 1, slot[:, far], inner[:, far], obs_v[:, :, far], wts_v[:, far])
    pass_on(2 * src + 1, 1).start()

    @pl.when(jnp.logical_not(late0))
    def _():
        y_v[...] += tile(2 * src, 0, slot[:, near], inner[:, near], obs_v[:, :, near], wts_v[:, near])
        pass_on(2 * src, 0).start()

    def spread():
        return [
            send(extra, resid.at[2], x_s.at[3], x_r.at[3], here0),
            send(extra, resid.at[2], x_s.at[4], x_r.at[3], device(me, PARTNER, 0)),
        ]

    @pl.when(early1)
    def _():
        for n, ref in enumerate((pairs_x, obs_x, wts_x)):
            drain(ref, x_r.at[n])
        y_v[...] += tile(None, 0, *places(pairs_x[...]), obs_x, wts_x)
        for move in spread():
            move.start()

    y_all = y_v[...]
    sums = [jnp.sum(y_all[q * ROWS : (q + 1) * ROWS] * mono, axis=0, keepdims=True) for q in range(4)]
    norm = 1.0 / math.sqrt(16384 * BLOCK_CHANNELS)
    grads = [
        -norm * sums[0],
        (-norm * TWO_PI) * amp_row * sums[2],
        (-norm * TWO_PI) * amp_row * sums[3],
        (norm * 2.0 * TWO_PI * math.pi) * amp_row * w_row * sums[1],
    ]

    rows8w = rows_iota((8, 512))
    pair = jnp.where(rows8w < 2, grads[1], grads[2])
    high = pair * 65537.0
    high = high - (high - pair)
    left = jnp.where((rows8w & 1) == 0, high, pair - high).astype(BF16)
    wide = lax.dot_general(left, hot_v[...], NT, preferred_element_type=F32)
    lanes1 = lax.broadcasted_iota(jnp.int32, (8, 128), 1)
    rows8n = rows_iota((8, 128))
    mine = (rows8n < 4) & (lax.shift_right_logical(rows8n, 1) == lax.shift_right_logical(lanes1, 5))
    cen_rows = jnp.sum(jnp.where(mine, wide, 0.0), axis=0, keepdims=True)
    for s in range(2):
        rows = rows_iota((8, 128))
        block = 0.0
        for h in range(2):
            lo = 256 * s + 128 * h
            for q in range(4):
                block = jnp.where(rows == 4 * h + q, grads[q][:, lo : lo + 128], block)
        part[s, 0:8, :] = block
        part[s, 8:9, :] = cen_rows

    def column(core):
        for i, off in enumerate(COLUMN):
            to = lax.div(lax.rem(z_me + (off[2] + 8), 8), 4)
            send(part.at[to], recv_a.at[2 * i + core], a_s, a_r, device(me, off, 1)).start()

    @pl.when(is0)
    def _():
        column(0)
        send(part.at[src], recv_a.at[14], a_s, a_r, here1).start()

    @pl.when(is1)
    def _():
        column(1)
        drain(recv_a, a_r)
        total = part[src]
        for i in range(15):
            total = total + recv_a[i]
        recv_b[0] = total
        for core in (1, 0):
            for i, off in enumerate(PLANE):
                send(recv_b.at[0], recv_b.at[i + 1], b_s.at[core], b_r, device(me, off, core)).start()
        send(recv_b.at[0], recv_b.at[0], b_s.at[0], b_r, here0).start()

    drain(resid.at[0], res_r.at[1])

    @pl.when(jnp.logical_not(early0))
    def _():
        drain(resid.at[0], res_r.at[0])

    @pl.when(is0)
    def _():
        drain(extra, x_r.at[3])

    for n in range(4):
        res_o[0, :, 128 * n : 128 * n + 128] = resid[n, 0:4, :]
        res_o[1, :, 128 * n : 128 * n + 128] = resid[n, 4:8, :]

    @pl.when(is0)
    def _():
        drain(recv_b, b_r)

    @pl.when(is1)
    def _():
        drain(recv_b.at[pl.ds(1, 15)], b_r)

    total = recv_b[0]
    for i in range(1, 16):
        total = total + recv_b[i]
    comp_o[:, 0:128] = total[0:4, :]
    comp_o[:, 128:256] = total[4:8, :]
    centre_o[0:1, :] = total[8:9, 0:32]
    centre_o[1:2, :] = total[8:9, 32:64]

    drain(resid.at[0], res_s.at[1])

    @pl.when(jnp.logical_not(late0))
    def _():
        drain(resid.at[0], res_s.at[0])

    @pl.when(early0)
    def _():
        for move in hand_over():
            move.wait_send()

    @pl.when(early1)
    def _():
        for move in spread():
            move.wait_send()

    @pl.when(is0)
    def _():
        drain(sibling, sib_s)
        drain(recv_a.at[pl.ds(0, 8)], a_s)

    @pl.when(is1)
    def _():
        @pl.when(at_end)
        def _():
            for core in (0, 1):
                drain(comp, cmp_s.at[core])

        drain(table, gat_s.at[0])
        drain(table.at[pl.ds(1, 15)], gat_s.at[1])
        drain(recv_a.at[pl.ds(0, 7)], a_s)
        drain(recv_b, b_s.at[0])
        drain(recv_b.at[pl.ds(1, 15)], b_s.at[1])


def deliver(*refs):
    sem = refs[6]
    moves = [pltpu.make_async_copy(refs[i], refs[3 + i], sem.at[i]) for i in range(3)]
    for move in moves:
        move.start()
    for move in moves:
        move.wait()


def on_device(observed, weights, pairs, positions, centres, assign, amplitude, offsets, widths, block_index):
    dma = pltpu.SemaphoreType.DMA
    operands = [
        pltpu.with_memory_space_constraint(v, pltpu.HBM)
        for v in (
            observed, weights, pairs, positions.T, centres, assign.reshape(1, 256), amplitude.reshape(1, 256), offsets,
            widths.reshape(1, 256),
        )
    ]
    sums = pl.pallas_call(
        kernel,
        out_shape=(
            jax.ShapeDtypeStruct((4, 256), F32),
            jax.ShapeDtypeStruct((2, 32), F32),
            jax.ShapeDtypeStruct((2, 4, 512), F32),
        ),
        in_specs=[pl.BlockSpec(memory_space=pltpu.HBM)] * 9 + [pl.BlockSpec(memory_space=pl.ANY)],
        out_specs=tuple([pl.BlockSpec(memory_space=pltpu.VMEM)] * 3),
        scratch_shapes=[
            pltpu.VMEM((2, 4, 256), F32),
            pltpu.VMEM((4, 256), F32),
            pltpu.VMEM((2, 256), jnp.int32),
            pltpu.VMEM((2, 16), F32),
            pltpu.VMEM((2, 32), F32),
            pltpu.VMEM((1, 256), jnp.int32),
            pltpu.VMEM((1, 256), F32),
            pltpu.VMEM((2, 256), F32),
            pltpu.VMEM((1, 256), F32),
            pltpu.SMEM((1,), jnp.int32),
            pltpu.SMEM((1, 128), F32),
            pltpu.VMEM((1, 128), F32),
            pltpu.VMEM((16, 1, 128), F32),
            pltpu.VMEM((2, 8, 256), F32),
            pltpu.VMEM((512, 128), F32),
            pltpu.VMEM((512, 128), F32),
            pltpu.VMEM((512, 128), F32),
            pltpu.VMEM((256, 512), BF16),
            pltpu.VMEM((256, 512), BF16),
            pltpu.VMEM((256, 512), BF16),
            pltpu.VMEM((256, 512), BF16),
            pltpu.VMEM((2, 9, 128), F32),
            pltpu.VMEM((15, 9, 128), F32),
            pltpu.VMEM((16, 9, 128), F32),
            pltpu.VMEM((4, 8, 128), F32),
            pltpu.VMEM((4, ROWS, 128), F32),
            pltpu.VMEM((12, ROWS, 128), F32),
            pltpu.VMEM((128, 512), BF16),
            pltpu.VMEM((4 * ROWS, 512), F32),
            pltpu.VMEM((2, 128), jnp.int32),
            pltpu.VMEM((2, 4, 128), F32),
            pltpu.VMEM((4, 128), F32),
            pltpu.VMEM((8, 128), F32),
            dma((10,)), dma(()), dma(()), dma(()), dma((2,)), dma(()), dma((2,)), dma(()), dma((2,)), dma((2,)), dma((5,)), dma((4,)), dma(()), dma(()),
            dma((2,)), dma(()),
        ],
        compiler_params=pltpu.CompilerParams(
            collective_id=0, has_side_effects=True, vmem_limit_bytes=32 * 1024 * 1024
        ),
        name="refit",
    )(*operands, block_index)
    return pl.pallas_call(
        deliver,
        out_shape=tuple(jax.ShapeDtypeStruct(v.shape, F32) for v in sums),
        in_specs=[pl.BlockSpec(memory_space=pltpu.VMEM)] * 3,
        out_specs=tuple([pl.BlockSpec(memory_space=pltpu.HBM)] * 3),
        scratch_shapes=[dma((3,))],
        name="deliver",
    )(*(pltpu.with_memory_space_constraint(v, pltpu.VMEM) for v in sums))


def solution(mesh):
    placed = (
        P(None, "ch", "bl"),
        P("ch", "bl"),
        P(None, "bl"),
        P("bl", None),
        P(),
        P("src"),
        P("src"),
        P(None, "src"),
        P("src"),
        P(),
    )
    return jax.shard_map(
        on_device,
        mesh=mesh,
        in_specs=placed,
        out_specs=(P(None, "src"), P(), P(None, "ch", "bl")),
        check_vma=False,
    )
```

```python
import functools
import math

import jax
import jax.numpy as jnp
from jax import lax
from jax.experimental import pallas as pl
from jax.experimental.pallas import tpu as pltpu
from jax.sharding import PartitionSpec as P

F32 = jnp.float32
BF16 = jnp.bfloat16
LOGICAL = pl.DeviceIdType.LOGICAL
BLOCK_CHANNELS = 16
NU_ZERO = 50000000.0
NU_STEP = 36621.09375
NU_REF = 100000000.0
DK = NU_STEP / NU_REF
CHANS = 4
TWO_PI = 2.0 * math.pi
ENV_COEF = 2.0 * math.pi * math.pi

SIN_COEFS = (4.44288283, -7.30824115, 3.60628896, -0.8457636, 0.10920575)
COS_COEFS = (-1.4142135, 6.97885099, -5.73946117, 1.88356299, -0.31069819)

ROUNDER = 12582912.0
NT = (((1,), (1,)), ((), ()))

TERMS = (
    [(a, n - a, 0) for n in range(4) for a in range(n, -1, -1)]
    + [(a, n - a, 1) for n in range(3) for a in range(n, -1, -1)]
    + [(a, n - a, 2) for n in range(2) for a in range(n, -1, -1)]
)
ROWS = 24
ODD = [j for j, t in enumerate(TERMS) if (t[0] + t[1]) % 2]

STEPS = (2, 1, -1, 0)
Z_STEPS = (-2, 1, -1, 0)


def far_first(offs):
    return sorted((o for o in offs if o != (0, 0, 0)), key=lambda o: (sum(map(abs, o)), o), reverse=True)


GATHER = far_first([(dx, 0, dz) for dx in STEPS for dz in Z_STEPS])
COLUMN = far_first([(0, 0, dz) for dz in (4, 3, 2, 1, 0, -1, -2, -3)])
PLANE = far_first([(dx, dy, 0) for dx in STEPS for dy in STEPS])
PARTNER = (0, 0, 4)
GREET = far_first(
    {((-dx + 1) % 4 - 1, (-dy + 1) % 4 - 1, (-dz + 3) % 8 - 3) for dx, dy, dz in GATHER + COLUMN + PLANE}
)


def here():
    bl = lax.axis_index("bl")
    src = lax.axis_index("src")
    return lax.div(bl, 8), lax.axis_index("ch"), src * 4 + lax.rem(lax.div(bl, 2), 4), lax.rem(bl, 2)


def device(me, off, core):
    x, y, z, _ = me
    dx, dy, dz = off
    x = lax.rem(x + (dx + 4), 4) if dx else x
    y = lax.rem(y + (dy + 4), 4) if dy else y
    z = lax.rem(z + (dz + 8), 8) if dz else z
    return lax.div(z, 4) * 128 + (x * 8 + lax.rem(z, 4) * 2 + core) * 4 + y


def slot_of(off):
    return (off[0] % 4) * 4 + off[2] % 4


def send(src_ref, dst_ref, send_sem, recv_sem, to):
    return pltpu.make_async_remote_copy(
        src_ref=src_ref, dst_ref=dst_ref, send_sem=send_sem, recv_sem=recv_sem, device_id=to, device_id_type=LOGICAL
    )


def drain(ref, sem):
    pltpu.make_async_copy(ref, ref, sem).wait()


def rows_iota(shape):
    return lax.broadcasted_iota(jnp.int32, shape, 0)


def one_of(rows, wanted):
    mask = None
    for w in wanted:
        mask = (rows == w) if mask is None else (mask | (rows == w))
    return mask


def pick(rows, pairs, other=0.0):
    out = other
    for wanted, value in pairs:
        if wanted:
            out = jnp.where(one_of(rows, wanted), value, out)
    return out


def selectors(shape):
    rows = rows_iota(shape)
    out = []
    for which, top in ((0, 3), (1, 3), (2, 2)):
        for n in range(top + 1):
            wanted = [j for j, t in enumerate(TERMS) if t[which] == n]
            out.append(jnp.where(one_of(rows, wanted), 1.0, 0.0) + jnp.zeros(shape, F32))
    return out


def monomials(u, v, w, sel):
    u2, v2 = u * u, v * v
    p = sel[0] + sel[1] * u + sel[2] * u2 + sel[3] * (u2 * u)
    q = sel[4] + sel[5] * v + sel[6] * v2 + sel[7] * (v2 * v)
    return p * q * (sel[8] + sel[9] * w + sel[10] * (w * w))


def channel_factors(k_mid, lanes):
    shape = (ROWS, lanes)
    rows = rows_iota(shape)
    consts = []
    for j, (a, b, e) in enumerate(TERMS):
        n = a + b
        sign = -1.0 if (n // 2) % 2 else 1.0
        consts.append(([j], sign * TWO_PI**n / (math.factorial(a) * math.factorial(b) * math.factorial(e))))
    base = pick(rows, consts) + jnp.zeros(shape, F32)
    out = []
    for f in range(CHANS):
        delta = (f - 0.5 * (CHANS - 1)) * DK
        kappa = (-ENV_COEF * delta) * (2.0 * k_mid + delta)
        phase = pick(
            rows,
            [([j for j, t in enumerate(TERMS) if t[0] + t[1] == n], delta**n) for n in range(1, 4)],
            1.0,
        )
        env = jnp.where(
            one_of(rows, [j for j, t in enumerate(TERMS) if t[2] == 1]),
            kappa,
            jnp.where(one_of(rows, [j for j, t in enumerate(TERMS) if t[2] == 2]), kappa * kappa, 1.0),
        )
        out.append(base * phase * env)
    return out


def split2(x):
    wide = x * 65537.0
    high = wide - (wide - x)
    return high.astype(BF16), (x - high).astype(BF16)


def split3(x):
    high = x.astype(BF16)
    rest = x - high.astype(F32)
    mid = rest.astype(BF16)
    return high, mid, (rest - mid.astype(F32)).astype(BF16)


def kernel(
    obs_h, wts_h, pairs_h, pos_h, cen_h, asg_h, amp_h, off_h, wid_h, blk_h,
    comp_o, centre_o, res_o,
    obs_v, wts_v, pairs_v, pos_v, cen_v, asg_v, amp_v, off_v, wid_v, blk_s, row_s,
    sibling, table, comp, lcol, mcol, wcol, ep_a, ep_b, ep_c, ep_d, part, recv_a, recv_b, resid, gs_v, sel_v, hot_v, y_v, pairs_x, obs_x, wts_x, extra,
    in_sem, row_sem, sib_s, sib_r, gat_s, gat_r, cmp_s, cmp_r, res_s, res_r, x_s, x_r, a_s, a_r, b_s, b_r,
):
    me = here()
    x_me, y_me, z_me, core_me = me
    src = lax.axis_index("src")
    z_low = lax.rem(z_me, 4)
    half = src * 256
    here0, here1 = device(me, (0, 0, 0), 0), device(me, (0, 0, 0), 1)
    is0, is1 = core_me == 0, core_me == 1
    late0 = is0 & (src == 1)
    early0 = is0 & (src == 0)
    early1 = is1 & (src == 0)
    at_end = (z_low == 0) | (z_low == 3)
    barrier = pltpu.get_barrier_semaphore()
    pl.semaphore_signal(barrier, 1, device_id=jnp.where(is0, here1, here0), device_id_type=LOGICAL)
    for off in GREET:
        pl.semaphore_signal(barrier, 1, device_id=device(me, off, 1), device_id_type=LOGICAL)

    halves = pl.ds(pl.multiple_of(half, 256), 256)
    loads = [
        pltpu.make_async_copy(a, b, in_sem.at[i])
        for i, (a, b) in enumerate(
            [
                (pos_h, pos_v), (cen_h, cen_v), (asg_h, asg_v), (amp_h, amp_v), (off_h, off_v), (wid_h, wid_v),
                (pairs_h.at[:, halves], pairs_v), (obs_h.at[:, :, halves], obs_v), (wts_h.at[:, halves], wts_v), (blk_h, blk_s),
            ]
        )
    ]
    for load in loads:
        load.start()

    def hand_over():
        third = slice(256, 384)
        return [
            send(pairs_h.at[:, third], pairs_x, x_s.at[0], x_r.at[0], here1),
            send(obs_h.at[:, :, third], obs_x, x_s.at[1], x_r.at[1], here1),
            send(wts_h.at[:, third], wts_x, x_s.at[2], x_r.at[2], here1),
        ]

    loads[0].wait()
    gap = jnp.zeros((1, 16), F32)
    xs, ys = pos_v[0:1, :], pos_v[1:2, :]
    tail = jnp.zeros((1, 64), F32)

    @pl.when(is0)
    def _():
        sibling[...] = jnp.concatenate([xs, gap, ys, gap, tail], axis=1)
        pl.semaphore_wait(barrier, 1)
        send(sibling, table.at[0], sib_s, sib_r, here1).start()

        @pl.when(early0)
        def _():
            for move in hand_over():
                move.start()

    @pl.when(is1)
    def _():
        sibling[...] = jnp.concatenate([gap, xs, gap, ys, tail], axis=1)

    for load in loads[1:6]:
        load.wait()
    assign = asg_v[...]
    onehot = (jnp.broadcast_to(assign, (32, 256)) == rows_iota((32, 256))).astype(BF16)
    cen_parts = split3(cen_v[...])
    centre = sum(jnp.dot(p, onehot, preferred_element_type=F32) for p in cen_parts)
    lm = centre + off_v[...]
    width = wid_v[...]
    rows8 = rows_iota((8, 256))
    comp[src] = pick(
        rows8,
        [
            ([0], lm[0:1, :]), ([1], lm[1:2, :]), ([2], width * width), ([3], amp_v[...]), ([4], width),
            ([5], assign.astype(F32)),
        ],
    )

    @pl.when(is1)
    def _():
        drain(table.at[0], sib_r)
        table[0] = table[0] + sibling[...]
        to_scalar = pltpu.make_async_copy(table.at[0], row_s, row_sem)
        to_scalar.start()
        to_scalar.wait()
        pl.semaphore_wait(barrier, 2 * len(GREET) + 1)

        def positions(chips):
            for off in chips:
                for core in (0, 1):
                    send(row_s, table.at[slot_of(off)], gat_s.at[core], gat_r, device(me, off, core)).start()

        positions(GATHER[:5])

        @pl.when(at_end)
        def _():
            for step in (1, 2):
                far = lax.rem(z_me + jnp.where(z_low == 0, 8 - step, step), 8)
                for core in (0, 1):
                    to = lax.div(far, 4) * 128 + (x_me * 8 + lax.rem(far, 4) * 2 + core) * 4 + y_me
                    send(comp.at[src], comp.at[src], cmp_s.at[core], cmp_r, to).start()

        positions(GATHER[5:])
        send(row_s, table.at[0], gat_s.at[0], gat_r, here0).start()

    loads[6].wait()
    loads[9].wait()
    first = blk_s[0] * BLOCK_CHANNELS + lax.axis_index("ch") * CHANS
    k_mid = (NU_ZERO + (first.astype(F32) + 0.5 * (CHANS - 1)) * NU_STEP) / NU_REF
    ks = [(NU_ZERO + (first + f).astype(F32) * NU_STEP) / NU_REF for f in range(CHANS)]
    for f, factor in enumerate(channel_factors(k_mid, 128)):
        gs_v[f] = factor
    choose = selectors((ROWS, 128))
    for n, one in enumerate(choose):
        sel_v[n] = one
    sel_v[11] = jnp.where(one_of(rows_iota((ROWS, 128)), ODD), 1.0, 0.0)

    def places(ant):
        chip = lax.shift_right_logical(ant, 5)
        return ((x_me - lax.shift_right_logical(chip, 2)) & 3) * 4 + ((z_low - chip) & 3), ant & 31

    slot, inner = places(pairs_v[...])
    rows16 = rows_iota((16, 128))

    drain(comp.at[0], cmp_r)
    both = jnp.concatenate([comp[0], comp[1]], axis=1)
    l_row, m_row, w2_row = both[0:1, :], both[1:2, :], both[2:3, :]
    amp_row, w_row = both[3:4, :], both[4:5, :]
    mono = monomials(l_row, m_row, w2_row, [jnp.concatenate([one] * 4, axis=1) for one in choose])
    amp_high, amp_low = split2(mono * amp_row)
    mono_amp = jnp.concatenate([amp_high.astype(F32), amp_low.astype(F32)], axis=0).astype(BF16)
    rows128 = rows_iota((128, 512))
    source = jnp.broadcast_to(both[5:6, :], (128, 512))
    hot_v[...] = ((source == (rows128 & 31).astype(F32)) & (rows128 < 64)).astype(BF16)
    cols = jnp.transpose(both)
    lcol[...] = jnp.broadcast_to(cols[:, 0:1], (512, 128))
    mcol[...] = jnp.broadcast_to(cols[:, 1:2], (512, 128))
    wcol[...] = jnp.broadcast_to(cols[:, 2:3], (512, 128))

    @pl.when(is0)
    def _():
        drain(table, gat_r)

    @pl.when(is1)
    def _():
        drain(table.at[pl.ds(1, 15)], gat_r)

    sites = table[:, 0, :]

    def offsets(slot, inner):
        got = []
        for shift in (0, 32):
            total = 0.0
            for a in range(2):
                idx = jnp.broadcast_to(inner[a : a + 1, :] + shift, (16, 128))
                val = jnp.take_along_axis(sites, idx, axis=1, mode="promise_in_bounds")
                val = jnp.where(jnp.broadcast_to(slot[a : a + 1, :], (16, 128)) == rows16, val, 0.0)
                total = total + val if a == 0 else total - val
            got.append(jnp.sum(total, axis=0, keepdims=True))
        return got[0], got[1]

    loads[7].wait()
    loads[8].wait()
    odd = sel_v[11] > 0.5
    gs = [gs_v[f] for f in range(CHANS)]
    sel = [sel_v[n] for n in range(11)]

    eps = (ep_a, ep_b, ep_c, ep_d)

    def terms(t, h, kx, ky, er):
        for i in range(16 * h, 16 * h + 16):
            rows = slice(16 * i, 16 * i + 16)
            lc, mc, wc = lcol[rows, :], mcol[rows, :], wcol[rows, :]
            turns = lc * kx + mc * ky
            env = jnp.exp(wc * er)
            r = turns - ((turns + ROUNDER) - ROUNDER)
            y = r * r
            s = SIN_COEFS[-1]
            for coef in SIN_COEFS[-2::-1]:
                s = s * y + coef
            s = s * r
            c = COS_COEFS[-1]
            for coef in COS_COEFS[-2::-1]:
                c = c * y + coef
            here_ep = eps[2 * t + i // 16]
            inner_rows = slice(16 * (i % 16), 16 * (i % 16) + 16)
            es = env * s
            high, low = split2(env - es * s)
            here_ep[inner_rows, 0:128] = high
            here_ep[inner_rows, 256:384] = low
            high, low = split2(es * c)
            here_ep[inner_rows, 128:256] = high
            here_ep[inner_rows, 384:512] = low

    def moments(t, h):
        part_c = slice(256 * h, 256 * h + 256)
        here_ep = eps[2 * t + h]
        high = jnp.dot(mono_amp[:, part_c], here_ep[:, 0:256], preferred_element_type=F32)
        low = jnp.dot(amp_high[:, part_c], here_ep[:, 256:512], preferred_element_type=F32)
        return high[0:ROWS] + high[ROWS:] + low

    def misfit(n, m_all, obs, wts, dx, dy, r2):
        m_r, m_i = m_all[:, 0:128], m_all[:, 128:256]
        base = monomials(dx, dy, r2, sel)
        n_r = base * jnp.where(odd, m_i, m_r)
        n_i = base * jnp.where(odd, -m_r, m_i)
        zero = jnp.zeros((ROWS, 128), F32)
        a0, d0, a1, d1, a2, d2 = zero, zero, zero, zero, zero, zero
        found = jnp.zeros((8, 128), F32)
        rows8 = rows_iota((8, 128))
        for f in range(CHANS):
            v_r = jnp.sum(gs[f] * n_r, axis=0, keepdims=True)
            v_i = jnp.sum(gs[f] * n_i, axis=0, keepdims=True)
            rr = obs[0, f : f + 1, :] - v_r
            ri = obs[1, f : f + 1, :] - v_i
            found = jnp.where(rows8 == f, rr, jnp.where(rows8 == CHANS + f, ri, found))
            wr = wts[f : f + 1, :] * rr
            wi = wts[f : f + 1, :] * ri
            k = ks[f]
            a0 += gs[f] * wr
            d0 += gs[f] * wi
            a1 += gs[f] * (k * wr)
            d1 += gs[f] * (k * wi)
            a2 += gs[f] * (k * k * wr)
            d2 += gs[f] * (k * k * wi)
        (extra if n is None else resid.at[n])[...] = found

        def sides(a, d):
            return jnp.where(odd, -d, a) * base, jnp.where(odd, a, d) * base

        c0, s0 = sides(a0, d0)
        c1, s1 = sides(a1, d1)
        c2, s2 = sides(a2, d2)
        left_r = jnp.concatenate([c0, c2 * r2, -s1 * dx, -s1 * dy], axis=0)
        left_i = jnp.concatenate([s0, s2 * r2, c1 * dx, c1 * dy], axis=0)
        high, low = split2(jnp.concatenate([left_r, left_i], axis=1))
        return high, jnp.concatenate([high, low], axis=0)

    def adjoint(t, left_high, left_both):
        out = []
        for h in range(2):
            here_ep = eps[2 * t + h]
            high = lax.dot_general(left_both, here_ep[:, 0:256], NT, preferred_element_type=F32)
            low = lax.dot_general(left_high, here_ep[:, 256:512], NT, preferred_element_type=F32)
            out.append(high[0 : 4 * ROWS] + high[4 * ROWS :] + low)
        return jnp.concatenate(out, axis=1)

    def tile(n, t, slot, inner, obs, wts):
        dx, dy = offsets(slot, inner)
        r2 = dx * dx + dy * dy
        scales = k_mid * dx, k_mid * dy, (-ENV_COEF * (k_mid * k_mid)) * r2
        terms(t, 0, *scales)
        m_all = moments(t, 0)
        terms(t, 1, *scales)
        m_all += moments(t, 1)
        return adjoint(t, *misfit(n, m_all, obs, wts, dx, dy, r2))

    partner = jnp.where(is0, device(me, PARTNER, 0), device(me, PARTNER, 1))

    def pass_on(n, t):
        return send(resid.at[n], resid.at[n], res_s.at[t], res_r.at[t], partner)

    far, near = slice(128, 256), slice(0, 128)
    y_v[...] = tile(2 * src + 1, 1, slot[:, far], inner[:, far], obs_v[:, :, far], wts_v[:, far])
    pass_on(2 * src + 1, 1).start()

    @pl.when(jnp.logical_not(late0))
    def _():
        y_v[...] += tile(2 * src, 0, slot[:, near], inner[:, near], obs_v[:, :, near], wts_v[:, near])
        pass_on(2 * src, 0).start()

    def spread():
        return [
            send(extra, resid.at[2], x_s.at[3], x_r.at[3], here0),
            send(extra, resid.at[2], x_s.at[4], x_r.at[3], device(me, PARTNER, 0)),
        ]

    @pl.when(early1)
    def _():
        for n, ref in enumerate((pairs_x, obs_x, wts_x)):
            drain(ref, x_r.at[n])
        y_v[...] += tile(None, 0, *places(pairs_x[...]), obs_x, wts_x)
        for move in spread():
            move.start()

    y_all = y_v[...]
    sums = [jnp.sum(y_all[q * ROWS : (q + 1) * ROWS] * mono, axis=0, keepdims=True) for q in range(4)]
    norm = 1.0 / math.sqrt(16384 * BLOCK_CHANNELS)
    grads = [
        -norm * sums[0],
        (-norm * TWO_PI) * amp_row * sums[2],
        (-norm * TWO_PI) * amp_row * sums[3],
        (norm * 2.0 * TWO_PI * math.pi) * amp_row * w_row * sums[1],
    ]

    rows8w = rows_iota((8, 512))
    pair = jnp.where(rows8w < 2, grads[1], grads[2])
    high = pair * 65537.0
    high = high - (high - pair)
    left = jnp.where((rows8w & 1) == 0, high, pair - high).astype(BF16)
    wide = lax.dot_general(left, hot_v[...], NT, preferred_element_type=F32)
    lanes1 = lax.broadcasted_iota(jnp.int32, (8, 128), 1)
    rows8n = rows_iota((8, 128))
    mine = (rows8n < 4) & (lax.shift_right_logical(rows8n, 1) == lax.shift_right_logical(lanes1, 5))
    cen_rows = jnp.sum(jnp.where(mine, wide, 0.0), axis=0, keepdims=True)
    for s in range(2):
        rows = rows_iota((8, 128))
        block = 0.0
        for h in range(2):
            lo = 256 * s + 128 * h
            for q in range(4):
                block = jnp.where(rows == 4 * h + q, grads[q][:, lo : lo + 128], block)
        part[s, 0:8, :] = block
        part[s, 8:9, :] = cen_rows

    def column(core):
        for i, off in enumerate(COLUMN):
            to = lax.div(lax.rem(z_me + (off[2] + 8), 8), 4)
            send(part.at[to], recv_a.at[2 * i + core], a_s, a_r, device(me, off, 1)).start()

    @pl.when(is0)
    def _():
        column(0)
        send(part.at[src], recv_a.at[14], a_s, a_r, here1).start()

    @pl.when(is1)
    def _():
        column(1)
        drain(recv_a, a_r)
        total = part[src]
        for i in range(15):
            total = total + recv_a[i]
        recv_b[0] = total
        for core in (1, 0):
            for i, off in enumerate(PLANE):
                send(recv_b.at[0], recv_b.at[i + 1], b_s.at[core], b_r, device(me, off, core)).start()
        send(recv_b.at[0], recv_b.at[0], b_s.at[0], b_r, here0).start()

    drain(resid.at[0], res_r.at[1])

    @pl.when(jnp.logical_not(early0))
    def _():
        drain(resid.at[0], res_r.at[0])

    @pl.when(is0)
    def _():
        drain(extra, x_r.at[3])

    for n in range(4):
        res_o[0, :, 128 * n : 128 * n + 128] = resid[n, 0:4, :]
        res_o[1, :, 128 * n : 128 * n + 128] = resid[n, 4:8, :]

    @pl.when(is0)
    def _():
        drain(recv_b, b_r)

    @pl.when(is1)
    def _():
        drain(recv_b.at[pl.ds(1, 15)], b_r)

    total = recv_b[0]
    for i in range(1, 16):
        total = total + recv_b[i]
    comp_o[:, 0:128] = total[0:4, :]
    comp_o[:, 128:256] = total[4:8, :]
    centre_o[0:1, :] = total[8:9, 0:32]
    centre_o[1:2, :] = total[8:9, 32:64]

    drain(resid.at[0], res_s.at[1])

    @pl.when(jnp.logical_not(late0))
    def _():
        drain(resid.at[0], res_s.at[0])

    @pl.when(early0)
    def _():
        for move in hand_over():
            move.wait_send()

    @pl.when(early1)
    def _():
        for move in spread():
            move.wait_send()

    @pl.when(is0)
    def _():
        drain(sibling, sib_s)
        drain(recv_a.at[pl.ds(0, 8)], a_s)

    @pl.when(is1)
    def _():
        @pl.when(at_end)
        def _():
            for core in (0, 1):
                drain(comp, cmp_s.at[core])

        drain(table, gat_s.at[0])
        drain(table.at[pl.ds(1, 15)], gat_s.at[1])
        drain(recv_a.at[pl.ds(0, 7)], a_s)
        drain(recv_b, b_s.at[0])
        drain(recv_b.at[pl.ds(1, 15)], b_s.at[1])


def deliver(*refs):
    sem = refs[6]
    moves = [pltpu.make_async_copy(refs[i], refs[3 + i], sem.at[i]) for i in range(3)]
    for move in moves:
        move.start()
    for move in moves:
        move.wait()


def on_device(observed, weights, pairs, positions, centres, assign, amplitude, offsets, widths, block_index):
    dma = pltpu.SemaphoreType.DMA
    operands = [
        pltpu.with_memory_space_constraint(v, pltpu.HBM)
        for v in (
            observed, weights, pairs, positions.T, centres, assign.reshape(1, 256), amplitude.reshape(1, 256), offsets,
            widths.reshape(1, 256),
        )
    ]
    sums = pl.pallas_call(
        kernel,
        out_shape=(
            jax.ShapeDtypeStruct((4, 256), F32),
            jax.ShapeDtypeStruct((2, 32), F32),
            jax.ShapeDtypeStruct((2, 4, 512), F32),
        ),
        in_specs=[pl.BlockSpec(memory_space=pltpu.HBM)] * 9 + [pl.BlockSpec(memory_space=pl.ANY)],
        out_specs=tuple([pl.BlockSpec(memory_space=pltpu.VMEM)] * 3),
        scratch_shapes=[
            pltpu.VMEM((2, 4, 256), F32),
            pltpu.VMEM((4, 256), F32),
            pltpu.VMEM((2, 256), jnp.int32),
            pltpu.VMEM((2, 16), F32),
            pltpu.VMEM((2, 32), F32),
            pltpu.VMEM((1, 256), jnp.int32),
            pltpu.VMEM((1, 256), F32),
            pltpu.VMEM((2, 256), F32),
            pltpu.VMEM((1, 256), F32),
            pltpu.SMEM((1,), jnp.int32),
            pltpu.SMEM((1, 128), F32),
            pltpu.VMEM((1, 128), F32),
            pltpu.VMEM((16, 1, 128), F32),
            pltpu.VMEM((2, 8, 256), F32),
            pltpu.VMEM((512, 128), F32),
            pltpu.VMEM((512, 128), F32),
            pltpu.VMEM((512, 128), F32),
            pltpu.VMEM((256, 512), BF16),
            pltpu.VMEM((256, 512), BF16),
            pltpu.VMEM((256, 512), BF16),
            pltpu.VMEM((256, 512), BF16),
            pltpu.VMEM((2, 9, 128), F32),
            pltpu.VMEM((15, 9, 128), F32),
            pltpu.VMEM((16, 9, 128), F32),
            pltpu.VMEM((4, 8, 128), F32),
            pltpu.VMEM((4, ROWS, 128), F32),
            pltpu.VMEM((12, ROWS, 128), F32),
            pltpu.VMEM((128, 512), BF16),
            pltpu.VMEM((4 * ROWS, 512), F32),
            pltpu.VMEM((2, 128), jnp.int32),
            pltpu.VMEM((2, 4, 128), F32),
            pltpu.VMEM((4, 128), F32),
            pltpu.VMEM((8, 128), F32),
            dma((10,)), dma(()), dma(()), dma(()), dma((2,)), dma(()), dma((2,)), dma(()), dma((2,)), dma((2,)), dma((5,)), dma((4,)), dma(()), dma(()),
            dma((2,)), dma(()),
        ],
        compiler_params=pltpu.CompilerParams(
            collective_id=0, has_side_effects=True, vmem_limit_bytes=32 * 1024 * 1024
        ),
        name="refit",
    )(*operands, block_index)
    return pl.pallas_call(
        deliver,
        out_shape=tuple(jax.ShapeDtypeStruct(v.shape, F32) for v in sums),
        in_specs=[pl.BlockSpec(memory_space=pltpu.VMEM)] * 3,
        out_specs=tuple([pl.BlockSpec(memory_space=pltpu.HBM)] * 3),
        scratch_shapes=[dma((3,))],
        name="deliver",
    )(*(pltpu.with_memory_space_constraint(v, pltpu.VMEM) for v in sums))


def solution(mesh):
    placed = (
        P(None, "ch", "bl"),
        P("ch", "bl"),
        P(None, "bl"),
        P("bl", None),
        P(),
        P("src"),
        P("src"),
        P(None, "src"),
        P("src"),
        P(),
    )
    return jax.shard_map(
        on_device,
        mesh=mesh,
        in_specs=placed,
        out_specs=(P(None, "src"), P(), P(None, "ch", "bl")),
        check_vma=False,
    )
```

```python
import functools
import math

import jax
import jax.numpy as jnp
from jax import lax
from jax.experimental import pallas as pl
from jax.experimental.pallas import tpu as pltpu
from jax.sharding import PartitionSpec as P

F32 = jnp.float32
BF16 = jnp.bfloat16
LOGICAL = pl.DeviceIdType.LOGICAL
BLOCK_CHANNELS = 16
NU_ZERO = 50000000.0
NU_STEP = 36621.09375
NU_REF = 100000000.0
DK = NU_STEP / NU_REF
CHANS = 4
TWO_PI = 2.0 * math.pi
ENV_COEF = 2.0 * math.pi * math.pi

SIN_COEFS = (4.44288283, -7.30824115, 3.60628896, -0.8457636, 0.10920575)
COS_COEFS = (-1.4142135, 6.97885099, -5.73946117, 1.88356299, -0.31069819)

ROUNDER = 12582912.0
NT = (((1,), (1,)), ((), ()))

TERMS = (
    [(a, n - a, 0) for n in range(4) for a in range(n, -1, -1)]
    + [(a, n - a, 1) for n in range(3) for a in range(n, -1, -1)]
    + [(a, n - a, 2) for n in range(2) for a in range(n, -1, -1)]
)
ROWS = 24
ODD = [j for j, t in enumerate(TERMS) if (t[0] + t[1]) % 2]

STEPS = (2, 1, -1, 0)
Z_STEPS = (-2, 1, -1, 0)


def far_first(offs):
    return sorted((o for o in offs if o != (0, 0, 0)), key=lambda o: (sum(map(abs, o)), o), reverse=True)


GATHER = far_first([(dx, 0, dz) for dx in STEPS for dz in Z_STEPS])
COLUMN = far_first([(0, 0, dz) for dz in (4, 3, 2, 1, 0, -1, -2, -3)])
PLANE = far_first([(dx, dy, 0) for dx in STEPS for dy in STEPS])
PARTNER = (0, 0, 4)
GREET = far_first(
    {((-dx + 1) % 4 - 1, (-dy + 1) % 4 - 1, (-dz + 3) % 8 - 3) for dx, dy, dz in GATHER + COLUMN + PLANE}
)


def here():
    bl = lax.axis_index("bl")
    src = lax.axis_index("src")
    return lax.div(bl, 8), lax.axis_index("ch"), src * 4 + lax.rem(lax.div(bl, 2), 4), lax.rem(bl, 2)


def device(me, off, core):
    x, y, z, _ = me
    dx, dy, dz = off
    x = lax.rem(x + (dx + 4), 4) if dx else x
    y = lax.rem(y + (dy + 4), 4) if dy else y
    z = lax.rem(z + (dz + 8), 8) if dz else z
    return lax.div(z, 4) * 128 + (x * 8 + lax.rem(z, 4) * 2 + core) * 4 + y


def slot_of(off):
    return (off[0] % 4) * 4 + off[2] % 4


def send(src_ref, dst_ref, send_sem, recv_sem, to):
    return pltpu.make_async_remote_copy(
        src_ref=src_ref, dst_ref=dst_ref, send_sem=send_sem, recv_sem=recv_sem, device_id=to, device_id_type=LOGICAL
    )


def drain(ref, sem):
    pltpu.make_async_copy(ref, ref, sem).wait()


def rows_iota(shape):
    return lax.broadcasted_iota(jnp.int32, shape, 0)


def one_of(rows, wanted):
    mask = None
    for w in wanted:
        mask = (rows == w) if mask is None else (mask | (rows == w))
    return mask


def pick(rows, pairs, other=0.0):
    out = other
    for wanted, value in pairs:
        if wanted:
            out = jnp.where(one_of(rows, wanted), value, out)
    return out


def selectors(shape):
    rows = rows_iota(shape)
    out = []
    for which, top in ((0, 3), (1, 3), (2, 2)):
        for n in range(top + 1):
            wanted = [j for j, t in enumerate(TERMS) if t[which] == n]
            out.append(jnp.where(one_of(rows, wanted), 1.0, 0.0) + jnp.zeros(shape, F32))
    return out


def monomials(u, v, w, sel):
    u2, v2 = u * u, v * v
    p = sel[0] + sel[1] * u + sel[2] * u2 + sel[3] * (u2 * u)
    q = sel[4] + sel[5] * v + sel[6] * v2 + sel[7] * (v2 * v)
    return p * q * (sel[8] + sel[9] * w + sel[10] * (w * w))


def channel_factors(k_mid, lanes):
    shape = (ROWS, lanes)
    rows = rows_iota(shape)
    consts = []
    for j, (a, b, e) in enumerate(TERMS):
        n = a + b
        sign = -1.0 if (n // 2) % 2 else 1.0
        consts.append(([j], sign * TWO_PI**n / (math.factorial(a) * math.factorial(b) * math.factorial(e))))
    base = pick(rows, consts) + jnp.zeros(shape, F32)
    out = []
    for f in range(CHANS):
        delta = (f - 0.5 * (CHANS - 1)) * DK
        kappa = (-ENV_COEF * delta) * (2.0 * k_mid + delta)
        phase = pick(
            rows,
            [([j for j, t in enumerate(TERMS) if t[0] + t[1] == n], delta**n) for n in range(1, 4)],
            1.0,
        )
        env = jnp.where(
            one_of(rows, [j for j, t in enumerate(TERMS) if t[2] == 1]),
            kappa,
            jnp.where(one_of(rows, [j for j, t in enumerate(TERMS) if t[2] == 2]), kappa * kappa, 1.0),
        )
        out.append(base * phase * env)
    return out


def split2(x):
    wide = x * 65537.0
    high = wide - (wide - x)
    return high.astype(BF16), (x - high).astype(BF16)


def split3(x):
    high = x.astype(BF16)
    rest = x - high.astype(F32)
    mid = rest.astype(BF16)
    return high, mid, (rest - mid.astype(F32)).astype(BF16)


def kernel(
    obs_h, wts_h, pairs_h, pos_h, cen_h, asg_h, amp_h, off_h, wid_h, blk_h,
    comp_o, centre_o, res_o,
    obs_v, wts_v, pairs_v, pos_v, cen_v, asg_v, amp_v, off_v, wid_v, blk_s, row_s,
    sibling, table, comp, lcol, mcol, wcol, ep_a, ep_b, ep_c, ep_d, part, recv_a, recv_b, resid, gs_v, sel_v, hot_v, y_v, pairs_x, obs_x, wts_x, extra,
    in_sem, row_sem, sib_s, sib_r, gat_s, gat_r, cmp_s, cmp_r, res_s, res_r, x_s, x_r, a_s, a_r, b_s, b_r,
):
    me = here()
    x_me, y_me, z_me, core_me = me
    src = lax.axis_index("src")
    z_low = lax.rem(z_me, 4)
    half = src * 256
    here0, here1 = device(me, (0, 0, 0), 0), device(me, (0, 0, 0), 1)
    is0, is1 = core_me == 0, core_me == 1
    late0 = is0 & (src == 1)
    early0 = is0 & (src == 0)
    early1 = is1 & (src == 0)
    at_end = (z_low == 0) | (z_low == 3)
    barrier = pltpu.get_barrier_semaphore()
    pl.semaphore_signal(barrier, 1, device_id=jnp.where(is0, here1, here0), device_id_type=LOGICAL)
    for off in GREET:
        pl.semaphore_signal(barrier, 1, device_id=device(me, off, 1), device_id_type=LOGICAL)

    halves = pl.ds(pl.multiple_of(half, 256), 256)
    loads = [
        pltpu.make_async_copy(a, b, in_sem.at[i])
        for i, (a, b) in enumerate(
            [
                (pos_h, pos_v), (cen_h, cen_v), (asg_h, asg_v), (amp_h, amp_v), (off_h, off_v), (wid_h, wid_v),
                (pairs_h.at[:, halves], pairs_v), (obs_h.at[:, :, halves], obs_v), (wts_h.at[:, halves], wts_v), (blk_h, blk_s),
            ]
        )
    ]
    for load in loads:
        load.start()

    def hand_over():
        third = slice(256, 384)
        return [
            send(pairs_h.at[:, third], pairs_x, x_s.at[0], x_r.at[0], here1),
            send(obs_h.at[:, :, third], obs_x, x_s.at[1], x_r.at[1], here1),
            send(wts_h.at[:, third], wts_x, x_s.at[2], x_r.at[2], here1),
        ]

    loads[0].wait()
    gap = jnp.zeros((1, 16), F32)
    xs, ys = pos_v[0:1, :], pos_v[1:2, :]
    tail = jnp.zeros((1, 64), F32)

    @pl.when(is0)
    def _():
        sibling[...] = jnp.concatenate([xs, gap, ys, gap, tail], axis=1)
        pl.semaphore_wait(barrier, 1)
        send(sibling, table.at[0], sib_s, sib_r, here1).start()

        @pl.when(early0)
        def _():
            for move in hand_over():
                move.start()

    @pl.when(is1)
    def _():
        sibling[...] = jnp.concatenate([gap, xs, gap, ys, tail], axis=1)

    for load in loads[1:6]:
        load.wait()
    assign = asg_v[...]
    onehot = (jnp.broadcast_to(assign, (32, 256)) == rows_iota((32, 256))).astype(BF16)
    cen_parts = split3(cen_v[...])
    centre = sum(jnp.dot(p, onehot, preferred_element_type=F32) for p in cen_parts)
    lm = centre + off_v[...]
    width = wid_v[...]
    rows8 = rows_iota((8, 256))
    comp[src] = pick(
        rows8,
        [
            ([0], lm[0:1, :]), ([1], lm[1:2, :]), ([2], width * width), ([3], amp_v[...]), ([4], width),
            ([5], assign.astype(F32)),
        ],
    )

    @pl.when(is1)
    def _():
        drain(table.at[0], sib_r)
        table[0] = table[0] + sibling[...]
        to_scalar = pltpu.make_async_copy(table.at[0], row_s, row_sem)
        to_scalar.start()
        to_scalar.wait()
        pl.semaphore_wait(barrier, 2 * len(GREET) + 1)

        def positions(chips):
            for off in chips:
                for core in (0, 1):
                    send(row_s, table.at[slot_of(off)], gat_s.at[core], gat_r, device(me, off, core)).start()

        positions(GATHER[:5])

        @pl.when(at_end)
        def _():
            for step in (1, 2):
                far = lax.rem(z_me + jnp.where(z_low == 0, 8 - step, step), 8)
                for core in (0, 1):
                    to = lax.div(far, 4) * 128 + (x_me * 8 + lax.rem(far, 4) * 2 + core) * 4 + y_me
                    send(comp.at[src], comp.at[src], cmp_s.at[core], cmp_r, to).start()

        positions(GATHER[5:])
        send(row_s, table.at[0], gat_s.at[0], gat_r, here0).start()

    loads[6].wait()
    loads[9].wait()
    first = blk_s[0] * BLOCK_CHANNELS + lax.axis_index("ch") * CHANS
    k_mid = (NU_ZERO + (first.astype(F32) + 0.5 * (CHANS - 1)) * NU_STEP) / NU_REF
    ks = [(NU_ZERO + (first + f).astype(F32) * NU_STEP) / NU_REF for f in range(CHANS)]
    for f, factor in enumerate(channel_factors(k_mid, 128)):
        gs_v[f] = factor
    choose = selectors((ROWS, 128))
    for n, one in enumerate(choose):
        sel_v[n] = one
    sel_v[11] = jnp.where(one_of(rows_iota((ROWS, 128)), ODD), 1.0, 0.0)

    def places(ant):
        chip = lax.shift_right_logical(ant, 5)
        return ((x_me - lax.shift_right_logical(chip, 2)) & 3) * 4 + ((z_low - chip) & 3), ant & 31

    slot, inner = places(pairs_v[...])
    rows16 = rows_iota((16, 128))

    drain(comp.at[0], cmp_r)
    both = jnp.concatenate([comp[0], comp[1]], axis=1)
    l_row, m_row, w2_row = both[0:1, :], both[1:2, :], both[2:3, :]
    amp_row, w_row = both[3:4, :], both[4:5, :]
    mono = monomials(l_row, m_row, w2_row, [jnp.concatenate([one] * 4, axis=1) for one in choose])
    amp_high, amp_low = split2(mono * amp_row)
    mono_amp = jnp.concatenate([amp_high.astype(F32), amp_low.astype(F32)], axis=0).astype(BF16)
    rows128 = rows_iota((128, 512))
    source = jnp.broadcast_to(both[5:6, :], (128, 512))
    hot_v[...] = ((source == (rows128 & 31).astype(F32)) & (rows128 < 64)).astype(BF16)
    cols = jnp.transpose(both)
    lcol[...] = jnp.broadcast_to(cols[:, 0:1], (512, 128))
    mcol[...] = jnp.broadcast_to(cols[:, 1:2], (512, 128))
    wcol[...] = jnp.broadcast_to(cols[:, 2:3], (512, 128))

    @pl.when(is0)
    def _():
        drain(table, gat_r)

    @pl.when(is1)
    def _():
        drain(table.at[pl.ds(1, 15)], gat_r)

    sites = table[:, 0, :]

    def offsets(slot, inner):
        got = []
        for shift in (0, 32):
            total = 0.0
            for a in range(2):
                idx = jnp.broadcast_to(inner[a : a + 1, :] + shift, (16, 128))
                val = jnp.take_along_axis(sites, idx, axis=1, mode="promise_in_bounds")
                val = jnp.where(jnp.broadcast_to(slot[a : a + 1, :], (16, 128)) == rows16, val, 0.0)
                total = total + val if a == 0 else total - val
            got.append(jnp.sum(total, axis=0, keepdims=True))
        return got[0], got[1]

    loads[7].wait()
    loads[8].wait()
    odd = sel_v[11] > 0.5
    gs = [gs_v[f] for f in range(CHANS)]
    sel = [sel_v[n] for n in range(11)]

    eps = (ep_a, ep_b, ep_c, ep_d)

    def terms(t, h, kx, ky, er):
        for i in range(16 * h, 16 * h + 16):
            rows = slice(16 * i, 16 * i + 16)
            lc, mc, wc = lcol[rows, :], mcol[rows, :], wcol[rows, :]
            turns = lc * kx + mc * ky
            env = jnp.exp(wc * er)
            r = turns - ((turns + ROUNDER) - ROUNDER)
            y = r * r
            s = SIN_COEFS[-1]
            for coef in SIN_COEFS[-2::-1]:
                s = s * y + coef
            s = s * r
            c = COS_COEFS[-1]
            for coef in COS_COEFS[-2::-1]:
                c = c * y + coef
            here_ep = eps[2 * t + i // 16]
            inner_rows = slice(16 * (i % 16), 16 * (i % 16) + 16)
            es = env * s
            high, low = split2(env - es * s)
            here_ep[inner_rows, 0:128] = high
            here_ep[inner_rows, 256:384] = low
            high, low = split2(es * c)
            here_ep[inner_rows, 128:256] = high
            here_ep[inner_rows, 384:512] = low

    def moments(t, h):
        part_c = slice(256 * h, 256 * h + 256)
        here_ep = eps[2 * t + h]
        high = jnp.dot(mono_amp[:, part_c], here_ep[:, 0:256], preferred_element_type=F32)
        low = jnp.dot(amp_high[:, part_c], here_ep[:, 256:512], preferred_element_type=F32)
        return high[0:ROWS] + high[ROWS:] + low

    def misfit(n, m_all, obs, wts, dx, dy, r2):
        m_r, m_i = m_all[:, 0:128], m_all[:, 128:256]
        base = monomials(dx, dy, r2, sel)
        n_r = base * jnp.where(odd, m_i, m_r)
        n_i = base * jnp.where(odd, -m_r, m_i)
        zero = jnp.zeros((ROWS, 128), F32)
        a0, d0, a1, d1, a2, d2 = zero, zero, zero, zero, zero, zero
        found = jnp.zeros((8, 128), F32)
        rows8 = rows_iota((8, 128))
        for f in range(CHANS):
            v_r = jnp.sum(gs[f] * n_r, axis=0, keepdims=True)
            v_i = jnp.sum(gs[f] * n_i, axis=0, keepdims=True)
            rr = obs[0, f : f + 1, :] - v_r
            ri = obs[1, f : f + 1, :] - v_i
            found = jnp.where(rows8 == f, rr, jnp.where(rows8 == CHANS + f, ri, found))
            wr = wts[f : f + 1, :] * rr
            wi = wts[f : f + 1, :] * ri
            k = ks[f]
            a0 += gs[f] * wr
            d0 += gs[f] * wi
            a1 += gs[f] * (k * wr)
            d1 += gs[f] * (k * wi)
            a2 += gs[f] * (k * k * wr)
            d2 += gs[f] * (k * k * wi)
        (extra if n is None else resid.at[n])[...] = found

        def sides(a, d):
            return jnp.where(odd, -d, a) * base, jnp.where(odd, a, d) * base

        c0, s0 = sides(a0, d0)
        c1, s1 = sides(a1, d1)
        c2, s2 = sides(a2, d2)
        left_r = jnp.concatenate([c0, c2 * r2, -s1 * dx, -s1 * dy], axis=0)
        left_i = jnp.concatenate([s0, s2 * r2, c1 * dx, c1 * dy], axis=0)
        high, low = split2(jnp.concatenate([left_r, left_i], axis=1))
        return high, jnp.concatenate([high, low], axis=0)

    def adjoint(t, left_high, left_both):
        out = []
        for h in range(2):
            here_ep = eps[2 * t + h]
            high = lax.dot_general(left_both, here_ep[:, 0:256], NT, preferred_element_type=F32)
            low = lax.dot_general(left_high, here_ep[:, 256:512], NT, preferred_element_type=F32)
            out.append(high[0 : 4 * ROWS] + high[4 * ROWS :] + low)
        return jnp.concatenate(out, axis=1)

    def tile(n, t, slot, inner, obs, wts):
        dx, dy = offsets(slot, inner)
        r2 = dx * dx + dy * dy
        scales = k_mid * dx, k_mid * dy, (-ENV_COEF * (k_mid * k_mid)) * r2
        terms(t, 0, *scales)
        m_all = moments(t, 0)
        terms(t, 1, *scales)
        m_all += moments(t, 1)
        return adjoint(t, *misfit(n, m_all, obs, wts, dx, dy, r2))

    partner = jnp.where(is0, device(me, PARTNER, 0), device(me, PARTNER, 1))

    def pass_on(n, t):
        return send(resid.at[n], resid.at[n], res_s.at[t], res_r.at[t], partner)

    far, near = slice(128, 256), slice(0, 128)
    y_v[...] = tile(2 * src + 1, 1, slot[:, far], inner[:, far], obs_v[:, :, far], wts_v[:, far])
    pass_on(2 * src + 1, 1).start()

    @pl.when(jnp.logical_not(late0))
    def _():
        y_v[...] += tile(2 * src, 0, slot[:, near], inner[:, near], obs_v[:, :, near], wts_v[:, near])
        pass_on(2 * src, 0).start()

    def spread():
        return [
            send(extra, resid.at[2], x_s.at[3], x_r.at[3], here0),
            send(extra, resid.at[2], x_s.at[4], x_r.at[3], device(me, PARTNER, 0)),
        ]

    @pl.when(early1)
    def _():
        for n, ref in enumerate((pairs_x, obs_x, wts_x)):
            drain(ref, x_r.at[n])
        y_v[...] += tile(None, 0, *places(pairs_x[...]), obs_x, wts_x)
        for move in spread():
            move.start()

    y_all = y_v[...]
    sums = [jnp.sum(y_all[q * ROWS : (q + 1) * ROWS] * mono, axis=0, keepdims=True) for q in range(4)]
    norm = 1.0 / math.sqrt(16384 * BLOCK_CHANNELS)
    grads = [
        -norm * sums[0],
        (-norm * TWO_PI) * amp_row * sums[2],
        (-norm * TWO_PI) * amp_row * sums[3],
        (norm * 2.0 * TWO_PI * math.pi) * amp_row * w_row * sums[1],
    ]

    rows8w = rows_iota((8, 512))
    pair = jnp.where(rows8w < 2, grads[1], grads[2])
    high = pair * 65537.0
    high = high - (high - pair)
    left = jnp.where((rows8w & 1) == 0, high, pair - high).astype(BF16)
    wide = lax.dot_general(left, hot_v[...], NT, preferred_element_type=F32)
    lanes1 = lax.broadcasted_iota(jnp.int32, (8, 128), 1)
    rows8n = rows_iota((8, 128))
    mine = (rows8n < 4) & (lax.shift_right_logical(rows8n, 1) == lax.shift_right_logical(lanes1, 5))
    cen_rows = jnp.sum(jnp.where(mine, wide, 0.0), axis=0, keepdims=True)
    for s in range(2):
        rows = rows_iota((8, 128))
        block = 0.0
        for h in range(2):
            lo = 256 * s + 128 * h
            for q in range(4):
                block = jnp.where(rows == 4 * h + q, grads[q][:, lo : lo + 128], block)
        part[s, 0:8, :] = block
        part[s, 8:9, :] = cen_rows

        for low in range(4):
            @pl.when(z_me != 4 * s + low)
            def _(s=s, low=low):
                back = lax.rem(4 * s + low + 8 - z_me, 8) - 1
                to = s * 128 + (x_me * 8 + low * 2 + 1) * 4 + y_me
                send(part.at[s], recv_a.at[2 * back + core_me], a_s, a_r, to).start()


    @pl.when(is0)
    def _():
        send(part.at[src], recv_a.at[14], a_s, a_r, here1).start()

    @pl.when(is1)
    def _():
        drain(recv_a, a_r)
        total = part[src]
        for i in range(15):
            total = total + recv_a[i]
        recv_b[0] = total
        for core in (1, 0):
            for i, off in enumerate(PLANE):
                send(recv_b.at[0], recv_b.at[i + 1], b_s.at[core], b_r, device(me, off, core)).start()
        send(recv_b.at[0], recv_b.at[0], b_s.at[0], b_r, here0).start()

    drain(resid.at[0], res_r.at[1])

    @pl.when(jnp.logical_not(early0))
    def _():
        drain(resid.at[0], res_r.at[0])

    @pl.when(is0)
    def _():
        drain(extra, x_r.at[3])

    for n in range(4):
        res_o[0, :, 128 * n : 128 * n + 128] = resid[n, 0:4, :]
        res_o[1, :, 128 * n : 128 * n + 128] = resid[n, 4:8, :]

    @pl.when(is0)
    def _():
        drain(recv_b, b_r)

    @pl.when(is1)
    def _():
        drain(recv_b.at[pl.ds(1, 15)], b_r)

    total = recv_b[0]
    for i in range(1, 16):
        total = total + recv_b[i]
    comp_o[:, 0:128] = total[0:4, :]
    comp_o[:, 128:256] = total[4:8, :]
    centre_o[0:1, :] = total[8:9, 0:32]
    centre_o[1:2, :] = total[8:9, 32:64]

    drain(resid.at[0], res_s.at[1])

    @pl.when(jnp.logical_not(late0))
    def _():
        drain(resid.at[0], res_s.at[0])

    @pl.when(early0)
    def _():
        for move in hand_over():
            move.wait_send()

    @pl.when(early1)
    def _():
        for move in spread():
            move.wait_send()

    @pl.when(is0)
    def _():
        drain(sibling, sib_s)
        drain(recv_a.at[pl.ds(0, 8)], a_s)

    @pl.when(is1)
    def _():
        @pl.when(at_end)
        def _():
            for core in (0, 1):
                drain(comp, cmp_s.at[core])

        drain(table, gat_s.at[0])
        drain(table.at[pl.ds(1, 15)], gat_s.at[1])
        drain(recv_a.at[pl.ds(0, 7)], a_s)
        drain(recv_b, b_s.at[0])
        drain(recv_b.at[pl.ds(1, 15)], b_s.at[1])


def deliver(*refs):
    sem = refs[6]
    moves = [pltpu.make_async_copy(refs[i], refs[3 + i], sem.at[i]) for i in range(3)]
    for move in moves:
        move.start()
    for move in moves:
        move.wait()


def on_device(observed, weights, pairs, positions, centres, assign, amplitude, offsets, widths, block_index):
    dma = pltpu.SemaphoreType.DMA
    operands = [
        pltpu.with_memory_space_constraint(v, pltpu.HBM)
        for v in (
            observed, weights, pairs, positions.T, centres, assign.reshape(1, 256), amplitude.reshape(1, 256), offsets,
            widths.reshape(1, 256),
        )
    ]
    sums = pl.pallas_call(
        kernel,
        out_shape=(
            jax.ShapeDtypeStruct((4, 256), F32),
            jax.ShapeDtypeStruct((2, 32), F32),
            jax.ShapeDtypeStruct((2, 4, 512), F32),
        ),
        in_specs=[pl.BlockSpec(memory_space=pltpu.HBM)] * 9 + [pl.BlockSpec(memory_space=pl.ANY)],
        out_specs=tuple([pl.BlockSpec(memory_space=pltpu.VMEM)] * 3),
        scratch_shapes=[
            pltpu.VMEM((2, 4, 256), F32),
            pltpu.VMEM((4, 256), F32),
            pltpu.VMEM((2, 256), jnp.int32),
            pltpu.VMEM((2, 16), F32),
            pltpu.VMEM((2, 32), F32),
            pltpu.VMEM((1, 256), jnp.int32),
            pltpu.VMEM((1, 256), F32),
            pltpu.VMEM((2, 256), F32),
            pltpu.VMEM((1, 256), F32),
            pltpu.SMEM((1,), jnp.int32),
            pltpu.SMEM((1, 128), F32),
            pltpu.VMEM((1, 128), F32),
            pltpu.VMEM((16, 1, 128), F32),
            pltpu.VMEM((2, 8, 256), F32),
            pltpu.VMEM((512, 128), F32),
            pltpu.VMEM((512, 128), F32),
            pltpu.VMEM((512, 128), F32),
            pltpu.VMEM((256, 512), BF16),
            pltpu.VMEM((256, 512), BF16),
            pltpu.VMEM((256, 512), BF16),
            pltpu.VMEM((256, 512), BF16),
            pltpu.VMEM((2, 9, 128), F32),
            pltpu.VMEM((15, 9, 128), F32),
            pltpu.VMEM((16, 9, 128), F32),
            pltpu.VMEM((4, 8, 128), F32),
            pltpu.VMEM((4, ROWS, 128), F32),
            pltpu.VMEM((12, ROWS, 128), F32),
            pltpu.VMEM((128, 512), BF16),
            pltpu.VMEM((4 * ROWS, 512), F32),
            pltpu.VMEM((2, 128), jnp.int32),
            pltpu.VMEM((2, 4, 128), F32),
            pltpu.VMEM((4, 128), F32),
            pltpu.VMEM((8, 128), F32),
            dma((10,)), dma(()), dma(()), dma(()), dma((2,)), dma(()), dma((2,)), dma(()), dma((2,)), dma((2,)), dma((5,)), dma((4,)), dma(()), dma(()),
            dma((2,)), dma(()),
        ],
        compiler_params=pltpu.CompilerParams(
            collective_id=0, has_side_effects=True, vmem_limit_bytes=32 * 1024 * 1024
        ),
        name="refit",
    )(*operands, block_index)
    return pl.pallas_call(
        deliver,
        out_shape=tuple(jax.ShapeDtypeStruct(v.shape, F32) for v in sums),
        in_specs=[pl.BlockSpec(memory_space=pltpu.VMEM)] * 3,
        out_specs=tuple([pl.BlockSpec(memory_space=pltpu.HBM)] * 3),
        scratch_shapes=[dma((3,))],
        name="deliver",
    )(*(pltpu.with_memory_space_constraint(v, pltpu.VMEM) for v in sums))


def solution(mesh):
    placed = (
        P(None, "ch", "bl"),
        P("ch", "bl"),
        P(None, "bl"),
        P("bl", None),
        P(),
        P("src"),
        P("src"),
        P(None, "src"),
        P("src"),
        P(),
    )
    return jax.shard_map(
        on_device,
        mesh=mesh,
        in_specs=placed,
        out_specs=(P(None, "src"), P(), P(None, "ch", "bl")),
        check_vma=False,
    )
```
